32 devices in a mesh: dp: 8 (over z, x), blk: 4 (over y, core).
Axes of the slice: x: 2, y: 2, z: 4, core: 2. Of those that a mesh axis runs over, the one named last changes fastest.
Arguments:
- patches: bfloat16 [8, 1024, 1024], P('dp', 'blk'), may hold values from -6 to 6
- cotangent: bfloat16 [8, 1024, 1024], P('dp', 'blk'), may hold values from -6 to 6
- image_lengths: int32 [8, 9], P('dp'), may hold values from 1 to 770, as said below
- params: float32 [12595200], P(('dp', 'blk')), may hold values from -1.5 to 1.75, as said below
- first_moment: float32 [12595200], P(('dp', 'blk')), may hold values from -0.0006 to 0.0006
- second_moment: float32 [12595200], P(('dp', 'blk')), may hold values from 1e-09 to 1e-07
Outputs:
- activations: bfloat16 [8, 1024, 1024], P('dp', 'blk')
- input_grad: bfloat16 [8, 1024, 1024], P('dp', 'blk')
- norms: float32 [12], replicated
- param_step: float32 [12595200], P(('dp', 'blk'))
- new_first: float32 [12595200], P(('dp', 'blk'))
- down_bias_grad: float32 [1024], replicated
The draws below stay inside these ranges and needn't reach their ends.
Inputs may be any that keep to these rules, and one draw needn't show every extreme that they name: `image_lengths`: each row holds the patch counts of 8 images of one packed sequence and then its padding count; a row sums to 1024; in each row exactly one image has 770 patches. `params`: parameters laid out as in the reference program.
All inputs are finite; a program needn't handle non-finite values.
Results may differ from the reference program's by a relative error of at most 0.014.
Values may be sent and summed in bfloat16 or wider, within the bound.
A program may use at most 256 MiB of HBM per device.

```python
import math
import jax
import jax.numpy as jnp
from jax import lax

D = 1024
FF = 4096
HEADS = 16
HEAD_DIM = 64
ROWS = 256
IMGS = 8
GROUPS = 12
NSEQ = 8
SEQ_LEN = 1024
RAW = 12595200
P_SIZE = 12595200


def draw_image_lengths(key, part):
    key = jax.random.fold_in(key, 5)
    remain = ROWS - 2
    longest = SEQ_LEN - ROWS + 2

    def one_row(row_key):
        pick_key, cut_key = jax.random.split(row_key)
        chosen = jax.random.randint(pick_key, (), 0, IMGS)
        shuffled = jax.random.permutation(cut_key, remain - 1) + 1
        cut_points = jnp.sort(shuffled[:IMGS - 1]).astype(jnp.int32)
        boundary = jnp.concatenate([jnp.zeros((1,), jnp.int32), cut_points, jnp.full((1,), remain, jnp.int32)])
        pieces = boundary[1:] - boundary[:-1]
        slot_ids = jnp.arange(IMGS, dtype=jnp.int32)
        source = jnp.clip(jnp.where(slot_ids < chosen, slot_ids, slot_ids - 1), 0, IMGS - 2)
        images = jnp.where(slot_ids == chosen, longest, pieces[source])
        return jnp.concatenate([images, pieces[IMGS - 1:]])
    return jax.vmap(one_row)(jax.random.split(key, NSEQ)).astype(jnp.int32)


def draw_params(key, part):
    key = jax.random.fold_in(key, 7)
    base = jnp.clip(jax.random.normal(key, (P_SIZE,), jnp.float32), -3.0, 3.0)
    square = D * D
    mlp_start = 7 * D + 4 * square
    marks = [0, D, 2 * D, 2 * D + 3 * square, 4 * D + 3 * square, 4 * D + 4 * square, 5 * D + 4 * square, 6 * D + 4 * square, mlp_start, mlp_start + D * FF, mlp_start + D * FF + FF, mlp_start + 2 * D * FF + FF, mlp_start + 2 * D * FF + FF + D]
    positions = jnp.arange(P_SIZE, dtype=jnp.int32)
    group_of = jnp.zeros((P_SIZE,), jnp.int32) - 1
    for mark in marks:
        group_of = group_of + (positions >= mark).astype(jnp.int32)
    scales = jnp.full((P_SIZE,), 0.2, jnp.float32)
    scales = jnp.where(group_of == 2, D ** (-0.5), scales)
    scales = jnp.where(group_of == 4, 16.0 * D ** (-0.5), scales)
    scales = jnp.where(group_of == 8, D ** (-0.5), scales)
    scales = jnp.where(group_of == 10, FF ** (-0.5), scales)
    scales = jnp.where(group_of == 12, 0.02, scales)
    gain_like = (group_of == 0) | (group_of == 6)
    return jnp.where(gain_like, 1.0 + 0.25 * base, scales * base).astype(jnp.float32)


def level_of(own_key, extent, cuts, least, top_value):
    def one(axis_at, blocks):
        draws = jax.random.uniform(jax.random.fold_in(jax.random.fold_in(own_key, 6), axis_at), (blocks,), jnp.float32, least / len(cuts), top_value / len(cuts))
        return jnp.repeat(jnp.exp(draws), extent[axis_at] // blocks).reshape((-1,) + (1,) * (len(extent) - axis_at - 1))

    gain = one(*cuts[0])
    for cut in cuts[1:]:
        gain = gain * one(*cut)
    return gain


def normal_values(own_key, dims, scale, bound, shards=(), kind=jnp.bfloat16):
    array = jax.random.normal(own_key, dims, jnp.float32) * scale
    if len(shards) > 0:
        array = level_of(own_key, dims, shards, -0.22, 0.18) * array
    return jnp.clip(array, min=-bound, max=bound).astype(kind)


def setup_inputs(seed: int = 0) -> dict:
    splits = jax.random.split(jax.random.key(seed), 7)
    return {
        "patches": normal_values(splits[0], (NSEQ, SEQ_LEN, D), 1.0, 6.0, ((0, 8), (1, 4))),
        "cotangent": normal_values(splits[1], (NSEQ, SEQ_LEN, D), 1.0, 6.0, ((0, 8), (1, 4))),
        "image_lengths": draw_image_lengths(jax.random.fold_in(splits[6], 71), 0),
        "params": draw_params(jax.random.fold_in(splits[6], 71), 0),
        "first_moment": normal_values(splits[4], (P_SIZE,), 0.0001, 0.0006, ((0, 32),), jnp.float32),
        "second_moment": jnp.clip(jnp.exp(math.log(1.0000000116860974e-07) - 4.6051702 * jax.random.uniform(splits[5], (P_SIZE,), jnp.float32) ** level_of(splits[5], (P_SIZE,), ((0, 32),), -0.2, 0.2)), 9.999999717180685e-10, 1.0000000116860974e-07),
    }


@jax.custom_vjp
def low(v):
    return lax.optimization_barrier(v.astype(jnp.bfloat16)).astype(jnp.float32)

@jax.custom_vjp
def low_back(v):
    return v

def low_keep(v):
    return (low(v), None)

def low_pass(kept, grad):
    return (grad,)

def back_keep(v):
    return (v, None)

def back_low(kept, grad):
    return (low(grad),)
low.defvjp(low_keep, low_pass)
low_back.defvjp(back_keep, back_low)
highest = lax.Precision.HIGHEST
eps_norm = 1e-06
neg_big = -1e+30

def starts_of(model_width, hidden):
    square = model_width * model_width
    mlp_start = 7 * model_width + 4 * square
    return [0, model_width, 2 * model_width, 2 * model_width + 3 * square, 4 * model_width + 3 * square, 4 * model_width + 4 * square, 5 * model_width + 4 * square, 6 * model_width + 4 * square, mlp_start, mlp_start + model_width * hidden, mlp_start + model_width * hidden + hidden, mlp_start + 2 * model_width * hidden + hidden, mlp_start + 2 * model_width * hidden + hidden + model_width]

def unpack(flat_params):
    marks = starts_of(D, FF)
    pieces = [flat_params[marks[member]:marks[member + 1]] for member in range(12)]
    return (pieces[0], pieces[1], pieces[2].reshape(D, 3 * D), pieces[3], pieces[4].reshape(D, D), pieces[5], pieces[6], pieces[7], pieces[8].reshape(D, FF), pieces[9], pieces[10].reshape(FF, D), pieces[11])

def layer_norm(values, gains, offsets):
    average = lax.optimization_barrier(jnp.mean(values, axis=-1, keepdims=True))
    centred = values - average
    spread = lax.optimization_barrier(jnp.mean(centred * centred, axis=-1, keepdims=True))
    return centred * lax.rsqrt(spread + eps_norm) * gains + offsets

def segment_ids(lengths, row_ids):
    bounds = jnp.cumsum(lengths).astype(jnp.int32)
    return lax.optimization_barrier(jnp.sum((row_ids[:, None] >= bounds[None, :]).astype(jnp.int32), axis=1))

def attend(queries, keys, values, labels):
    scale_of = HEAD_DIM ** (-0.5)
    size = math.gcd(SEQ_LEN, 512)
    count = SEQ_LEN // size

    def one_block(members):
        query_block, label_block = members
        raw = low_back(jnp.einsum('qhd,khd->hqk', query_block, keys, precision=highest))
        allowed = label_block[:, None] == labels[None, :]
        scores = jnp.where(allowed[None], raw * scale_of, neg_big)
        top_score = lax.optimization_barrier(jnp.max(scores, axis=-1, keepdims=True))
        weights = jnp.where(allowed[None], jnp.exp(scores - top_score), 0.0)
        probs = low(weights / lax.optimization_barrier(jnp.sum(weights, axis=-1, keepdims=True)))
        return jnp.einsum('hqk,khd->qhd', probs, values, precision=highest)
    outputs = lax.map(jax.checkpoint(one_block), (queries.reshape(count, size, HEADS, HEAD_DIM), labels.reshape(count, size)))
    return outputs.reshape(SEQ_LEN, D)

def layer(flat_params, patch_rows, labels):
    gain_one, shift_one, w_qkv, bias_qv, w_out, bias_out, gain_two, shift_two, w_up, bias_up, w_down, bias_down = unpack(low(flat_params))
    normed_one = low(layer_norm(patch_rows, gain_one, shift_one))
    bias_all = jnp.concatenate([bias_qv[:D], jnp.zeros((D,), jnp.float32), bias_qv[D:]])
    projected = low(low_back(jnp.dot(normed_one, w_qkv, precision=highest) + bias_all))
    queries = projected[:, :D].reshape(SEQ_LEN, HEADS, HEAD_DIM)
    keys = projected[:, D:2 * D].reshape(SEQ_LEN, HEADS, HEAD_DIM)
    values = projected[:, 2 * D:].reshape(SEQ_LEN, HEADS, HEAD_DIM)
    attended = low(low_back(attend(queries, keys, values, labels)))
    branch = low_back(jnp.dot(attended, w_out, precision=highest) + bias_out)
    middle = patch_rows + branch
    normed_two = low(layer_norm(middle, gain_two, shift_two))
    hidden_pre = low_back(jnp.dot(normed_two, w_up, precision=highest) + bias_up)
    activated = low(jax.nn.gelu(hidden_pre, approximate=False))
    return middle + low_back(jnp.dot(activated, w_down, precision=highest) + bias_down)

def reference(patches, cotangent, image_lengths, params, first_moment, second_moment):
    row_ids = jnp.arange(SEQ_LEN, dtype=jnp.int32)

    def one_sequence(running, seq_items):
        patch_rows, cot_rows, lengths = seq_items
        labels = segment_ids(lengths, row_ids)
        outputs, pullback = jax.vjp(lambda flat_params, inputs: layer(flat_params, inputs, labels), params, patch_rows.astype(jnp.float32))
        grad_flat, grad_in = pullback(cot_rows.astype(jnp.float32))
        return (running + grad_flat, (outputs.astype(jnp.bfloat16), grad_in.astype(jnp.bfloat16)))
    grads, (activations, input_grad) = lax.scan(one_sequence, jnp.zeros_like(params), (patches, cotangent, image_lengths))
    marks = starts_of(D, FF)
    down_bias_grad = grads[marks[11]:marks[12]]
    norms = jnp.stack([jnp.sum(grads[marks[member]:marks[member + 1]] * grads[marks[member]:marks[member + 1]]) for member in range(GROUPS)])
    clip_factor = 1.0 / jnp.maximum(jnp.sqrt(jnp.sum(norms)), 1.0)
    square = D * D
    decayed = jnp.concatenate([jnp.zeros((2 * D,), jnp.float32), jnp.ones((3 * square,), jnp.float32), jnp.zeros((2 * D,), jnp.float32), jnp.ones((square,), jnp.float32), jnp.zeros((3 * D,), jnp.float32), jnp.ones((D * FF,), jnp.float32), jnp.zeros((FF,), jnp.float32), jnp.ones((FF * D,), jnp.float32), jnp.zeros((D + P_SIZE - RAW,), jnp.float32)])
    scaled = clip_factor * grads
    new_first = 0.9 * first_moment + 0.1 * scaled
    new_second = 0.999 * second_moment + 0.001 * scaled * scaled
    direction = new_first / (1.0 - 0.9 ** 10) / (jnp.sqrt(new_second / (1.0 - 0.999 ** 10)) + 1e-08)
    param_step = -0.001 * 0.9 ** 12 * (direction + 0.05 * decayed * params)
    return (activations, input_grad, norms, param_step, new_first, down_bias_grad)
```

```python
from functools import partial
import math

import jax
import jax.numpy as jnp
from jax import lax
from jax.experimental import pallas as pl
from jax.experimental.pallas import tpu as pltpu
from jax.sharding import PartitionSpec as P

D = 1024
FF = 4096
HEADS = 16
HEAD_DIM = 64
GROUPS = 12
RAW = 12595200


eps_norm = 1e-06
neg_big = -1e30


def starts_of(model_width, hidden):
    square = model_width * model_width
    mlp_start = 7 * model_width + 4 * square
    return [
        0,
        model_width,
        2 * model_width,
        2 * model_width + 3 * square,
        4 * model_width + 3 * square,
        4 * model_width + 4 * square,
        5 * model_width + 4 * square,
        6 * model_width + 4 * square,
        mlp_start,
        mlp_start + model_width * hidden,
        mlp_start + model_width * hidden + hidden,
        mlp_start + 2 * model_width * hidden + hidden,
        mlp_start + 2 * model_width * hidden + hidden + model_width,
    ]


def unpack(flat_params):
    marks = starts_of(D, FF)
    pieces = [flat_params[marks[member] : marks[member + 1]] for member in range(12)]
    return (
        pieces[0],
        pieces[1],
        pieces[2].reshape(D, 3 * D),
        pieces[3],
        pieces[4].reshape(D, D),
        pieces[5],
        pieces[6],
        pieces[7],
        pieces[8].reshape(D, FF),
        pieces[9],
        pieces[10].reshape(FF, D),
        pieces[11],
    )


def layer_norm(values, gains, offsets):
    average = jnp.mean(values, axis=-1, keepdims=True)
    centred = values - average
    spread = jnp.mean(centred * centred, axis=-1, keepdims=True)
    return centred * lax.rsqrt(spread + eps_norm) * gains + offsets


def segment_ids(lengths, row_ids):
    bounds = jnp.cumsum(lengths)
    return jnp.sum((row_ids[:, None] >= bounds[None, :]).astype(jnp.int32), axis=1)


def shards(patches, cotangent, image_lengths, params, first_moment, second_moment):
    local_rows = patches.shape[1]
    seq_len = local_rows * lax.axis_size("blk")
    scale_of = HEAD_DIM ** (-0.5)
    inputs = patches[0].astype(jnp.float32)
    lengths = image_lengths[0]
    query_ids = lax.axis_index("blk") * local_rows + jnp.arange(local_rows, dtype=jnp.int32)
    query_labels = segment_ids(lengths, query_ids)
    weights_low = lax.all_gather(params.astype(jnp.bfloat16), ("dp", "blk"), axis=0, tiled=True)
    (
        gain_one,
        shift_one,
        w_qkv,
        bias_qv,
        w_out,
        bias_out,
        gain_two,
        shift_two,
        w_up,
        bias_up,
        w_down,
        bias_down,
    ) = unpack(weights_low)
    normed_one, pull_one = jax.vjp(
        layer_norm, inputs, gain_one.astype(jnp.float32), shift_one.astype(jnp.float32)
    )
    normed_low = normed_one.astype(jnp.bfloat16)
    bias_all = jnp.concatenate(
        [
            bias_qv[:D].astype(jnp.float32),
            jnp.zeros((D,), jnp.float32),
            bias_qv[D:].astype(jnp.float32),
        ]
    )
    projected = (jnp.dot(normed_low, w_qkv, preferred_element_type=jnp.float32) + bias_all).astype(
        jnp.bfloat16
    )
    queries = projected[:, :D].reshape(local_rows, HEADS, HEAD_DIM)
    key_value = projected[:, D:]

    def attend_block(state, block, block_labels):
        allowed = query_labels[:, None] == block_labels[None, :]
        best_in, total_in, summed_in = state
        raw = jnp.einsum("qhd,khd->hqk", queries, block[:, 0], preferred_element_type=jnp.float32)
        scores = jnp.where(allowed[None], raw * scale_of, neg_big)
        new_best = jnp.maximum(best_in, jnp.max(scores, axis=-1))
        factor = jnp.exp(best_in - new_best)
        weights = jnp.where(allowed[None], jnp.exp(scores - new_best[..., None]), 0.0)
        new_total = total_in * factor + jnp.sum(weights, axis=-1)
        added = jnp.einsum(
            "hqk,khd->qhd",
            weights.astype(jnp.bfloat16),
            block[:, 1],
            preferred_element_type=jnp.float32,
        )
        return (new_best, new_total, summed_in * factor.T[..., None] + added)

    start_state = (
        jnp.full((HEADS, local_rows), neg_big, jnp.float32),
        jnp.zeros((HEADS, local_rows), jnp.float32),
        jnp.zeros((local_rows, HEADS, HEAD_DIM), jnp.float32),
    )
    carry = start_state
    piece = lax.all_gather(key_value, "blk", axis=0, tiled=True)
    count = piece.shape[0]
    size = math.gcd(count, 512)
    blocks = piece.reshape(count // size, size, 2, HEADS, HEAD_DIM)
    labels = segment_ids(lengths, jnp.arange(count, dtype=jnp.int32)).reshape(count // size, size)

    def one_block(state, members):
        return (attend_block(state, members[0], members[1]), None)

    carry, ignored = lax.scan(one_block, carry, (blocks, labels))
    best, total, summed = carry
    attended = summed / total.T[..., None]
    log_total = best + jnp.log(total)
    attended_low = attended.reshape(local_rows, D).astype(jnp.bfloat16)
    branch = jnp.dot(attended_low, w_out, preferred_element_type=jnp.float32) + bias_out.astype(
        jnp.float32
    )
    middle = inputs + branch
    normed_two, pull_two = jax.vjp(
        layer_norm, middle, gain_two.astype(jnp.float32), shift_two.astype(jnp.float32)
    )
    normed_two_low = normed_two.astype(jnp.bfloat16)
    hidden_pre = jnp.dot(normed_two_low, w_up, preferred_element_type=jnp.float32) + bias_up.astype(
        jnp.float32
    )
    activated, pull_gelu = jax.vjp(partial(jax.nn.gelu, approximate=False), hidden_pre)
    activated_low = activated.astype(jnp.bfloat16)
    result = middle + (
        jnp.dot(activated_low, w_down, preferred_element_type=jnp.float32)
        + bias_down.astype(jnp.float32)
    )
    grad_out = cotangent[0]
    grad_down = jnp.dot(activated_low.T, grad_out, preferred_element_type=jnp.float32)
    grad_bias_down = jnp.sum(grad_out.astype(jnp.float32), axis=0)
    grad_act = jnp.dot(grad_out, w_down.T, preferred_element_type=jnp.float32)
    grad_hidden_low = pull_gelu(grad_act)[0].astype(jnp.bfloat16)
    grad_up = jnp.dot(normed_two_low.T, grad_hidden_low, preferred_element_type=jnp.float32)
    grad_bias_up = jnp.sum(grad_hidden_low.astype(jnp.float32), axis=0)
    grad_normed_two = jnp.dot(grad_hidden_low, w_up.T, preferred_element_type=jnp.float32)
    grad_mid_norm, grad_gain_two, grad_shift_two = pull_two(grad_normed_two)
    grad_middle = grad_out.astype(jnp.float32) + grad_mid_norm
    grad_middle_low = grad_middle.astype(jnp.bfloat16)
    grad_w_out = jnp.dot(attended_low.T, grad_middle_low, preferred_element_type=jnp.float32)
    grad_bias_out = jnp.sum(grad_middle_low.astype(jnp.float32), axis=0)
    grad_attended = (
        jnp.dot(grad_middle_low, w_out.T, preferred_element_type=jnp.float32)
        .astype(jnp.bfloat16)
        .reshape(local_rows, HEADS, HEAD_DIM)
    )
    delta_rows = jnp.sum(grad_attended.astype(jnp.float32) * attended, axis=-1).T
    gathered = lax.all_gather(key_value, "blk", axis=0, tiled=True)
    size = math.gcd(seq_len, 512)
    key_blocks = gathered.reshape(seq_len // size, size, 2, HEADS, HEAD_DIM)
    key_labels = segment_ids(lengths, jnp.arange(seq_len, dtype=jnp.int32)).reshape(
        seq_len // size, size
    )

    def back_block(grad_query, members):
        block, block_labels = members
        allowed = query_labels[:, None] == block_labels[None, :]
        raw = jnp.einsum("qhd,khd->hqk", queries, block[:, 0], preferred_element_type=jnp.float32)
        scores = jnp.where(allowed[None], raw * scale_of, neg_big)
        probs = jnp.where(allowed[None], jnp.exp(scores - log_total[..., None]), 0.0)
        grad_probs = jnp.einsum(
            "qhd,khd->hqk", grad_attended, block[:, 1], preferred_element_type=jnp.float32
        )
        grad_raw = (probs * (grad_probs - delta_rows[..., None]) * scale_of).astype(jnp.bfloat16)
        new_grad = grad_query + jnp.einsum(
            "hqk,khd->qhd", grad_raw, block[:, 0], preferred_element_type=jnp.float32
        )
        grad_keys = jnp.einsum(
            "hqk,qhd->khd", grad_raw, queries, preferred_element_type=jnp.float32
        )
        grad_values = jnp.einsum(
            "hqk,qhd->khd",
            probs.astype(jnp.bfloat16),
            grad_attended,
            preferred_element_type=jnp.float32,
        )
        return (new_grad, jnp.stack([grad_keys, grad_values], axis=1))

    grad_query, grad_kv_blocks = lax.scan(
        back_block, jnp.zeros((local_rows, HEADS, HEAD_DIM), jnp.float32), (key_blocks, key_labels)
    )
    grad_kv = lax.psum_scatter(
        grad_kv_blocks.reshape(seq_len, 2 * D).astype(jnp.bfloat16),
        "blk",
        scatter_dimension=0,
        tiled=True,
    ).astype(jnp.float32)
    grad_projected = jnp.concatenate([grad_query.reshape(local_rows, D), grad_kv], axis=1).astype(
        jnp.bfloat16
    )
    grad_w_qkv = jnp.dot(normed_low.T, grad_projected, preferred_element_type=jnp.float32)
    grad_proj_rows = jnp.sum(grad_projected.astype(jnp.float32), axis=0)
    grad_bias_qv = jnp.concatenate([grad_proj_rows[:D], grad_proj_rows[2 * D :]])
    grad_normed_one = jnp.dot(grad_projected, w_qkv.T, preferred_element_type=jnp.float32)
    grad_in_norm, grad_gain_one, grad_shift_one = pull_one(grad_normed_one)
    grad_inputs = grad_middle + grad_in_norm
    shard_len = params.shape[0]
    total_params = shard_len * lax.axis_size(("dp", "blk"))
    flat_grad = jnp.concatenate(
        [
            grad_gain_one,
            grad_shift_one,
            grad_w_qkv.reshape(-1),
            grad_bias_qv,
            grad_w_out.reshape(-1),
            grad_bias_out,
            grad_gain_two,
            grad_shift_two,
            grad_up.reshape(-1),
            grad_bias_up,
            grad_down.reshape(-1),
            grad_bias_down,
            jnp.zeros((total_params - RAW,), jnp.float32),
        ]
    )
    shard_grad = lax.psum_scatter(
        lax.slice_in_dim(flat_grad, 0, lax.axis_size(("dp", "blk")) * shard_len, axis=0),
        ("dp", "blk"),
        scatter_dimension=0,
        tiled=True,
    )
    positions = lax.axis_index(("dp", "blk")) * shard_len + jnp.arange(shard_len, dtype=jnp.int32)
    marks = jnp.array(starts_of(D, FF), dtype=jnp.int32)
    group_of = jnp.sum((positions[:, None] >= marks[None, :]).astype(jnp.int32), axis=1) - 1
    squares = shard_grad * shard_grad
    partials = jnp.sum(
        jnp.where(
            group_of[None, :] == jnp.arange(GROUPS, dtype=jnp.int32)[:, None], squares[None, :], 0.0
        ),
        axis=1,
    )
    norms, bias_total = lax.psum((partials, grad_bias_down), ("dp", "blk"))
    clip_factor = 1.0 / jnp.maximum(jnp.sqrt(jnp.sum(norms)), 1.0)
    decayed = ((group_of == 2) | (group_of == 4) | (group_of == 8) | (group_of == 10)).astype(
        jnp.float32
    )
    scaled = clip_factor * shard_grad
    new_first = 0.9 * first_moment + 0.1 * scaled
    new_second = 0.999 * second_moment + 0.001 * scaled * scaled
    direction = new_first / (1.0 - 0.9**10) / (jnp.sqrt(new_second / (1.0 - 0.999**10)) + 1e-08)
    param_step = -0.001 * 0.9**12 * (direction + 0.05 * decayed * params)
    return (
        result.astype(jnp.bfloat16)[None],
        grad_inputs.astype(jnp.bfloat16)[None],
        norms,
        param_step,
        new_first,
        bias_total,
    )


MESH = pl.DeviceIdType.MESH
LANE = 128


def pick(cond, yes, no):
    return jnp.where(cond, jnp.int32(yes), jnp.int32(no))


def rdma(src, dst, ssem, rsem, dev):
    return pltpu.make_async_remote_copy(src_ref=src, dst_ref=dst, send_sem=ssem, recv_sem=rsem, device_id=dev, device_id_type=MESH)


def rows(ref, start, size, step=128):
    return ref.at[pl.ds(pl.multiple_of(start, step), size)]


def gate(peers):
    sem = pltpu.get_barrier_semaphore()
    for peer in peers:
        pl.semaphore_signal(sem, inc=1, device_id=peer, device_id_type=MESH)
    pl.semaphore_wait(sem, len(peers))


class Place:
    def __init__(self):
        self.dp = lax.axis_index("dp")
        self.blk = lax.axis_index("blk")
        self.d = self.dp * 4 + self.blk
        self.z = self.dp // 2
        self.x = self.dp % 2
        self.y = self.blk // 2
        self.c = self.blk % 2
        self.xpeer = (self.z * 2 + 1 - self.x, self.blk)
        self.zs = [lax.rem(self.z + k, 4) for k in (1, 3, 2)]
        self.zpeers = [(zz * 2 + self.x, self.blk) for zz in self.zs]
        self.quad = [(self.dp, lax.rem(self.blk + k, 4)) for k in (1, 2, 3)]
        up = lax.rem(self.d + 1, 32)
        down = lax.rem(self.d + 31, 32)
        self.next = (up // 4, up % 4)
        self.prev = (down // 4, down % 4)
        d = self.d
        self.is_qkv = d < 8
        self.is_out = (d == 8) | (d == 9)
        self.is_mix_out = d == 10
        self.is_up = (d >= 11) & (d < 21)
        self.is_mix_down = d == 21
        self.is_down = d >= 22
        self.is_seg = self.is_out | self.is_down
        self.is_mix = self.is_mix_out | self.is_mix_down
        self.base = pick(d < 8, 16, pick(d < 11, 32, pick(d < 21, 56, 88))) - 3 * d
        self.seg0 = pick(d < 11, 3 * (d - 8), jnp.maximum(3 * (d - 21) - 1, 0))
        self.mix_up = pick(self.is_mix_out, 2074, -7)
        self.mix_seg = pick(self.is_mix_out, 2, 1049)

    def seg_home(self, n):
        seg = self.seg0 + n // 4
        panel = n % 4
        out_row = 3072 + 256 * panel + 128 * (seg % 2)
        down_row = 8192 + 1024 * panel + 128 * (seg // 4)
        low = self.d < 11
        return pick(low, seg // 2, seg % 4), pick(low, out_row, down_row)

    def block_home(self, n):
        part, row = self.seg_home(n)
        return pick(self.is_qkv, n // 3, part), pick(self.is_qkv, (n % 3) * 1024 + 128 * self.d, row)

    def up_home(self, n):
        start = pick(self.is_up, 32 + 96 * (self.d - 11), pick(self.is_mix_out, 0, 992))
        return n // 4, 4096 + 1024 * (n % 4) + start


def chunk_row(q, k):
    first = (k // 4) * 1024 + 512 * q + 128 * (k % 4)
    turn = 3 * (q - 2) + k // 4
    panel = k % 4
    other = pick(
        turn < 2,
        3072 + 256 * panel + 128 * turn,
        pick(turn < 10, 4096 + 1024 * panel + 128 * (turn - 2), 8192 + 1024 * panel + 128 * (turn - 10)),
    )
    return pick(q < 2, first, other)


def loop(count, body):
    def step(i, carry):
        body(i)
        return carry

    lax.fori_loop(0, count, step, 0)


def unit_span(start, stride):
    return pl.ds(start, 16, stride=stride)


def for_tiles(me, visit):
    e0 = 24 + me.base

    @pl.when(me.is_qkv)
    def _():
        def body(rb):
            for ct in range(24):
                n = ((ct % 8) // 2) * 3 + ct // 8
                visit(e0 + 384 * rb + ct, 24, n * 128 + 16 * rb, 128 * (ct % 2))

        loop(8, body)

    @pl.when(me.is_up)
    def _():
        def body(rb):
            for ct in range(32):
                n = (ct % 4) * 4 + ct // 8
                visit(e0 + 512 * rb + ct, 32, n * 96 + 16 * rb, 128 * ((ct // 4) % 2))

        loop(6, body)

    def segs(count, first):
        def body(i):
            for ct in range(8):
                visit(first + 128 * i + ct, 8, ((i // 8) * 4 + ct // 2) * 128 + 16 * (i % 8), 128 * (ct % 2))

        loop(count, body)

    @pl.when(me.is_seg)
    def _():
        segs(24, e0)

    @pl.when(me.is_mix)
    def _():
        segs(16, 24 + me.mix_seg)

        def body(rb):
            for ct in range(32):
                n = (ct % 4) * 4 + ct // 8
                visit(24 + me.mix_up + 512 * rb + ct, 32, 1024 + n * 32 + 16 * rb, 128 * ((ct // 4) % 2))

        loop(2, body)


def for_pieces(me, visit):
    @pl.when(me.is_qkv | me.is_seg)
    def _():
        def body(n):
            part, row = me.block_home(n)
            visit(n, n * 128, 128, part, row, 128)

        loop(12, body)

    @pl.when(me.is_up)
    def _():
        def body(n):
            part, row = me.up_home(n)
            visit(n, n * 96, 96, part, row, 32)

        loop(16, body)

    @pl.when(me.is_mix)
    def _():
        def body(n):
            part, row = me.seg_home(n)
            visit(n, n * 128, 128, part, row, 128)

        loop(8, body)

        def body_up(n):
            part, row = me.up_home(n)
            visit(8 + n, 1024 + n * 32, 32, part, row, 32)

        loop(16, body_up)


def vec_spots(me, visit):
    for cond, row, unit, count in (
        (me.d == 0, 0, 0, 16),
        (me.d == 7, 0, 3067, 8),
        (me.d == 8, 0, 0, 8),
        (me.d == 10, 8, 2050, 24),
        (me.d == 21, 0, 1017, 32),
        (me.d == 31, 0, 3067, 8),
    ):

        @pl.when(cond)
        def _(row=row, unit=unit, count=count):
            visit(row, 24 + unit, count)


def send_rows(me, src, dst, ssem, rsem):
    mine = pl.ds(pl.multiple_of(me.blk * 256, 256), 256)
    return [rdma(src, dst.at[mine], ssem, rsem, peer) for peer in me.quad]


def gather(me, r):
    gate(me.quad + me.zpeers + [me.xpeer, me.next, me.prev])
    r.tail[...] = r.par[3051:3075, :]
    up = rdma(r.tail, r.hp, r.hsem.at[0], r.hsem.at[1], me.next)
    down = rdma(r.par.at[0:24], r.hn, r.hsem.at[2], r.hsem.at[3], me.prev)
    up.start()
    down.start()
    sends = send_rows(me, r.pat, r.PA, r.asem.at[0], r.asem.at[1]) + send_rows(me, r.cot, r.CA, r.asem.at[2], r.asem.at[3])
    mine = pl.ds(pl.multiple_of(me.blk * 256, 256), 256)
    r.PA[mine, :] = r.pat[...]
    r.CA[mine, :] = r.cot[...]

    def put(i):
        r.E[pl.ds(pl.multiple_of(24 + 64 * i, 8), 64), :] = r.par[pl.ds(pl.multiple_of(64 * i, 8), 64), :]

    loop(48, put)
    r.E[3096:3099, :] = r.par[3072:3075, :]
    up.wait()
    down.wait()
    r.E[0:24, :] = r.hp[...]
    r.E[3099:3123, :] = r.hn[...]

    def tile(unit, stride, row, lane):
        r.S[pl.ds(pl.multiple_of(row, 16), 16), lane : lane + 128] = r.E[unit_span(unit, stride), :].astype(jnp.bfloat16)

    for_tiles(me, tile)
    r.VS[...] = jnp.zeros_like(r.VS)

    def vec(row, unit, count):
        r.VS[row : row + count, :] = r.E[unit : unit + count, :].astype(jnp.bfloat16).astype(jnp.float32)

    vec_spots(me, vec)

    def piece(go):
        def visit(i, srow, size, part, frow, step):
            src = rows(r.S, srow, size, 32)
            dst = rows(r.F, frow, size, step)

            @pl.when(part != me.blk)
            def _():
                cp = rdma(src, dst, r.qsem.at[i], r.csem, (me.dp, part))
                cp.start() if go else cp.wait_send()

            if go:

                @pl.when(part == me.blk)
                def _():
                    pltpu.make_async_copy(src, dst, r.csem).start()

        return visit

    vq = [rdma(r.VS, r.VQ.at[me.blk], r.vsem.at[0], r.vsem.at[1], peer) for peer in me.quad]
    for v in vq:
        v.start()
    for_pieces(me, piece(True))
    r.VQ[me.blk] = r.VS[...]
    pltpu.make_async_copy(r.VQ.at[0:3], r.VQ.at[0:3], r.vsem.at[0]).wait()
    pltpu.make_async_copy(r.VQ.at[0:3], r.VQ.at[0:3], r.vsem.at[1]).wait()
    r.XV[me.dp] = r.VQ[0] + r.VQ[1] + r.VQ[2] + r.VQ[3]
    pltpu.make_async_copy(r.F.at[0:1536], r.F.at[0:1536], r.csem).wait()

    def block(q, k):
        return rows(r.F, chunk_row(q, k), 128)

    def xsend(q, zsrc, g):
        for i in range(4):
            ref = block(q, g * 4 + i)
            rdma(ref, ref, r.xs, r.xr.at[zsrc * 3 + g], me.xpeer).start()

    def vsend(q, zsrc):
        rdma(r.XV.at[q], r.XV.at[q], r.vxs, r.vxr.at[zsrc], me.xpeer).start()

    for g in range(3):
        for i in range(4):
            ref = block(me.dp, g * 4 + i)
            for peer in me.zpeers:
                rdma(ref, ref, r.zs, r.zr.at[me.z * 3 + g], peer).start()
        xsend(me.dp, me.z, g)
    for peer in me.zpeers:
        rdma(r.XV.at[me.dp], r.XV.at[me.dp], r.vzs, r.vzr.at[me.z], peer).start()
    vsend(me.dp, me.z)

    for s in sends:
        s.start()

    def arrived(ref, sem):
        pltpu.make_async_copy(ref, ref, sem).wait()

    four = r.F.at[0:512]
    for g in range(3):
        for zz in me.zs:
            arrived(four, r.zr.at[zz * 3 + g])
            xsend(zz * 2 + me.x, zz, g)
    for zz in me.zs:
        arrived(r.XV.at[0], r.vzr.at[zz])
        vsend(zz * 2 + me.x, zz)
    for zz in [me.z] + me.zs:
        arrived(r.XV.at[0], r.vxr.at[zz])
        for g in range(3):
            arrived(four, r.xr.at[zz * 3 + g])
    arrived(r.F.at[0:4608], r.zs)
    arrived(r.F.at[0:6144], r.xs)
    arrived(r.XV.at[0:3], r.vzs)
    arrived(r.XV.at[0:4], r.vxs)
    for_pieces(me, piece(False))
    for i in range(4):
        arrived(r.PA.at[0:768], r.asem.at[i])


GATHER_SCRATCH = dict(
    E=pltpu.VMEM((3128, 128), jnp.float32),
    tail=pltpu.VMEM((24, 128), jnp.float32),
    hp=pltpu.VMEM((24, 128), jnp.float32),
    hn=pltpu.VMEM((24, 128), jnp.float32),
    S=pltpu.VMEM((1536, 256), jnp.bfloat16),
    VS=pltpu.VMEM((32, 128), jnp.float32),
    VQ=pltpu.VMEM((4, 32, 128), jnp.float32),
    hsem=pltpu.SemaphoreType.DMA((4,)),
    asem=pltpu.SemaphoreType.DMA((4,)),
    qsem=pltpu.SemaphoreType.DMA((24,)),
    csem=pltpu.SemaphoreType.DMA,
    vsem=pltpu.SemaphoreType.DMA((2,)),
    xs=pltpu.SemaphoreType.DMA,
    xr=pltpu.SemaphoreType.DMA((12,)),
    zs=pltpu.SemaphoreType.DMA,
    zr=pltpu.SemaphoreType.DMA((12,)),
    vxs=pltpu.SemaphoreType.DMA,
    vxr=pltpu.SemaphoreType.DMA((4,)),
    vzs=pltpu.SemaphoreType.DMA,
    vzr=pltpu.SemaphoreType.DMA((4,)),
)


class Refs:
    pass


def call(phase, ins, outs, scratch, cid, args):
    names = list(ins) + list(outs) + list(scratch)

    def kernel(*refs):
        r = Refs()
        for name, ref in zip(names, refs):
            setattr(r, name, ref)
        phase(Place(), r)

    whole = pl.BlockSpec(memory_space=pltpu.VMEM)
    return pl.pallas_call(
        kernel,
        out_shape=[jax.ShapeDtypeStruct(*o) for o in outs.values()],
        in_specs=[whole] * len(ins),
        out_specs=[whole] * len(outs),
        scratch_shapes=list(scratch.values()),
        compiler_params=pltpu.CompilerParams(collective_id=cid, has_side_effects=True, vmem_limit_bytes=62 * 2**20),
    )(*args)


def k1(par, pat, cot):
    return call(
        gather,
        ("par", "pat", "cot"),
        dict(
            F=((12288, 256), jnp.bfloat16),
            XV=((8, 32, 128), jnp.float32),
            PA=((1024, 1024), jnp.bfloat16),
            CA=((1024, 1024), jnp.bfloat16),
        ),
        GATHER_SCRATCH,
        0,
        (par, pat, cot),
    )


BF, F32 = jnp.bfloat16, jnp.float32
EPS = 1e-06
OUT0, UP0, DOWN0 = 3072, 4096, 8192


def dot(a, b):
    return lax.dot_general(a, b, (((1,), (0,)), ((), ())), preferred_element_type=F32)


def dot_nt(a, b):
    return lax.dot_general(a, b, (((1,), (1,)), ((), ())), preferred_element_type=F32)


def dot_tn(a, b):
    return lax.dot_general(a, b, (((0,), (0,)), ((), ())), preferred_element_type=F32)


def block_of(i):
    return pl.ds(pl.multiple_of(i * 256, 256), 256)


def wide(r, q, first, count=8):
    return jnp.concatenate([r.XV[q, first + i : first + i + 1, :] for i in range(count)], axis=1)


def narrow(r, q, first):
    return jnp.concatenate([r.XV[q, pl.ds(first + i, 1), :] for i in range(2)], axis=1)


def put_vec(r, q, first, row, add=False):
    for i in range(row.shape[1] // 128):
        part = row[:, i * 128 : i * 128 + 128]
        if add:
            part = part + r.VG[q, first + i : first + i + 1, :]
        r.VG[q, first + i : first + i + 1, :] = part


def normalize(x):
    mean = jnp.mean(x, axis=-1, keepdims=True)
    cen = x - mean
    var = jnp.mean(cen * cen, axis=-1, keepdims=True)
    scale = lax.rsqrt(var + EPS)
    return cen * scale, scale


def norm_back(dy, xhat, scale, gain):
    t = dy * gain
    return scale * (t - jnp.mean(t, axis=-1, keepdims=True) - xhat * jnp.mean(t * xhat, axis=-1, keepdims=True))


def quad_sum(me, r, make, sems, finish, slot=2):
    y, c = me.y, me.c
    sib, yp = (me.dp, y * 2 + 1 - c), (me.dp, (1 - y) * 2 + c)
    far_sib, far, near_sib, own = (1 - y) * 2 + 1 - c, (1 - y) * 2 + c, y * 2 + 1 - c, me.blk
    ssem, rsem = sems
    make(far_sib)
    a = rdma(r.PB.at[block_of(far_sib)], r.RB.at[0], ssem.at[0], rsem.at[0], sib)
    a.start()
    make(far)
    a.wait_recv()
    for i in range(4):
        at = pl.ds(pl.multiple_of(far * 256 + 64 * i, 64), 64)
        lo = slice(64 * i, 64 * i + 64)
        r.RB[3, lo, :] = (r.PB[at, :].astype(F32) + r.RB[0, lo, :].astype(F32)).astype(BF)
    b = rdma(r.RB.at[3], r.RB.at[slot], ssem.at[1], rsem.at[1], yp)
    b.start()
    make(near_sib)
    d = rdma(r.PB.at[block_of(near_sib)], r.RB.at[1], ssem.at[2], rsem.at[2], sib)
    d.start()
    make(own)
    d.wait_recv()
    b.wait_recv()
    for i in range(4):
        at = pl.ds(pl.multiple_of(own * 256 + 64 * i, 64), 64)
        lo = slice(64 * i, 64 * i + 64)
        finish(lo, r.PB[at, :].astype(F32) + r.RB[1, lo, :].astype(F32) + r.RB[slot, lo, :].astype(F32))
    a.wait_send()
    b.wait_send()
    d.wait_send()


def quad_share(me, r, buf, sems):
    y, c = me.y, me.c
    sib, yp = (me.dp, y * 2 + 1 - c), (me.dp, (1 - y) * 2 + c)
    ssem, rsem = sems

    def part(dev, i):
        return buf.at[pl.ds(pl.multiple_of(dev * 256 + 64 * i, 64), 64)]

    far = (1 - y) * 2 + c
    over = [rdma(part(me.blk, i), part(me.blk, i), ssem.at[i], rsem.at[i], yp) for i in range(4)]
    near = rdma(buf.at[block_of(me.blk)], buf.at[block_of(me.blk)], ssem.at[8], rsem.at[8], sib)
    pass_on = [rdma(part(far, i), part(far, i), ssem.at[4 + i], rsem.at[4 + i], sib) for i in range(4)]
    for o in over:
        o.start()
    near.start()
    for i in range(4):
        over[i].wait_recv()
        pass_on[i].start()
    near.wait()
    for i in range(4):
        over[i].wait_send()
        pass_on[i].wait()


def labels_at(r, at):
    total = jnp.zeros_like(at)
    bound = 0
    for k in range(9):
        bound = bound + r.lens[k]
        total = total + (at >= bound).astype(jnp.int32)
    return total


def lane_mask(h):
    lane = lax.broadcasted_iota(jnp.int32, (1, 128), 1)
    return ((lane // 64) == h).astype(BF)


def forward_a(me, r):
    gain, shift = wide(r, 0, 0), wide(r, 0, 8)

    def ln(i):
        at = pl.ds(pl.multiple_of(i * 64, 64), 64)
        xhat, _ = normalize(r.PA[at, :].astype(F32))
        r.NO[at, :] = (xhat * gain + shift).astype(BF)

    loop(16, ln)
    bias = [narrow(r, 1, 2 * me.blk), None, narrow(r, 2, 2 * me.blk)]

    def proj(i):
        at = block_of(i)
        for j in range(3):
            out = dot(r.NO[at, :], r.F[j * 1024 : j * 1024 + 1024, :])
            if bias[j] is not None:
                out = out + bias[j]
            r.QKV[j, at, :] = out.astype(BF)

    loop(4, proj)
    key_labels = labels_at(r, lax.broadcasted_iota(jnp.int32, (1, 1024), 1))

    def attend(i):
        at = block_of(i)
        row_labels = labels_at(r, lax.broadcasted_iota(jnp.int32, (256, 1), 0) + i * 256)
        allowed = row_labels == key_labels
        for t in range(2):
            lanes = slice(128 * t, 128 * t + 128)
            q = r.QKV[0, at, lanes]
            k = r.QKV[1, :, lanes]
            v = r.QKV[2, :, lanes]
            out = jnp.zeros((256, 128), F32)
            for h in range(2):
                m = lane_mask(h)
                s = jnp.where(allowed, dot_nt(q * m, k) * 0.125, -1e30)
                w = jnp.exp(s - jnp.max(s, axis=-1, keepdims=True))
                p = (w * (1.0 / jnp.sum(w, axis=-1, keepdims=True))).astype(BF)
                r.P[2 * t + h, at, :] = p
                out = out + dot(p, v * m)
            r.AT[at, lanes] = out.astype(BF)

    loop(4, attend)


def forward_b(me, r):
    def term(i):
        at = block_of(i)
        for p in range(4):
            r.PB[at, 256 * p : 256 * p + 256] = dot(r.AT[at, :], r.F[OUT0 + 256 * p : OUT0 + 256 * p + 256, :]).astype(BF)

    bias_out = wide(r, 2, 8)
    gain, shift = wide(r, 2, 16), wide(r, 2, 24)

    def finish(lo, total):
        x = r.pat[lo, :].astype(F32) + (total + bias_out)
        r.MID[lo, :] = x
        xhat, _ = normalize(x)
        r.NT[pl.ds(pl.multiple_of(me.blk * 256 + lo.start, 64), 64), :] = (xhat * gain + shift).astype(BF)

    quad_sum(me, r, term, (r.s1s, r.s1r), finish)
    quad_share(me, r, r.NT, (r.g1s, r.g1r))


def forward_c(me, r):
    biases = [jnp.concatenate([r.XV[5, pl.ds(4 * (2 * p + i) + me.blk, 1), :] for i in range(2)], axis=1) for p in range(4)]

    def up(i):
        at = pl.ds(pl.multiple_of(i * 128, 128), 128)
        for p in range(4):
            h = dot(r.NT[at, :], r.F[UP0 + 1024 * p : UP0 + 1024 * p + 1024, :]) + biases[p]
            phi = 0.5 + 0.5 * lax.erf(h * 0.7071067811865476)
            lanes = slice(256 * p, 256 * p + 256)
            r.AC[at, lanes] = (h * phi).astype(BF)
            r.GP[at, lanes] = (phi + h * (jnp.exp(-0.5 * h * h) * 0.3989422804014327)).astype(BF)

    loop(8, up)


def forward_d(me, r):
    def term(i):
        at = block_of(i)
        for p in range(4):
            r.PB[at, 256 * p : 256 * p + 256] = dot(r.AC[at, :], r.F[DOWN0 + 1024 * p : DOWN0 + 1024 * p + 1024, :]).astype(BF)

    bias_down = wide(r, 7, 0)

    def finish(lo, total):
        r.act[lo, :] = (r.MID[lo, :] + (total + bias_down)).astype(BF)

    quad_sum(me, r, term, (r.s2s, r.s2r), finish, 4)


def backward_a(me, r):
    r.VG[...] = jnp.zeros_like(r.VG)

    def hidden(i):
        at = block_of(i)
        for p in range(4):
            lanes = slice(256 * p, 256 * p + 256)
            acc = jnp.zeros((256, 256), F32)
            for k in range(4):
                acc = acc + dot_nt(r.CA[at, 256 * k : 256 * k + 256], r.F[DOWN0 + 1024 * k + 256 * p : DOWN0 + 1024 * k + 256 * p + 256, :])
            r.GH[at, lanes] = (acc * r.GP[at, lanes].astype(F32)).astype(BF)

    loop(4, hidden)
    for p in range(4):
        sums = jnp.sum(r.GH[:, 256 * p : 256 * p + 256].astype(F32), axis=0, keepdims=True)
        for i in range(2):
            r.VG[5, pl.ds(4 * (2 * p + i) + me.blk, 1), :] = sums[:, 128 * i : 128 * i + 128]
    put_vec(r, 7, 0, jnp.sum(r.cot[...].astype(F32), axis=0, keepdims=True))


def weight_grad(r, left, right, base, height):
    def body(i):
        cols = pl.ds(pl.multiple_of(i * 256, 256), 256)
        lt = left[:, cols].T
        for p in range(right.shape[1] // 256):
            out = dot(lt, right[:, 256 * p : 256 * p + 256])
            r.G[pl.ds(pl.multiple_of(base + p * height + i * 256, 256), 256), :] = out.astype(BF)

    loop(height // 256, body)


def backward_b(me, r):
    weight_grad(r, r.AC, r.CA, DOWN0, 1024)
    weight_grad(r, r.NT, r.GH, UP0, 1024)


def backward_c(me, r):
    def term(i):
        at = block_of(i)
        for n in range(4):
            acc = jnp.zeros((256, 256), F32)
            for p in range(4):
                acc = acc + dot_nt(r.GH[at, 256 * p : 256 * p + 256], r.F[UP0 + 1024 * p + 256 * n : UP0 + 1024 * p + 256 * n + 256, :])
            r.PB[at, 256 * n : 256 * n + 256] = acc.astype(BF)

    gain = wide(r, 2, 16)
    sums = [jnp.zeros((1, 1024), F32)] * 3

    def finish(lo, dy):
        xhat, scale = normalize(r.MID[lo, :])
        gm = r.cot[lo, :].astype(F32) + norm_back(dy, xhat, scale, gain)
        r.MID[lo, :] = gm
        low = gm.astype(BF)
        r.GM[pl.ds(pl.multiple_of(me.blk * 256 + lo.start, 64), 64), :] = low
        for n, term_of in enumerate((low.astype(F32), dy * xhat, dy)):
            sums[n] = sums[n] + jnp.sum(term_of, axis=0, keepdims=True)

    quad_sum(me, r, term, (r.s3s, r.s3r), finish)
    quad_share(me, r, r.GM, (r.g2s, r.g2r))
    for n in range(3):
        put_vec(r, 2, 8 + 8 * n, sums[n])


def backward_d(me, r):
    weight_grad(r, r.AT, r.GM, OUT0, 256)

    def attended(i):
        at = block_of(i)
        acc = jnp.zeros((256, 256), F32)
        for p in range(4):
            acc = acc + dot_nt(r.GM[at, 256 * p : 256 * p + 256], r.F[OUT0 + 256 * p : OUT0 + 256 * p + 256, :])
        r.DA[at, :] = acc.astype(BF)

    loop(4, attended)
    r.KV[...] = jnp.zeros_like(r.KV)

    def attend(i):
        at = block_of(i)
        for t in range(2):
            lanes = slice(128 * t, 128 * t + 128)
            q = r.QKV[0, at, lanes]
            k = r.QKV[1, :, lanes]
            v = r.QKV[2, :, lanes]
            da = r.DA[at, lanes]
            dq = jnp.zeros((256, 128), F32)
            for h in range(2):
                m = lane_mask(h)
                p = r.P[2 * t + h, at, :]
                pf = p.astype(F32)
                dp = dot_nt(da * m, v)
                delta = jnp.sum(pf * dp, axis=-1, keepdims=True)
                ds = (pf * (dp - delta) * 0.125).astype(BF)
                dq = dq + dot(ds, k * m)
                r.KV[0, :, lanes] += dot_tn(ds, q * m)
                r.KV[1, :, lanes] += dot_tn(p, da * m)
            r.DQ[0, at, lanes] = dq.astype(BF)

    loop(4, attend)
    r.DQ[1] = r.KV[0].astype(BF)
    r.DQ[2] = r.KV[1].astype(BF)
    for j, q in ((0, 1), (2, 2)):
        sums = jnp.sum(r.DQ[j].astype(F32), axis=0, keepdims=True)
        for i in range(2):
            r.VG[q, pl.ds(2 * me.blk + i, 1), :] = sums[:, 128 * i : 128 * i + 128]


def backward_e(me, r):
    def body(i):
        cols = pl.ds(pl.multiple_of(i * 256, 256), 256)
        lt = r.NO[:, cols].T
        for j in range(3):
            r.G[pl.ds(pl.multiple_of(j * 1024 + i * 256, 256), 256), :] = dot(lt, r.DQ[j]).astype(BF)

    loop(4, body)


def backward_f(me, r):
    def term(i):
        at = block_of(i)
        for n in range(4):
            acc = jnp.zeros((256, 256), F32)
            for j in range(3):
                acc = acc + dot_nt(r.DQ[j, at, :], r.F[1024 * j + 256 * n : 1024 * j + 256 * n + 256, :])
            r.PB[at, 256 * n : 256 * n + 256] = acc.astype(BF)

    gain = wide(r, 0, 0)
    sums = [jnp.zeros((1, 1024), F32)] * 2

    def finish(lo, dy):
        xhat, scale = normalize(r.pat[lo, :].astype(F32))
        r.ing[lo, :] = (r.MID[lo, :] + norm_back(dy, xhat, scale, gain)).astype(BF)
        for n, term_of in enumerate((dy * xhat, dy)):
            sums[n] = sums[n] + jnp.sum(term_of, axis=0, keepdims=True)

    quad_sum(me, r, term, (r.s4s, r.s4r), finish, 4)
    for n in range(2):
        put_vec(r, 0, 8 * n, sums[n])


def compute(me, r):
    gate(me.quad)
    for phase in (forward_a, forward_b, forward_c, forward_d, backward_a, backward_b, backward_c, backward_d, backward_e, backward_f):
        phase(me, r)


DMA = pltpu.SemaphoreType.DMA
COMPUTE_SCRATCH = dict(
    NO=pltpu.VMEM((1024, 1024), BF),
    QKV=pltpu.VMEM((3, 1024, 256), BF),
    P=pltpu.VMEM((4, 1024, 1024), BF),
    AT=pltpu.VMEM((1024, 256), BF),
    PB=pltpu.VMEM((1024, 1024), BF),
    RB=pltpu.VMEM((5, 256, 1024), BF),
    MID=pltpu.VMEM((256, 1024), F32),
    NT=pltpu.VMEM((1024, 1024), BF),
    AC=pltpu.VMEM((1024, 1024), BF),
    GP=pltpu.VMEM((1024, 1024), BF),
    GH=pltpu.VMEM((1024, 1024), BF),
    GM=pltpu.VMEM((1024, 1024), BF),
    DA=pltpu.VMEM((1024, 256), BF),
    KV=pltpu.VMEM((2, 1024, 256), F32),
    DQ=pltpu.VMEM((3, 1024, 256), BF),
    s1s=DMA((3,)), s1r=DMA((3,)), s2s=DMA((3,)), s2r=DMA((3,)), s3s=DMA((3,)), s3r=DMA((3,)), s4s=DMA((3,)), s4r=DMA((3,)),
    g1s=DMA((9,)), g1r=DMA((9,)), g2s=DMA((9,)), g2r=DMA((9,)),
)


def k2(lens, pat, cot, F, XV, PA, CA):
    ins = ("lens", "pat", "cot", "F", "XV", "PA", "CA")
    outs = dict(G=((12288, 256), BF), VG=((8, 32, 128), F32), act=((256, 1024), BF), ing=((256, 1024), BF))
    names = list(ins) + list(outs) + list(COMPUTE_SCRATCH)

    def kernel(*refs):
        r = Refs()
        for name, ref in zip(names, refs):
            setattr(r, name, ref)
        compute(Place(), r)

    whole = pl.BlockSpec(memory_space=pltpu.VMEM)
    return pl.pallas_call(
        kernel,
        out_shape=[jax.ShapeDtypeStruct(*o) for o in outs.values()],
        in_specs=[pl.BlockSpec(memory_space=pltpu.SMEM)] + [whole] * 6,
        out_specs=[whole] * len(outs),
        scratch_shapes=list(COMPUTE_SCRATCH.values()),
        compiler_params=pltpu.CompilerParams(collective_id=1, has_side_effects=True, vmem_limit_bytes=62 * 2**20),
    )(lens, pat, cot, F, XV, PA, CA)


def crow(q, k):
    return pick(q < 2, 128 * k, 384 * (k % 4) + 128 * (k // 4))


class Other(Place):
    def __init__(self, me, i):
        d = me.dp * 4 + i
        self.d, self.blk, self.dp = d, i, me.dp
        self.is_qkv = d < 8
        self.is_out = (d == 8) | (d == 9)
        self.is_mix_out = d == 10
        self.is_up = (d >= 11) & (d < 21)
        self.is_mix_down = d == 21
        self.is_down = d >= 22
        self.is_seg = self.is_out | self.is_down
        self.is_mix = self.is_mix_out | self.is_mix_down
        self.seg0 = pick(d < 11, 3 * (d - 8), jnp.maximum(3 * (d - 21) - 1, 0))

    def seg_spot(self, n):
        seg = self.seg0 + n // 4
        low = self.d < 11
        turn = pick(low, seg % 2, 10 + seg // 4 - 3 * (self.dp - 2))
        return pick(low, seg // 2, seg % 4), 384 * (n % 4) + 128 * turn

    def block_spot(self, n):
        part, row = self.seg_spot(n)
        return pick(self.is_qkv, n // 3, part), pick(self.is_qkv, (n % 3) * 512 + 128 * (self.d % 4), row)

    def up_spot(self, n):
        start = pick(self.is_up, 32 + 96 * (self.d - 11), pick(self.is_mix_out, 0, 992))
        return n // 4, 384 * (n % 4) + 256 + start - 384 * (self.dp - 2)

    def pieces(self, visit):
        @pl.when(self.is_qkv | self.is_seg)
        def _():
            loop(12, lambda n: visit(n, n * 128, 128, *self.block_spot(n)))

        @pl.when(self.is_up)
        def _():
            loop(16, lambda n: visit(n, n * 96, 96, *self.up_spot(n)))

        @pl.when(self.is_mix)
        def _():
            loop(8, lambda n: visit(n, n * 128, 128, *self.seg_spot(n)))
            loop(16, lambda n: visit(8 + n, 1024 + n * 32, 32, *self.up_spot(n)))


def arrived(ref, sem):
    pltpu.make_async_copy(ref, ref, sem).wait()


def squares(x):
    s = jnp.sum(x * x, axis=0, keepdims=True)
    return s[:, :128] + s[:, 128:] if x.shape[1] == 256 else s


def reduce_x(me, r, zz, groups=(0, 1, 2)):
    q = zz * 2 + 1 - me.x
    for g in groups:
        for i in range(4):
            k = g * 4 + i
            rdma(rows(r.G, chunk_row(q, k), 128), rows(r.XR.at[zz], crow(q, k), 128), r.rxs, r.rxr.at[zz * 3 + g], me.xpeer).start()


def reduce_z(me, r, zz, g):
    q = zz * 2 + me.x
    arrived(r.G.at[0:512], r.rxr.at[zz * 3 + g])
    for i in range(4):
        k = g * 4 + i
        src, at = pl.ds(pl.multiple_of(chunk_row(q, k), 128), 128), pl.ds(pl.multiple_of(crow(q, k), 128), 128)
        total = r.G[src, :].astype(F32) + r.XR[zz, at, :].astype(F32)
        r.XR[zz, at, :] = total.astype(BF)

        @pl.when(me.z != zz)
        def _():
            rdma(rows(r.XR.at[zz], crow(q, k), 128), rows(r.ZR.at[me.z], crow(q, k), 128), r.rzs.at[zz], r.rzr.at[me.z * 3 + g], (q, me.blk)).start()


def reduce_phase(me, r):
    for zz in (3, 2, 1, 0):
        reduce_x(me, r, zz)
    for zz in range(4):
        rdma(r.VG.at[zz * 2 + 1 - me.x], r.VX.at[zz], r.wxs, r.wxr.at[zz], me.xpeer).start()
    for zz in (3, 2, 1, 0):
        for g in range(3):
            reduce_z(me, r, zz, g)
    reduce_vectors(me, r)
    finish_chunk(me, r)


def reduce_vectors(me, r):
    for zz in range(4):
        arrived(r.VX.at[0], r.wxr.at[zz])
        r.VX[zz] = r.VX[zz] + r.VG[zz * 2 + me.x]

        @pl.when(me.z != zz)
        def _():
            rdma(r.VX.at[zz], r.VZ.at[me.z], r.wzs.at[zz], r.wzr.at[me.z], (zz * 2 + me.x, me.blk)).start()

    total = r.VX[me.z]
    for zz in me.zs:
        arrived(r.VZ.at[0], r.wzr.at[zz])
        total = total + r.VZ[zz]
    r.VT[me.blk] = total
    outs = [rdma(r.VT.at[me.blk], r.VT.at[me.blk], r.wqs, r.wqr.at[me.blk], peer) for peer in me.quad]
    for o in outs:
        o.start()
    for k in (1, 2, 3):
        arrived(r.VT.at[0], r.wqr.at[lax.rem(me.blk + k, 4)])
    r.VS[...] = r.VT[0] + r.VT[1] + r.VT[2] + r.VT[3]


def finish_chunk(me, r):
    r.NB[0] = jnp.zeros((24, 128), F32)
    first_tensor = pick(me.dp < 2, 2, pick(me.dp == 2, 4, pick(me.dp < 6, 8, 10)))
    for g in range(3):
        for zz in me.zs:
            arrived(r.G.at[0:512], r.rzr.at[zz * 3 + g])
        part = jnp.zeros((1, 128), F32)
        for i in range(4):
            at = pl.ds(pl.multiple_of(crow(me.dp, g * 4 + i), 128), 128)
            total = r.XR[me.z, at, :].astype(F32)
            for zz in me.zs:
                total = total + r.ZR[zz, at, :].astype(F32)
            part = part + squares(total)
            r.C[at, :] = total.astype(BF)
        tensor = first_tensor
        if g == 2:
            tensor = pick(me.dp == 2, 8, tensor)
        if g >= 1:
            tensor = pick(me.dp == 5, 10, tensor)
        r.NB[0, pl.ds(tensor, 1), :] += part
    for i in range(4):
        def visit(n, srow, size, part, row, i=i):
            src, dst = rows(r.C, row, size, 32), rows(r.S, srow, size, 32)

            @pl.when((part == me.blk) & (me.blk != i))
            def _():
                rdma(src, dst, r.qsem2.at[i * 24 + n], r.csem2, (me.dp, i)).start()

            @pl.when((part == me.blk) & (me.blk == i))
            def _():
                pltpu.make_async_copy(src, dst, r.csem2).start()

        Other(me, i).pieces(visit)
    for q, tensors in ((0, (0, 1, None, None)), (1, (3, None, None, None)), (2, (3, 5, 6, 7)), (5, (9, 9, 9, 9)), (7, (11, None, None, None))):
        @pl.when((me.dp == q) & (me.blk == 0))
        def _(q=q, tensors=tensors):
            for g, tensor in enumerate(tensors):
                if tensor is not None:
                    r.NB[0, tensor : tensor + 1, :] += squares(r.VS[8 * g : 8 * g + 8, :])
            if q == 7:
                r.NB[0, 16:24, :] = r.VS[0:8, :]


def norm_exchange(me, r):
    zx = [(me.z + 1 - 2 * (me.z % 2)), lax.rem(me.z + 2, 4)]
    peers = [(me.dp, me.y * 2 + 1 - me.c), (me.dp, (1 - me.y) * 2 + me.c), me.xpeer] + [(z * 2 + me.x, me.blk) for z in zx]
    for n, peer in enumerate(peers):
        cp = rdma(r.NB.at[n], r.NR.at[n], r.nsem.at[n], r.nrsem.at[n], peer)
        cp.start()
        cp.wait()
        r.NB[n + 1] = r.NB[n] + r.NR[n]


def units_phase(me, r):
    arrived(r.S, r.csem2)

    def clear(i):
        r.E[pl.ds(pl.multiple_of(i * 8, 8), 8), :] = jnp.zeros((8, 128), F32)

    for i in (0, 1, 2, 3, 4, 5, 385, 386, 387, 388, 389, 390):
        clear(i)

    def tile(unit, stride, row, lane):
        r.E[unit_span(unit, stride), :] = r.S[pl.ds(pl.multiple_of(row, 16), 16), lane : lane + 128].astype(F32)

    for_tiles(me, tile)

    def vec(row, unit, count):
        r.E[unit : unit + count, :] = r.VS[row : row + count, :]

    vec_spots(me, vec)
    r.tail[...] = r.E[3099:3123, :]
    up = rdma(r.tail, r.hp, r.hsem2.at[0], r.hsem2.at[1], me.next)
    down = rdma(r.E.at[0:24], r.hn, r.hsem2.at[2], r.hsem2.at[3], me.prev)
    up.start()
    down.start()
    up.wait()
    down.wait()
    r.E[24:48, :] += r.hp[...]
    r.E[3075:3099, :] += r.hn[...]


SPOTS = ((0, 16), (24592, 24608), (32800, 32824), (65592, 65624), (98392, 98400))


def update(me, r):
    nb = r.NB[5]
    norms = jnp.sum(nb[0:16, :], axis=1, keepdims=True)
    r.norms[...] = jnp.broadcast_to(norms, (16, 128))
    r.down[...] = nb[16:24, :]
    total = jnp.sum(norms[0:12, :], axis=0, keepdims=True)
    clip = 1.0 / jnp.maximum(jnp.sqrt(total), 1.0)

    def part(start, count):
        grad = clip * r.E[pl.ds(24 + start, count), :]
        at = pl.ds(start, count)
        unit = me.d * 3075 + start + lax.broadcasted_iota(jnp.int32, (count, 128), 0)
        plain = jnp.zeros((count, 128), jnp.bool_)
        for lo, hi in SPOTS:
            plain = plain | ((unit >= lo) & (unit < hi))
        first = 0.9 * r.m[at, :] + 0.1 * grad
        second = 0.999 * r.v[at, :] + 0.001 * grad * grad
        direction = first / (1.0 - 0.9**10) / (jnp.sqrt(second / (1.0 - 0.999**10)) + 1e-08)
        r.first[at, :] = first
        r.step[at, :] = -0.001 * 0.9**12 * (direction + jnp.where(plain, 0.0, 0.05 * r.par[at, :]))

    loop(48, lambda i: part(pl.multiple_of(i * 64, 8), 64))
    part(3072, 3)


def final(me, r):
    gate(me.quad + me.zpeers + [me.xpeer, me.next, me.prev])
    reduce_phase(me, r)
    norm_exchange(me, r)
    units_phase(me, r)
    update(me, r)
    reduce_drain(me, r)


def reduce_drain(me, r):
    arrived(r.G.at[0:6144], r.rxs)
    arrived(r.VX.at[0:3], r.wqs)
    arrived(r.VX, r.wxs)
    for i in range(4):

        @pl.when(me.z != i)
        def _():
            arrived(r.G.at[0:1536], r.rzs.at[i])
            arrived(r.VX.at[0], r.wzs.at[i])

        def visit(n, srow, size, part, row, i=i):
            @pl.when((part == me.blk) & (me.blk != i))
            def _():
                arrived(rows(r.C, row, size, 32), r.qsem2.at[i * 24 + n])

        Other(me, i).pieces(visit)


FINAL_SCRATCH = dict(
    XR=pltpu.VMEM((4, 1536, 256), BF),
    ZR=pltpu.VMEM((4, 1536, 256), BF),
    C=pltpu.VMEM((1536, 256), BF),
    S=pltpu.VMEM((1536, 256), BF),
    E=pltpu.VMEM((3128, 128), F32),
    VX=pltpu.VMEM((4, 32, 128), F32),
    VZ=pltpu.VMEM((4, 32, 128), F32),
    VT=pltpu.VMEM((4, 32, 128), F32),
    VS=pltpu.VMEM((32, 128), F32),
    NB=pltpu.VMEM((6, 24, 128), F32),
    NR=pltpu.VMEM((5, 24, 128), F32),
    tail=pltpu.VMEM((24, 128), F32),
    hp=pltpu.VMEM((24, 128), F32),
    hn=pltpu.VMEM((24, 128), F32),
    hsem2=DMA((4,)), rxs=DMA, rxr=DMA((12,)), rzs=DMA((4,)), rzr=DMA((12,)),
    wxs=DMA, wxr=DMA((4,)), wzs=DMA((4,)), wzr=DMA((4,)), wqs=DMA, wqr=DMA((4,)),
    qsem2=DMA((96,)), csem2=DMA, nsem=DMA((5,)), nrsem=DMA((5,)),
)


def k3(G, VG, par, m, v):
    return call(
        final,
        ("G", "VG", "par", "m", "v"),
        dict(step=((3075, 128), F32), first=((3075, 128), F32), norms=((16, 128), F32), down=((8, 128), F32)),
        FINAL_SCRATCH,
        2,
        (G, VG, par, m, v),
    )


def fast_shards(pat, cot, lens, params, m, v):
    def units(a):
        return a.reshape(-1, LANE)

    par = units(params)
    F, XV, PA, CA = k1(par, pat[0], cot[0])
    G, VG, act, ing = k2(lens[0], pat[0], cot[0], F, XV, PA, CA)
    step, first, norms, down = k3(G, VG, par, units(m), units(v))
    return act[None], ing[None], norms[:GROUPS, 0], step.reshape(-1), first.reshape(-1), down.reshape(-1)


def solution(mesh):
    act, flat = P("dp", "blk", None), P(("dp", "blk"))
    specs = dict(
        in_specs=(act, act, P("dp", None), flat, flat, flat), out_specs=(act, act, P(), flat, flat, P()), check_vma=False
    )

    def layer(patches, cotangent, image_lengths, params, first_moment, second_moment):
        fits = (dict(mesh.shape), patches.shape, params.shape) == (dict(dp=8, blk=4), (8, 1024, D), (RAW,))
        step = jax.shard_map(fast_shards if fits else shards, mesh=mesh, **specs)
        return step(patches, cotangent, image_lengths, params, first_moment, second_moment)

    return layer
```

```python
from functools import partial
import math

import jax
import jax.numpy as jnp
from jax import lax
from jax.experimental import pallas as pl
from jax.experimental.pallas import tpu as pltpu
from jax.sharding import PartitionSpec as P

D = 1024
FF = 4096
HEADS = 16
HEAD_DIM = 64
GROUPS = 12
RAW = 12595200


eps_norm = 1e-06
neg_big = -1e30


def starts_of(model_width, hidden):
    square = model_width * model_width
    mlp_start = 7 * model_width + 4 * square
    return [
        0,
        model_width,
        2 * model_width,
        2 * model_width + 3 * square,
        4 * model_width + 3 * square,
        4 * model_width + 4 * square,
        5 * model_width + 4 * square,
        6 * model_width + 4 * square,
        mlp_start,
        mlp_start + model_width * hidden,
        mlp_start + model_width * hidden + hidden,
        mlp_start + 2 * model_width * hidden + hidden,
        mlp_start + 2 * model_width * hidden + hidden + model_width,
    ]


def unpack(flat_params):
    marks = starts_of(D, FF)
    pieces = [flat_params[marks[member] : marks[member + 1]] for member in range(12)]
    return (
        pieces[0],
        pieces[1],
        pieces[2].reshape(D, 3 * D),
        pieces[3],
        pieces[4].reshape(D, D),
        pieces[5],
        pieces[6],
        pieces[7],
        pieces[8].reshape(D, FF),
        pieces[9],
        pieces[10].reshape(FF, D),
        pieces[11],
    )


def layer_norm(values, gains, offsets):
    average = jnp.mean(values, axis=-1, keepdims=True)
    centred = values - average
    spread = jnp.mean(centred * centred, axis=-1, keepdims=True)
    return centred * lax.rsqrt(spread + eps_norm) * gains + offsets


def segment_ids(lengths, row_ids):
    bounds = jnp.cumsum(lengths)
    return jnp.sum((row_ids[:, None] >= bounds[None, :]).astype(jnp.int32), axis=1)


def shards(patches, cotangent, image_lengths, params, first_moment, second_moment):
    local_rows = patches.shape[1]
    seq_len = local_rows * lax.axis_size("blk")
    scale_of = HEAD_DIM ** (-0.5)
    inputs = patches[0].astype(jnp.float32)
    lengths = image_lengths[0]
    query_ids = lax.axis_index("blk") * local_rows + jnp.arange(local_rows, dtype=jnp.int32)
    query_labels = segment_ids(lengths, query_ids)
    weights_low = lax.all_gather(params.astype(jnp.bfloat16), ("dp", "blk"), axis=0, tiled=True)
    (
        gain_one,
        shift_one,
        w_qkv,
        bias_qv,
        w_out,
        bias_out,
        gain_two,
        shift_two,
        w_up,
        bias_up,
        w_down,
        bias_down,
    ) = unpack(weights_low)
    normed_one, pull_one = jax.vjp(
        layer_norm, inputs, gain_one.astype(jnp.float32), shift_one.astype(jnp.float32)
    )
    normed_low = normed_one.astype(jnp.bfloat16)
    bias_all = jnp.concatenate(
        [
            bias_qv[:D].astype(jnp.float32),
            jnp.zeros((D,), jnp.float32),
            bias_qv[D:].astype(jnp.float32),
        ]
    )
    projected = (jnp.dot(normed_low, w_qkv, preferred_element_type=jnp.float32) + bias_all).astype(
        jnp.bfloat16
    )
    queries = projected[:, :D].reshape(local_rows, HEADS, HEAD_DIM)
    key_value = projected[:, D:]

    def attend_block(state, block, block_labels):
        allowed = query_labels[:, None] == block_labels[None, :]
        best_in, total_in, summed_in = state
        raw = jnp.einsum("qhd,khd->hqk", queries, block[:, 0], preferred_element_type=jnp.float32)
        scores = jnp.where(allowed[None], raw * scale_of, neg_big)
        new_best = jnp.maximum(best_in, jnp.max(scores, axis=-1))
        factor = jnp.exp(best_in - new_best)
        weights = jnp.where(allowed[None], jnp.exp(scores - new_best[..., None]), 0.0)
        new_total = total_in * factor + jnp.sum(weights, axis=-1)
        added = jnp.einsum(
            "hqk,khd->qhd",
            weights.astype(jnp.bfloat16),
            block[:, 1],
            preferred_element_type=jnp.float32,
        )
        return (new_best, new_total, summed_in * factor.T[..., None] + added)

    start_state = (
        jnp.full((HEADS, local_rows), neg_big, jnp.float32),
        jnp.zeros((HEADS, local_rows), jnp.float32),
        jnp.zeros((local_rows, HEADS, HEAD_DIM), jnp.float32),
    )
    carry = start_state
    piece = lax.all_gather(key_value, "blk", axis=0, tiled=True)
    count = piece.shape[0]
    size = math.gcd(count, 512)
    blocks = piece.reshape(count // size, size, 2, HEADS, HEAD_DIM)
    labels = segment_ids(lengths, jnp.arange(count, dtype=jnp.int32)).reshape(count // size, size)

    def one_block(state, members):
        return (attend_block(state, members[0], members[1]), None)

    carry, ignored = lax.scan(one_block, carry, (blocks, labels))
    best, total, summed = carry
    attended = summed / total.T[..., None]
    log_total = best + jnp.log(total)
    attended_low = attended.reshape(local_rows, D).astype(jnp.bfloat16)
    branch = jnp.dot(attended_low, w_out, preferred_element_type=jnp.float32) + bias_out.astype(
        jnp.float32
    )
    middle = inputs + branch
    normed_two, pull_two = jax.vjp(
        layer_norm, middle, gain_two.astype(jnp.float32), shift_two.astype(jnp.float32)
    )
    normed_two_low = normed_two.astype(jnp.bfloat16)
    hidden_pre = jnp.dot(normed_two_low, w_up, preferred_element_type=jnp.float32) + bias_up.astype(
        jnp.float32
    )
    activated, pull_gelu = jax.vjp(partial(jax.nn.gelu, approximate=False), hidden_pre)
    activated_low = activated.astype(jnp.bfloat16)
    result = middle + (
        jnp.dot(activated_low, w_down, preferred_element_type=jnp.float32)
        + bias_down.astype(jnp.float32)
    )
    grad_out = cotangent[0]
    grad_down = jnp.dot(activated_low.T, grad_out, preferred_element_type=jnp.float32)
    grad_bias_down = jnp.sum(grad_out.astype(jnp.float32), axis=0)
    grad_act = jnp.dot(grad_out, w_down.T, preferred_element_type=jnp.float32)
    grad_hidden_low = pull_gelu(grad_act)[0].astype(jnp.bfloat16)
    grad_up = jnp.dot(normed_two_low.T, grad_hidden_low, preferred_element_type=jnp.float32)
    grad_bias_up = jnp.sum(grad_hidden_low.astype(jnp.float32), axis=0)
    grad_normed_two = jnp.dot(grad_hidden_low, w_up.T, preferred_element_type=jnp.float32)
    grad_mid_norm, grad_gain_two, grad_shift_two = pull_two(grad_normed_two)
    grad_middle = grad_out.astype(jnp.float32) + grad_mid_norm
    grad_middle_low = grad_middle.astype(jnp.bfloat16)
    grad_w_out = jnp.dot(attended_low.T, grad_middle_low, preferred_element_type=jnp.float32)
    grad_bias_out = jnp.sum(grad_middle_low.astype(jnp.float32), axis=0)
    grad_attended = (
        jnp.dot(grad_middle_low, w_out.T, preferred_element_type=jnp.float32)
        .astype(jnp.bfloat16)
        .reshape(local_rows, HEADS, HEAD_DIM)
    )
    delta_rows = jnp.sum(grad_attended.astype(jnp.float32) * attended, axis=-1).T
    gathered = lax.all_gather(key_value, "blk", axis=0, tiled=True)
    size = math.gcd(seq_len, 512)
    key_blocks = gathered.reshape(seq_len // size, size, 2, HEADS, HEAD_DIM)
    key_labels = segment_ids(lengths, jnp.arange(seq_len, dtype=jnp.int32)).reshape(
        seq_len // size, size
    )

    def back_block(grad_query, members):
        block, block_labels = members
        allowed = query_labels[:, None] == block_labels[None, :]
        raw = jnp.einsum("qhd,khd->hqk", queries, block[:, 0], preferred_element_type=jnp.float32)
        scores = jnp.where(allowed[None], raw * scale_of, neg_big)
        probs = jnp.where(allowed[None], jnp.exp(scores - log_total[..., None]), 0.0)
        grad_probs = jnp.einsum(
            "qhd,khd->hqk", grad_attended, block[:, 1], preferred_element_type=jnp.float32
        )
        grad_raw = (probs * (grad_probs - delta_rows[..., None]) * scale_of).astype(jnp.bfloat16)
        new_grad = grad_query + jnp.einsum(
            "hqk,khd->qhd", grad_raw, block[:, 0], preferred_element_type=jnp.float32
        )
        grad_keys = jnp.einsum(
            "hqk,qhd->khd", grad_raw, queries, preferred_element_type=jnp.float32
        )
        grad_values = jnp.einsum(
            "hqk,qhd->khd",
            probs.astype(jnp.bfloat16),
            grad_attended,
            preferred_element_type=jnp.float32,
        )
        return (new_grad, jnp.stack([grad_keys, grad_values], axis=1))

    grad_query, grad_kv_blocks = lax.scan(
        back_block, jnp.zeros((local_rows, HEADS, HEAD_DIM), jnp.float32), (key_blocks, key_labels)
    )
    grad_kv = lax.psum_scatter(
        grad_kv_blocks.reshape(seq_len, 2 * D).astype(jnp.bfloat16),
        "blk",
        scatter_dimension=0,
        tiled=True,
    ).astype(jnp.float32)
    grad_projected = jnp.concatenate([grad_query.reshape(local_rows, D), grad_kv], axis=1).astype(
        jnp.bfloat16
    )
    grad_w_qkv = jnp.dot(normed_low.T, grad_projected, preferred_element_type=jnp.float32)
    grad_proj_rows = jnp.sum(grad_projected.astype(jnp.float32), axis=0)
    grad_bias_qv = jnp.concatenate([grad_proj_rows[:D], grad_proj_rows[2 * D :]])
    grad_normed_one = jnp.dot(grad_projected, w_qkv.T, preferred_element_type=jnp.float32)
    grad_in_norm, grad_gain_one, grad_shift_one = pull_one(grad_normed_one)
    grad_inputs = grad_middle + grad_in_norm
    shard_len = params.shape[0]
    total_params = shard_len * lax.axis_size(("dp", "blk"))
    flat_grad = jnp.concatenate(
        [
            grad_gain_one,
            grad_shift_one,
            grad_w_qkv.reshape(-1),
            grad_bias_qv,
            grad_w_out.reshape(-1),
            grad_bias_out,
            grad_gain_two,
            grad_shift_two,
            grad_up.reshape(-1),
            grad_bias_up,
            grad_down.reshape(-1),
            grad_bias_down,
            jnp.zeros((total_params - RAW,), jnp.float32),
        ]
    )
    shard_grad = lax.psum_scatter(
        lax.slice_in_dim(flat_grad, 0, lax.axis_size(("dp", "blk")) * shard_len, axis=0),
        ("dp", "blk"),
        scatter_dimension=0,
        tiled=True,
    )
    positions = lax.axis_index(("dp", "blk")) * shard_len + jnp.arange(shard_len, dtype=jnp.int32)
    marks = jnp.array(starts_of(D, FF), dtype=jnp.int32)
    group_of = jnp.sum((positions[:, None] >= marks[None, :]).astype(jnp.int32), axis=1) - 1
    squares = shard_grad * shard_grad
    partials = jnp.sum(
        jnp.where(
            group_of[None, :] == jnp.arange(GROUPS, dtype=jnp.int32)[:, None], squares[None, :], 0.0
        ),
        axis=1,
    )
    norms, bias_total = lax.psum((partials, grad_bias_down), ("dp", "blk"))
    clip_factor = 1.0 / jnp.maximum(jnp.sqrt(jnp.sum(norms)), 1.0)
    decayed = ((group_of == 2) | (group_of == 4) | (group_of == 8) | (group_of == 10)).astype(
        jnp.float32
    )
    scaled = clip_factor * shard_grad
    new_first = 0.9 * first_moment + 0.1 * scaled
    new_second = 0.999 * second_moment + 0.001 * scaled * scaled
    direction = new_first / (1.0 - 0.9**10) / (jnp.sqrt(new_second / (1.0 - 0.999**10)) + 1e-08)
    param_step = -0.001 * 0.9**12 * (direction + 0.05 * decayed * params)
    return (
        result.astype(jnp.bfloat16)[None],
        grad_inputs.astype(jnp.bfloat16)[None],
        norms,
        param_step,
        new_first,
        bias_total,
    )


MESH = pl.DeviceIdType.MESH
LANE = 128


def pick(cond, yes, no):
    return jnp.where(cond, jnp.int32(yes), jnp.int32(no))


def rdma(src, dst, ssem, rsem, dev):
    return pltpu.make_async_remote_copy(src_ref=src, dst_ref=dst, send_sem=ssem, recv_sem=rsem, device_id=dev, device_id_type=MESH)


def rows(ref, start, size, step=128):
    return ref.at[pl.ds(pl.multiple_of(start, step), size)]


def gate(peers):
    sem = pltpu.get_barrier_semaphore()
    for peer in peers:
        pl.semaphore_signal(sem, inc=1, device_id=peer, device_id_type=MESH)
    pl.semaphore_wait(sem, len(peers))


class Place:
    def __init__(self):
        self.dp = lax.axis_index("dp")
        self.blk = lax.axis_index("blk")
        self.d = self.dp * 4 + self.blk
        self.z = self.dp // 2
        self.x = self.dp % 2
        self.y = self.blk // 2
        self.c = self.blk % 2
        self.xpeer = (self.z * 2 + 1 - self.x, self.blk)
        self.zs = [lax.rem(self.z + k, 4) for k in (1, 3, 2)]
        self.zpeers = [(zz * 2 + self.x, self.blk) for zz in self.zs]
        self.quad = [(self.dp, lax.rem(self.blk + k, 4)) for k in (1, 2, 3)]
        up = lax.rem(self.d + 1, 32)
        down = lax.rem(self.d + 31, 32)
        self.above = (self.dp + 2, self.blk)
        self.below = (self.dp - 2, self.blk)
        self.others = self.zpeers + [(zz * 2 + 1 - self.x, self.blk) for zz in self.zs]
        self.next = (up // 4, up % 4)
        self.prev = (down // 4, down % 4)
        d = self.d
        self.is_qkv = d < 8
        self.is_out = (d == 8) | (d == 9)
        self.is_mix_out = d == 10
        self.is_up = (d >= 11) & (d < 21)
        self.is_mix_down = d == 21
        self.is_down = d >= 22
        self.is_seg = self.is_out | self.is_down
        self.is_mix = self.is_mix_out | self.is_mix_down
        self.base = pick(d < 8, 16, pick(d < 11, 32, pick(d < 21, 56, 88))) - 3 * d
        self.seg0 = pick(d < 11, 3 * (d - 8), jnp.maximum(3 * (d - 21) - 1, 0))
        self.mix_up = pick(self.is_mix_out, 2074, -7)
        self.mix_seg = pick(self.is_mix_out, 2, 1049)

    def seg_home(self, n):
        seg = self.seg0 + n // 4
        panel = n % 4
        out_row = 3072 + 256 * panel + 128 * (seg % 2)
        down_row = 8192 + 1024 * panel + 128 * (seg // 4)
        low = self.d < 11
        return pick(low, seg // 2, seg % 4), pick(low, out_row, down_row)

    def block_home(self, n):
        part, row = self.seg_home(n)
        return pick(self.is_qkv, n // 3, part), pick(self.is_qkv, (n % 3) * 1024 + 128 * self.d, row)

    def up_home(self, n):
        start = pick(self.is_up, 32 + 96 * (self.d - 11), pick(self.is_mix_out, 0, 992))
        return n // 4, 4096 + 1024 * (n % 4) + start


def chunk_row(q, k):
    first = (k // 4) * 1024 + 512 * q + 128 * (k % 4)
    turn = 3 * (q - 2) + k // 4
    panel = k % 4
    other = pick(
        turn < 2,
        3072 + 256 * panel + 128 * turn,
        pick(turn < 10, 4096 + 1024 * panel + 128 * (turn - 2), 8192 + 1024 * panel + 128 * (turn - 10)),
    )
    return pick(q < 2, first, other)


def loop(count, body):
    def step(i, carry):
        body(i)
        return carry

    lax.fori_loop(0, count, step, 0)


def unit_span(start, stride):
    return pl.ds(start, 16, stride=stride)


def for_tiles(me, visit):
    e0 = 24 + me.base

    @pl.when(me.is_qkv)
    def _():
        def body(rb):
            for ct in range(24):
                n = ((ct % 8) // 2) * 3 + ct // 8
                visit(e0 + 384 * rb + ct, 24, n * 128 + 16 * rb, 128 * (ct % 2))

        loop(8, body)

    @pl.when(me.is_up)
    def _():
        def body(rb):
            for ct in range(32):
                n = (ct % 4) * 4 + ct // 8
                visit(e0 + 512 * rb + ct, 32, n * 96 + 16 * rb, 128 * ((ct // 4) % 2))

        loop(6, body)

    def segs(count, first):
        def body(i):
            for ct in range(8):
                visit(first + 128 * i + ct, 8, ((i // 8) * 4 + ct // 2) * 128 + 16 * (i % 8), 128 * (ct % 2))

        loop(count, body)

    @pl.when(me.is_seg)
    def _():
        segs(24, e0)

    @pl.when(me.is_mix)
    def _():
        segs(16, 24 + me.mix_seg)

        def body(rb):
            for ct in range(32):
                n = (ct % 4) * 4 + ct // 8
                visit(24 + me.mix_up + 512 * rb + ct, 32, 1024 + n * 32 + 16 * rb, 128 * ((ct // 4) % 2))

        loop(2, body)


def for_pieces(me, visit):
    @pl.when(me.is_qkv | me.is_seg)
    def _():
        def body(n):
            part, row = me.block_home(n)
            visit(n, n * 128, 128, part, row, 128)

        loop(12, body)

    @pl.when(me.is_up)
    def _():
        def body(n):
            part, row = me.up_home(n)
            visit(n, n * 96, 96, part, row, 32)

        loop(16, body)

    @pl.when(me.is_mix)
    def _():
        def body(n):
            part, row = me.seg_home(n)
            visit(n, n * 128, 128, part, row, 128)

        loop(8, body)

        def body_up(n):
            part, row = me.up_home(n)
            visit(8 + n, 1024 + n * 32, 32, part, row, 32)

        loop(16, body_up)


def vec_spots(me, visit):
    for cond, row, unit, count in (
        (me.d == 0, 0, 0, 16),
        (me.d == 7, 0, 3067, 8),
        (me.d == 8, 0, 0, 8),
        (me.d == 10, 8, 2050, 24),
        (me.d == 21, 0, 1017, 32),
        (me.d == 31, 0, 3067, 8),
    ):

        @pl.when(cond)
        def _(row=row, unit=unit, count=count):
            visit(row, 24 + unit, count)


BF, F32 = jnp.bfloat16, jnp.float32
EPS = 1e-06
OUT0, UP0, DOWN0 = 3072, 4096, 8192


def dot(a, b):
    return lax.dot_general(a, b, (((1,), (0,)), ((), ())), preferred_element_type=F32)


def dot_nt(a, b):
    return lax.dot_general(a, b, (((1,), (1,)), ((), ())), preferred_element_type=F32)


def dot_tn(a, b):
    return lax.dot_general(a, b, (((0,), (0,)), ((), ())), preferred_element_type=F32)


def block_of(i):
    return pl.ds(pl.multiple_of(i * 256, 256), 256)


def wide(r, q, first, count=8):
    return jnp.concatenate([r.XV[q, first + i : first + i + 1, :] for i in range(count)], axis=1)


def narrow(r, q, first):
    return jnp.concatenate([r.XV[q, pl.ds(first + i, 1), :] for i in range(2)], axis=1)


def put_vec(r, q, first, row, add=False):
    for i in range(row.shape[1] // 128):
        part = row[:, i * 128 : i * 128 + 128]
        if add:
            part = part + r.VG[q, first + i : first + i + 1, :]
        r.VG[q, first + i : first + i + 1, :] = part


def normalize(x):
    mean = jnp.mean(x, axis=-1, keepdims=True)
    cen = x - mean
    var = jnp.mean(cen * cen, axis=-1, keepdims=True)
    scale = lax.rsqrt(var + EPS)
    return cen * scale, scale


def norm_back(dy, xhat, scale, gain):
    t = dy * gain
    return scale * (t - jnp.mean(t, axis=-1, keepdims=True) - xhat * jnp.mean(t * xhat, axis=-1, keepdims=True))


def labels_at(r, at):
    total = jnp.zeros_like(at)
    bound = 0
    for k in range(9):
        bound = bound + r.lens[k]
        total = total + (at >= bound).astype(jnp.int32)
    return total


def lane_mask(h):
    lane = lax.broadcasted_iota(jnp.int32, (1, 128), 1)
    return ((lane // 64) == h).astype(BF)


def crow(q, k):
    return pick(q < 2, 128 * k, 384 * (k % 4) + 128 * (k // 4))


class Other(Place):
    def __init__(self, me, i):
        d = me.dp * 4 + i
        self.d, self.blk, self.dp = d, i, me.dp
        self.is_qkv = d < 8
        self.is_out = (d == 8) | (d == 9)
        self.is_mix_out = d == 10
        self.is_up = (d >= 11) & (d < 21)
        self.is_mix_down = d == 21
        self.is_down = d >= 22
        self.is_seg = self.is_out | self.is_down
        self.is_mix = self.is_mix_out | self.is_mix_down
        self.seg0 = pick(d < 11, 3 * (d - 8), jnp.maximum(3 * (d - 21) - 1, 0))

    def seg_spot(self, n):
        seg = self.seg0 + n // 4
        low = self.d < 11
        turn = pick(low, seg % 2, 10 + seg // 4 - 3 * (self.dp - 2))
        return pick(low, seg // 2, seg % 4), 384 * (n % 4) + 128 * turn

    def block_spot(self, n):
        part, row = self.seg_spot(n)
        return pick(self.is_qkv, n // 3, part), pick(self.is_qkv, (n % 3) * 512 + 128 * (self.d % 4), row)

    def up_spot(self, n):
        start = pick(self.is_up, 32 + 96 * (self.d - 11), pick(self.is_mix_out, 0, 992))
        return n // 4, 384 * (n % 4) + 256 + start - 384 * (self.dp - 2)

    def pieces(self, visit):
        @pl.when(self.is_qkv | self.is_seg)
        def _():
            loop(12, lambda n: visit(n, n * 128, 128, *self.block_spot(n)))

        @pl.when(self.is_up)
        def _():
            loop(16, lambda n: visit(n, n * 96, 96, *self.up_spot(n)))

        @pl.when(self.is_mix)
        def _():
            loop(8, lambda n: visit(n, n * 128, 128, *self.seg_spot(n)))
            loop(16, lambda n: visit(8 + n, 1024 + n * 32, 32, *self.up_spot(n)))


def arrived(ref, sem):
    pltpu.make_async_copy(ref, ref, sem).wait()


def squares(x):
    s = jnp.sum(x * x, axis=0, keepdims=True)
    return s[:, :128] + s[:, 128:] if x.shape[1] == 256 else s


def reduce_vectors(me, r):
    for zz in range(4):
        arrived(r.VX.at[0], r.wxr.at[zz])
        r.VX[zz] = r.VX[zz] + r.VG[zz * 2 + me.x]

        @pl.when(me.z != zz)
        def _():
            rdma(r.VX.at[zz], r.VZ.at[me.z], r.wzs.at[zz], r.wzr.at[me.z], (zz * 2 + me.x, me.blk)).start()

    total = r.VX[me.z]
    for zz in me.zs:
        arrived(r.VZ.at[0], r.wzr.at[zz])
        total = total + r.VZ[zz]
    r.VT[me.blk] = total
    outs = [rdma(r.VT.at[me.blk], r.VT.at[me.blk], r.wqs, r.wqr.at[me.blk], peer) for peer in me.quad]
    for o in outs:
        o.start()
    for k in (1, 2, 3):
        arrived(r.VT.at[0], r.wqr.at[lax.rem(me.blk + k, 4)])
    r.VS[...] = r.VT[0] + r.VT[1] + r.VT[2] + r.VT[3]


def norm_exchange(me, r):
    zx = [(me.z + 1 - 2 * (me.z % 2)), lax.rem(me.z + 2, 4)]
    peers = [(me.dp, me.y * 2 + 1 - me.c), (me.dp, (1 - me.y) * 2 + me.c), me.xpeer] + [(z * 2 + me.x, me.blk) for z in zx]
    for n, peer in enumerate(peers):
        cp = rdma(r.NB.at[n], r.NR.at[n], r.nsem.at[n], r.nrsem.at[n], peer)
        cp.start()
        cp.wait()
        r.NB[n + 1] = r.NB[n] + r.NR[n]


def by_z(me, values):
    out = jnp.int32(values[0])
    for n in (1, 2, 3):
        out = pick(me.z == n, values[n], out)
    return out


GATHER_ORDER = (
    (0, 1, 2, 3, 4, 5, 6, 7, 8, 9, 10, 11),
    (3, 0, 1, 2, 4, 5, 6, 7, 8, 9, 10, 11),
    (6, 7, 0, 1, 2, 9, 3, 10, 4, 11, 8, 5),
    (9, 10, 11, 0, 1, 2, 6, 3, 7, 4, 8, 5),
)
REDUCE_ORDER = (
    (9, 10, 11, 6, 7, 8, 3, 4, 5, 12, 12, 12, 12, 12),
    (12, 9, 10, 11, 6, 7, 8, 12, 12, 12, 12, 0, 1, 2),
    (12, 12, 9, 10, 11, 12, 12, 3, 4, 5, 0, 1, 2, 12),
    (12, 12, 12, 6, 7, 8, 3, 4, 5, 0, 1, 2, 12, 12),
)


def prepare(me, r):
    r.tail[...] = r.par[3051:3075, :]
    up = rdma(r.tail, r.hp, r.hsem.at[0], r.hsem.at[1], me.next)
    down = rdma(r.par.at[0:24], r.hn, r.hsem.at[2], r.hsem.at[3], me.prev)
    up.start()
    down.start()

    def put(i):
        r.E[pl.ds(pl.multiple_of(24 + 64 * i, 8), 64), :] = r.par[pl.ds(pl.multiple_of(64 * i, 8), 64), :]

    loop(48, put)
    r.E[3096:3099, :] = r.par[3072:3075, :]
    r.VS[...] = jnp.zeros_like(r.VS)

    def vec(row, unit, count):
        r.VS[row : row + count, :] = r.E[unit : unit + count, :].astype(BF).astype(F32)

    vec_spots(me, vec)
    vq = [rdma(r.VS, r.VQ.at[me.blk], r.vsem.at[0], r.vsem.at[1], peer) for peer in me.quad]
    for v in vq:
        v.start()
    r.VQ[me.blk] = r.VS[...]
    up.wait()
    down.wait()
    r.E[0:24, :] = r.hp[...]
    r.E[3099:3123, :] = r.hn[...]

    def tile(unit, stride, row, lane):
        r.S[pl.ds(pl.multiple_of(row, 16), 16), lane : lane + 128] = r.E[unit_span(unit, stride), :].astype(BF)

    for_tiles(me, tile)

    def visit(i, srow, size, part, frow, step):
        src, dst = rows(r.S, srow, size, 32), rows(r.F, frow, size, step)

        @pl.when(part != me.blk)
        def _():
            rdma(src, dst, r.qsem.at[i], r.csem, (me.dp, part)).start()

        @pl.when(part == me.blk)
        def _():
            pltpu.make_async_copy(src, dst, r.csem).start()

    for_pieces(me, visit)
    arrived(r.VQ.at[0:3], r.vsem.at[0])
    arrived(r.VQ.at[0:3], r.vsem.at[1])
    r.XV[me.dp] = r.VQ[0] + r.VQ[1] + r.VQ[2] + r.VQ[3]
    for peer in me.others + [me.xpeer]:
        rdma(r.XV.at[me.dp], r.XV.at[me.dp], r.vxs, r.vxr.at[me.dp], peer).start()
    arrived(r.F.at[0:1536], r.csem)


def prepare_drain(me, r):
    def visit(i, srow, size, part, frow, step):
        @pl.when(part != me.blk)
        def _():
            arrived(rows(r.S, srow, size, 32), r.qsem.at[i])

    for_pieces(me, visit)
    arrived(r.XV.at[0:7], r.vxs)


def gather_step(me, r, s):
    e = by_z(me, [order[s] for order in GATHER_ORDER])
    zz, g = e // 3, e % 3

    @pl.when(zz != me.z)
    def _():
        arrived(r.F.at[0:512], r.zr.at[e])

    def block(i):
        return rows(r.F, chunk_row(zz * 2 + me.x, g * 4 + i), 128)

    @pl.when((zz <= me.z) & (me.z < 3))
    def _():
        for i in range(4):
            rdma(block(i), block(i), r.zsu.at[zz], r.zr.at[e], me.above).start()

    @pl.when((zz >= me.z) & (me.z > 0))
    def _():
        for i in range(4):
            rdma(block(i), block(i), r.zsd.at[zz], r.zr.at[e], me.below).start()

    for i in range(4):
        rdma(block(i), block(i), r.xs, r.xr.at[e], me.xpeer).start()


def gathered(me, r, entries):
    for e in entries:
        arrived(r.F.at[0:512], r.xr.at[e])


def gather_drain(me, r):
    arrived(r.F.at[0:6144], r.xs)
    for zz in range(4):
        @pl.when((zz <= me.z) & (me.z < 3))
        def _():
            arrived(r.F.at[0:1536], r.zsu.at[zz])

        @pl.when((zz >= me.z) & (me.z > 0))
        def _():
            arrived(r.F.at[0:1536], r.zsd.at[zz])


def share_rows(me, r):
    mine = block_of(me.blk)
    for n, (src, dst) in enumerate(((r.pat, r.PA), (r.cot, r.CA))):
        for peer in me.quad:
            rdma(src, dst.at[mine], r.asem.at[2 * n], r.asem.at[2 * n + 1], peer).start()
        dst[mine, :] = src[...]


def nothing(n):
    pass


def quad_sum(me, r, make, sems, finish, slot, buf=None, idle=nothing):
    y, c = me.y, me.c
    sib, yp = (me.dp, y * 2 + 1 - c), (me.dp, (1 - y) * 2 + c)
    far_sib, far, near_sib, own = (1 - y) * 2 + 1 - c, (1 - y) * 2 + c, y * 2 + 1 - c, me.blk
    ssem, rsem = sems

    def copy(src, dst, n, dev):
        return rdma(src, dst, ssem.at[n], rsem.at[n], dev)

    def at(dev, i):
        return pl.ds(pl.multiple_of(dev * 256 + 64 * i, 64), 64)

    make(far_sib)
    a = copy(r.PB.at[block_of(far_sib)], r.RB.at[0], 0, sib)
    a.start()
    make(far)
    a.wait_recv()
    over = []
    for i in range(4):
        lo = pl.ds(64 * i, 64)
        r.RB[3, lo, :] = (r.PB[at(far, i), :].astype(F32) + r.RB[0, lo, :].astype(F32)).astype(BF)
        over.append(copy(r.RB.at[3, lo], r.RB.at[slot, lo], 2 + i, yp))
        over[i].start()
    make(near_sib)
    d = copy(r.PB.at[block_of(near_sib)], r.RB.at[1], 1, sib)
    d.start()
    make(own)
    idle(0)
    d.wait_recv()
    out, near, on = [], [], []
    for i in range(4):
        over[i].wait_recv()
        lo = slice(64 * i, 64 * i + 64)
        finish(lo, r.PB[at(own, i), :].astype(F32) + r.RB[1, lo, :].astype(F32) + r.RB[slot, lo, :].astype(F32))
        if buf is not None:
            part, passed = buf.at[at(own, i)], buf.at[at(far, i)]
            out.append(copy(part, part, 6 + i, yp))
            near.append(copy(part, part, 10 + i, sib))
            on.append(copy(passed, passed, 14 + i, sib))
            out[i].start()
            near[i].start()
    idle(1)
    for i in range(len(out)):
        out[i].wait_recv()
        on[i].start()
    for cp in near + on:
        cp.wait()
    for cp in [a, d] + over + out:
        cp.wait_send()


def first_norm(me, r):
    arrived(r.PA.at[0:768], r.asem.at[1])
    for peer in range(1, 8):
        arrived(r.XV.at[0], r.vxr.at[lax.rem(me.dp + peer, 8)])
    gain, shift = wide(r, 0, 0), wide(r, 0, 8)

    def ln(i):
        at = pl.ds(pl.multiple_of(i * 64, 64), 64)
        xhat, _ = normalize(r.PA[at, :].astype(F32))
        r.PA[at, :] = (xhat * gain + shift).astype(BF)

    loop(16, ln)


def attention(me, r, idle):
    bias = [narrow(r, 1, 2 * me.blk), None, narrow(r, 2, 2 * me.blk)]

    def proj(i):
        at = block_of(i)
        for j in range(3):
            out = dot(r.PA[at, :], r.F[j * 1024 : j * 1024 + 1024, :])
            if bias[j] is not None:
                out = out + bias[j]
            r.QKV[j, at, :] = out.astype(BF)

    loop(4, proj)
    idle(0)
    key_labels = labels_at(r, lax.broadcasted_iota(jnp.int32, (1, 1024), 1))

    def attend(i):
        at = block_of(i)
        row_labels = labels_at(r, lax.broadcasted_iota(jnp.int32, (256, 1), 0) + i * 256)
        allowed = row_labels == key_labels
        for t in range(2):
            lanes = slice(128 * t, 128 * t + 128)
            q = r.QKV[0, at, lanes]
            k = r.QKV[1, :, lanes]
            v = r.QKV[2, :, lanes]
            out = jnp.zeros((256, 128), F32)
            for h in range(2):
                m = lane_mask(h)
                s = jnp.where(allowed, dot_nt(q * m, k) * 0.125, -1e30)
                w = jnp.exp(s - jnp.max(s, axis=-1, keepdims=True))
                p = (w * (1.0 / jnp.sum(w, axis=-1, keepdims=True))).astype(BF)
                r.P[2 * t + h, at, :] = p
                out = out + dot(p, v * m)
            r.AT[at, lanes] = out.astype(BF)

    loop(2, attend)
    idle(1)
    loop(2, lambda i: attend(i + 2))


def second_norm(me, r, idle):
    def term(i):
        at = block_of(i)
        for p in range(4):
            r.PB[at, 256 * p : 256 * p + 256] = dot(r.AT[at, :], r.F[OUT0 + 256 * p : OUT0 + 256 * p + 256, :]).astype(BF)

    bias_out = wide(r, 2, 8)
    gain, shift = wide(r, 2, 16), wide(r, 2, 24)

    def finish(lo, total):
        x = r.pat[lo, :].astype(F32) + (total + bias_out)
        r.MID[lo, :] = x
        xhat, _ = normalize(x)
        r.NT[pl.ds(pl.multiple_of(me.blk * 256 + lo.start, 64), 64), :] = (xhat * gain + shift).astype(BF)

    quad_sum(me, r, term, (r.s1s, r.s1r), finish, 2, r.NT, idle)


def hidden(me, r):
    biases = [jnp.concatenate([r.XV[5, pl.ds(4 * (2 * p + i) + me.blk, 1), :] for i in range(2)], axis=1) for p in range(4)]

    def up(i):
        at = pl.ds(pl.multiple_of(i * 128, 128), 128)
        for p in range(4):
            h = dot(r.NT[at, :], r.F[UP0 + 1024 * p : UP0 + 1024 * p + 1024, :]) + biases[p]
            phi = 0.5 + 0.5 * lax.erf(h * 0.7071067811865476)
            lanes = slice(256 * p, 256 * p + 256)
            r.AC[at, lanes] = (h * phi).astype(BF)
            r.GP[at, lanes] = (phi + h * (jnp.exp(-0.5 * h * h) * 0.3989422804014327)).astype(BF)

    loop(8, up)


def hidden_grad(me, r):
    arrived(r.CA.at[0:768], r.asem.at[3])

    def body(i):
        at = block_of(i)
        for p in range(4):
            lanes = slice(256 * p, 256 * p + 256)
            acc = jnp.zeros((256, 256), F32)
            for k in range(4):
                down = r.F[DOWN0 + 1024 * k + 256 * p : DOWN0 + 1024 * k + 256 * p + 256, :]
                acc = acc + dot_nt(r.CA[at, 256 * k : 256 * k + 256], down)
            r.GH[at, lanes] = (acc * r.GP[at, lanes].astype(F32)).astype(BF)

    loop(4, body)


def hidden_sums(me, r):
    for p in range(4):
        sums = jnp.sum(r.GH[:, 256 * p : 256 * p + 256].astype(F32), axis=0, keepdims=True)
        for i in range(2):
            r.VG[5, pl.ds(4 * (2 * p + i) + me.blk, 1), :] = sums[:, 128 * i : 128 * i + 128]
    put_vec(r, 7, 0, jnp.sum(r.cot[...].astype(F32), axis=0, keepdims=True))


def weight_grad(r, left, right, base, height):
    def body(i):
        cols = pl.ds(pl.multiple_of(i * 256, 256), 256)
        lt = left[:, cols].T
        for p in range(right.shape[1] // 256):
            out = dot(lt, right[:, 256 * p : 256 * p + 256])
            r.G[pl.ds(pl.multiple_of(base + p * height + i * 256, 256), 256), :] = out.astype(BF)

    loop(height // 256, body)


def middle_grad(me, r, idle):
    def term(i):
        at = block_of(i)
        for n in range(4):
            acc = jnp.zeros((256, 256), F32)
            for p in range(4):
                up = r.F[UP0 + 1024 * p + 256 * n : UP0 + 1024 * p + 256 * n + 256, :]
                acc = acc + dot_nt(r.GH[at, 256 * p : 256 * p + 256], up)
            r.PB[at, 256 * n : 256 * n + 256] = acc.astype(BF)

    gain = wide(r, 2, 16)
    sums = [jnp.zeros((1, 1024), F32)] * 3

    def finish(lo, dy):
        xhat, scale = normalize(r.MID[lo, :])
        gm = r.cot[lo, :].astype(F32) + norm_back(dy, xhat, scale, gain)
        r.GMID[lo, :] = gm
        low = gm.astype(BF)
        r.NT[pl.ds(pl.multiple_of(me.blk * 256 + lo.start, 64), 64), :] = low
        for n, term_of in enumerate((low.astype(F32), dy * xhat, dy)):
            sums[n] = sums[n] + jnp.sum(term_of, axis=0, keepdims=True)

    quad_sum(me, r, term, (r.s2s, r.s2r), finish, 4, r.NT, idle)
    for n in range(3):
        put_vec(r, 2, 8 + 8 * n, sums[n])


def attended_grad(me, r):
    def body(i):
        at = block_of(i)
        acc = jnp.zeros((256, 256), F32)
        for p in range(4):
            acc = acc + dot_nt(r.NT[at, 256 * p : 256 * p + 256], r.F[OUT0 + 256 * p : OUT0 + 256 * p + 256, :])
        r.GP[at, 768:1024] = acc.astype(BF)

    loop(4, body)


def attention_grad(me, r, idle):
    r.KV[...] = jnp.zeros_like(r.KV)

    def attend(i):
        at = block_of(i)
        for t in range(2):
            lanes = slice(128 * t, 128 * t + 128)
            q = r.QKV[0, at, lanes]
            k = r.QKV[1, :, lanes]
            v = r.QKV[2, :, lanes]
            da = r.GP[at, 768 + 128 * t : 896 + 128 * t]
            dq = jnp.zeros((256, 128), F32)
            for h in range(2):
                m = lane_mask(h)
                p = r.P[2 * t + h, at, :]
                pf = p.astype(F32)
                dp = dot_nt(da * m, v)
                delta = jnp.sum(pf * dp, axis=-1, keepdims=True)
                ds = (pf * (dp - delta) * 0.125).astype(BF)
                dq = dq + dot(ds, k * m)
                r.KV[0, :, lanes] += dot_tn(ds, q * m)
                r.KV[1, :, lanes] += dot_tn(p, da * m)
            r.GP[at, lanes] = dq.astype(BF)

    loop(2, attend)
    idle(0)
    loop(2, lambda i: attend(i + 2))
    r.GP[:, 256:512] = r.KV[0].astype(BF)
    r.GP[:, 512:768] = r.KV[1].astype(BF)


def projection_sums(me, r):
    for j, q in ((0, 1), (2, 2)):
        sums = jnp.sum(r.GP[:, 256 * j : 256 * j + 256].astype(F32), axis=0, keepdims=True)
        for i in range(2):
            r.VG[q, pl.ds(2 * me.blk + i, 1), :] = sums[:, 128 * i : 128 * i + 128]


def projection_grad(me, r):
    def body(i):
        cols = pl.ds(pl.multiple_of(i * 256, 256), 256)
        lt = r.PA[:, cols].T
        for j in range(3):
            r.G[pl.ds(pl.multiple_of(j * 1024 + i * 256, 256), 256), :] = dot(lt, r.GP[:, 256 * j : 256 * j + 256]).astype(BF)

    loop(4, body)


def input_grad(me, r, idle):
    def term(i):
        at = block_of(i)
        for n in range(4):
            acc = jnp.zeros((256, 256), F32)
            for j in range(3):
                acc = acc + dot_nt(r.GP[at, 256 * j : 256 * j + 256], r.F[1024 * j + 256 * n : 1024 * j + 256 * n + 256, :])
            r.PB[at, 256 * n : 256 * n + 256] = acc.astype(BF)

    gain = wide(r, 0, 0)
    sums = [jnp.zeros((1, 1024), F32)] * 2

    def finish(lo, dy):
        xhat, scale = normalize(r.pat[lo, :].astype(F32))
        r.ing[lo, :] = (r.GMID[lo, :] + norm_back(dy, xhat, scale, gain)).astype(BF)
        for n, term_of in enumerate((dy * xhat, dy)):
            sums[n] = sums[n] + jnp.sum(term_of, axis=0, keepdims=True)

    quad_sum(me, r, term, (r.s3s, r.s3r), finish, 2, None, idle)
    for n in range(2):
        put_vec(r, 0, 8 * n, sums[n])


def layer_out(me, r, idle):
    def term(i):
        at = block_of(i)
        for p in range(4):
            r.PB[at, 256 * p : 256 * p + 256] = dot(r.AC[at, :], r.F[DOWN0 + 1024 * p : DOWN0 + 1024 * p + 1024, :]).astype(BF)

    bias_down = wide(r, 7, 0)

    def finish(lo, total):
        r.act[lo, :] = (r.MID[lo, :] + (total + bias_down)).astype(BF)

    quad_sum(me, r, term, (r.s4s, r.s4r), finish, 4, None, idle)


def reduce_send(me, r, entries):
    for e in entries:
        zz, g = e // 3, e % 3
        q = zz * 2 + 1 - me.x

        def body(i, q=q, zz=zz, g=g, e=e):
            k = g * 4 + i
            rdma(rows(r.G, chunk_row(q, k), 128), rows(r.XR.at[zz], crow(q, k), 128), r.rxs, r.rxr.at[e], me.xpeer).start()

        loop(4, body)


def reduce_step(me, r, s):
    e = by_z(me, [order[s] for order in REDUCE_ORDER])

    @pl.when(e < 12)
    def _():
        zz, g = e // 3, e % 3
        q = zz * 2 + me.x
        down = zz < me.z
        arrived(r.G.at[0:512], r.rxr.at[e])

        @pl.when((me.z > 0) & (me.z < 3))
        def _():
            arrived(r.G.at[0:512], r.rzr.at[e])

        def body(i):
            k = g * 4 + i
            src, at = pl.ds(pl.multiple_of(chunk_row(q, k), 128), 128), pl.ds(pl.multiple_of(crow(q, k), 128), 128)
            total = r.G[src, :].astype(F32) + r.XR[zz, at, :].astype(F32) + r.ZR[zz, at, :].astype(F32)
            r.XR[zz, at, :] = total.astype(BF)
            sent = rows(r.XR.at[zz], crow(q, k), 128)

            @pl.when(down)
            def _():
                rdma(sent, rows(r.ZR.at[zz], crow(q, k), 128), r.rzs.at[zz], r.rzr.at[e], me.below).start()

            @pl.when(jnp.logical_not(down))
            def _():
                last = zz == me.z + 1
                slot, sem = pick(last, 4, zz), pick(last, 12 + g, e)
                rdma(sent, rows(r.ZR.at[slot], crow(q, k), 128), r.rzs.at[zz], r.rzr.at[sem], me.above).start()

        loop(4, body)


def reduce_last(me, r):
    first_tensor = pick(me.dp < 2, 2, pick(me.dp == 2, 4, pick(me.dp < 6, 8, 10)))
    for g in range(3):
        e = me.z * 3 + g
        arrived(r.G.at[0:512], r.rxr.at[e])

        @pl.when(me.z < 3)
        def _():
            arrived(r.G.at[0:512], r.rzr.at[e])

        @pl.when(me.z > 0)
        def _():
            arrived(r.G.at[0:512], r.rzr.at[12 + g])

        part = jnp.zeros((1, 128), F32)
        for i in range(4):
            k = g * 4 + i
            src, at = pl.ds(pl.multiple_of(chunk_row(me.dp, k), 128), 128), pl.ds(pl.multiple_of(crow(me.dp, k), 128), 128)
            total = r.G[src, :].astype(F32) + r.XR[me.z, at, :].astype(F32)
            total = total + (r.ZR[me.z, at, :].astype(F32) + r.ZR[4, at, :].astype(F32))
            part = part + squares(total)
            r.XR[me.z, at, :] = total.astype(BF)
        tensor = first_tensor
        if g == 2:
            tensor = pick(me.dp == 2, 8, tensor)
        if g >= 1:
            tensor = pick(me.dp == 5, 10, tensor)
        r.NB[0, pl.ds(tensor, 1), :] += part
    for i in range(4):
        def visit(n, srow, size, part, row, i=i):
            src, dst = rows(r.XR.at[me.z], row, size, 32), rows(r.S, srow, size, 32)

            @pl.when((part == me.blk) & (me.blk != i))
            def _():
                rdma(src, dst, r.qsem2.at[i * 24 + n], r.csem2, (me.dp, i)).start()

            @pl.when((part == me.blk) & (me.blk == i))
            def _():
                pltpu.make_async_copy(src, dst, r.csem2).start()

        Other(me, i).pieces(visit)


def vector_squares(me, r):
    for q, tensors in ((0, (0, 1, None, None)), (1, (3, None, None, None)), (2, (3, 5, 6, 7)), (5, (9, 9, 9, 9)), (7, (11, None, None, None))):
        @pl.when((me.dp == q) & (me.blk == 0))
        def _(q=q, tensors=tensors):
            for g, tensor in enumerate(tensors):
                if tensor is not None:
                    r.NB[0, tensor : tensor + 1, :] += squares(r.VS[8 * g : 8 * g + 8, :])
            if q == 7:
                r.NB[0, 16:24, :] = r.VS[0:8, :]


def reduce_drain(me, r):
    arrived(r.G.at[0:6144], r.rxs)
    arrived(r.VX.at[0:3], r.wqs)
    arrived(r.VX, r.wxs)
    for i in range(4):
        @pl.when(me.z != i)
        def _(i=i):
            arrived(r.G.at[0:1536], r.rzs.at[i])
            arrived(r.VX.at[0], r.wzs.at[i])

        def visit(n, srow, size, part, row, i=i):
            @pl.when((part == me.blk) & (me.blk != i))
            def _():
                arrived(rows(r.XR.at[me.z], row, size, 32), r.qsem2.at[i * 24 + n])

        Other(me, i).pieces(visit)


def units_phase(me, r):
    arrived(r.S, r.csem2)
    for lo, hi in ((0, 48), (3072, 3128)):
        r.E[lo:hi, :] = jnp.zeros((hi - lo, 128), F32)

    def tile(unit, stride, row, lane):
        r.E[unit_span(unit, stride), :] = r.S[pl.ds(pl.multiple_of(row, 16), 16), lane : lane + 128].astype(F32)

    for_tiles(me, tile)

    def vec(row, unit, count):
        r.E[unit : unit + count, :] = r.VS[row : row + count, :]

    vec_spots(me, vec)
    r.tail[...] = r.E[3099:3123, :]
    up = rdma(r.tail, r.hp, r.hsem2.at[0], r.hsem2.at[1], me.next)
    down = rdma(r.E.at[0:24], r.hn, r.hsem2.at[2], r.hsem2.at[3], me.prev)
    up.start()
    down.start()

    def put(i):
        r.grad[pl.ds(pl.multiple_of(64 * i, 8), 64), :] = r.E[pl.ds(pl.multiple_of(24 + 64 * i, 8), 64), :]

    loop(48, put)
    r.grad[3072:3075, :] = r.E[3096:3099, :]
    up.wait()
    down.wait()
    r.grad[0:24, :] += r.hp[...]
    r.grad[3051:3075, :] += r.hn[...]


def whole_layer(me, r):
    r.VG[...] = jnp.zeros_like(r.VG)
    r.NB[0] = jnp.zeros((24, 128), F32)

    def clear(slot):
        r.ZR[slot] = jnp.zeros((1536, 256), BF)

    @pl.when(me.z == 0)
    def _():
        loop(4, lambda i: clear(i + 1))

    @pl.when(me.z == 3)
    def _():
        loop(4, clear)

    gate(me.quad + me.others + [me.xpeer, me.next, me.prev])
    prepare(me, r)
    for s in range(3):
        gather_step(me, r, s)
        if s == 0:
            share_rows(me, r)
    first_norm(me, r)
    for s in range(3, 6):
        gather_step(me, r, s)
    prepare_drain(me, r)
    gathered(me, r, (0, 1, 2))
    attention(me, r, lambda n: gather_step(me, r, 6 + n))
    gather_step(me, r, 8)
    gather_step(me, r, 9)
    gathered(me, r, (3, 4))
    second_norm(me, r, lambda n: gather_step(me, r, 10 + n))
    gathered(me, r, (5, 6, 7, 8))
    hidden(me, r)
    gathered(me, r, (9, 10, 11))
    gather_drain(me, r)
    hidden_grad(me, r)
    weight_grad(r, r.AC, r.CA, DOWN0, 1024)
    reduce_send(me, r, (9, 10, 11))
    weight_grad(r, r.NT, r.GH, UP0, 1024)
    reduce_send(me, r, (6, 7, 8))

    def steps(*numbers):
        for s in numbers:
            reduce_step(me, r, s)

    middle_grad(me, r, lambda n: steps(2 * n, 2 * n + 1))
    weight_grad(r, r.AT, r.NT, OUT0, 256)
    reduce_send(me, r, (3, 4, 5))
    attended_grad(me, r)
    attention_grad(me, r, lambda n: steps(4))
    projection_grad(me, r)
    reduce_send(me, r, (0, 1, 2))
    steps(5, 6)
    hidden_sums(me, r)
    projection_sums(me, r)
    input_grad(me, r, lambda n: steps(7 + n))
    for zz in range(4):
        rdma(r.VG.at[zz * 2 + 1 - me.x], r.VX.at[zz], r.wxs, r.wxr.at[zz], me.xpeer).start()
    layer_out(me, r, lambda n: steps(9 + n))
    steps(11, 12, 13)
    reduce_vectors(me, r)
    vector_squares(me, r)
    reduce_last(me, r)
    norm_exchange(me, r)
    units_phase(me, r)
    r.norms[...] = r.NB[5]
    reduce_drain(me, r)
    arrived(r.PA.at[0:768], r.asem.at[0])
    arrived(r.PA.at[0:768], r.asem.at[2])


DMA = pltpu.SemaphoreType.DMA
VMEM = pltpu.VMEM
SCRATCH = dict(
    F=VMEM((12288, 256), BF),
    G=VMEM((12288, 256), BF),
    XV=VMEM((8, 32, 128), F32),
    PA=VMEM((1024, 1024), BF),
    CA=VMEM((1024, 1024), BF),
    E=VMEM((3128, 128), F32),
    S=VMEM((1536, 256), BF),
    VS=VMEM((32, 128), F32),
    VQ=VMEM((4, 32, 128), F32),
    VG=VMEM((8, 32, 128), F32),
    VX=VMEM((4, 32, 128), F32),
    VZ=VMEM((4, 32, 128), F32),
    VT=VMEM((4, 32, 128), F32),
    NB=VMEM((6, 24, 128), F32),
    NR=VMEM((5, 24, 128), F32),
    tail=VMEM((24, 128), F32),
    hp=VMEM((24, 128), F32),
    hn=VMEM((24, 128), F32),
    XR=VMEM((4, 1536, 256), BF),
    ZR=VMEM((5, 1536, 256), BF),
    QKV=VMEM((3, 1024, 256), BF),
    P=VMEM((4, 1024, 1024), BF),
    AT=VMEM((1024, 256), BF),
    PB=VMEM((1024, 1024), BF),
    RB=VMEM((5, 256, 1024), BF),
    MID=VMEM((256, 1024), F32),
    GMID=VMEM((256, 1024), F32),
    NT=VMEM((1024, 1024), BF),
    AC=VMEM((1024, 1024), BF),
    GP=VMEM((1024, 1024), BF),
    GH=VMEM((1024, 1024), BF),
    KV=VMEM((2, 1024, 256), F32),
    hsem=DMA((4,)), asem=DMA((4,)), qsem=DMA((24,)), csem=DMA, vsem=DMA((2,)), vxs=DMA, vxr=DMA((8,)),
    xs=DMA, xr=DMA((12,)), zsu=DMA((4,)), zsd=DMA((4,)), zr=DMA((12,)),
    s1s=DMA((18,)), s1r=DMA((18,)), s2s=DMA((18,)), s2r=DMA((18,)),
    s3s=DMA((18,)), s3r=DMA((18,)), s4s=DMA((18,)), s4r=DMA((18,)),
    hsem2=DMA((4,)), rxs=DMA, rxr=DMA((12,)), rzs=DMA((4,)), rzr=DMA((15,)),
    wxs=DMA, wxr=DMA((4,)), wzs=DMA((4,)), wzr=DMA((4,)), wqs=DMA, wqr=DMA((4,)),
    qsem2=DMA((96,)), csem2=DMA, nsem=DMA((5,)), nrsem=DMA((5,)),
)


class Refs:
    pass


def fast_layer(lens, pat, cot, par):
    outs = dict(
        act=((256, 1024), BF), ing=((256, 1024), BF), grad=((3075, 128), F32), norms=((24, 128), F32)
    )
    names = ["lens", "pat", "cot", "par"] + list(outs) + list(SCRATCH)

    def kernel(*refs):
        r = Refs()
        for name, ref in zip(names, refs):
            setattr(r, name, ref)
        whole_layer(Place(), r)

    whole = pl.BlockSpec(memory_space=pltpu.VMEM)
    return pl.pallas_call(
        kernel,
        out_shape=[jax.ShapeDtypeStruct(*o) for o in outs.values()],
        in_specs=[pl.BlockSpec(memory_space=pltpu.SMEM)] + [whole] * 3,
        out_specs=[whole] * len(outs),
        scratch_shapes=list(SCRATCH.values()),
        compiler_params=pltpu.CompilerParams(collective_id=0, has_side_effects=True, vmem_limit_bytes=VMEM_LIMIT),
    )(lens, pat, cot, par)


VMEM_LIMIT = 63 * 2**20
PLAIN_UNITS = ((0, 16), (24592, 24608), (32800, 32824), (65592, 65624), (98392, 98400))


def fast_shards(pat, cot, lens, params, m, v):
    def units(a):
        return a.reshape(-1, LANE)

    par = units(params)
    act, ing, grad, nb = fast_layer(lens[0], pat[0], cot[0], par)
    norms = jnp.sum(nb[:GROUPS], axis=1)
    clip = 1.0 / jnp.maximum(jnp.sqrt(jnp.sum(norms)), 1.0)
    start = lax.axis_index(("dp", "blk")) * par.shape[0]
    unit = start + lax.broadcasted_iota(jnp.int32, par.shape, 0)
    plain = jnp.zeros(par.shape, jnp.bool_)
    for lo, hi in PLAIN_UNITS:
        plain = plain | ((unit >= lo) & (unit < hi))
    scaled = clip * grad
    first = 0.9 * units(m) + 0.1 * scaled
    second = 0.999 * units(v) + 0.001 * scaled * scaled
    direction = first / (1.0 - 0.9**10) / (jnp.sqrt(second / (1.0 - 0.999**10)) + 1e-08)
    step = -0.001 * 0.9**12 * (direction + jnp.where(plain, 0.0, 0.05 * par))
    return act[None], ing[None], norms, step.reshape(-1), first.reshape(-1), nb[16:24].reshape(-1)


def solution(mesh):
    act, flat = P("dp", "blk", None), P(("dp", "blk"))
    specs = dict(
        in_specs=(act, act, P("dp", None), flat, flat, flat), out_specs=(act, act, P(), flat, flat, P()), check_vma=False
    )

    def layer(patches, cotangent, image_lengths, params, first_moment, second_moment):
        fits = (dict(mesh.shape), patches.shape, params.shape) == (dict(dp=8, blk=4), (8, 1024, D), (RAW,))
        step = jax.shard_map(fast_shards if fits else shards, mesh=mesh, **specs)
        return step(patches, cotangent, image_lengths, params, first_moment, second_moment)

    return layer
```

```python
from functools import partial
import math

import jax
import jax.numpy as jnp
from jax import lax
from jax.experimental import pallas as pl
from jax.experimental.pallas import tpu as pltpu
from jax.sharding import PartitionSpec as P

D = 1024
FF = 4096
HEADS = 16
HEAD_DIM = 64
GROUPS = 12
RAW = 12595200


eps_norm = 1e-06
neg_big = -1e30


def starts_of(model_width, hidden):
    square = model_width * model_width
    mlp_start = 7 * model_width + 4 * square
    return [
        0,
        model_width,
        2 * model_width,
        2 * model_width + 3 * square,
        4 * model_width + 3 * square,
        4 * model_width + 4 * square,
        5 * model_width + 4 * square,
        6 * model_width + 4 * square,
        mlp_start,
        mlp_start + model_width * hidden,
        mlp_start + model_width * hidden + hidden,
        mlp_start + 2 * model_width * hidden + hidden,
        mlp_start + 2 * model_width * hidden + hidden + model_width,
    ]


def unpack(flat_params):
    marks = starts_of(D, FF)
    pieces = [flat_params[marks[member] : marks[member + 1]] for member in range(12)]
    return (
        pieces[0],
        pieces[1],
        pieces[2].reshape(D, 3 * D),
        pieces[3],
        pieces[4].reshape(D, D),
        pieces[5],
        pieces[6],
        pieces[7],
        pieces[8].reshape(D, FF),
        pieces[9],
        pieces[10].reshape(FF, D),
        pieces[11],
    )


def layer_norm(values, gains, offsets):
    average = jnp.mean(values, axis=-1, keepdims=True)
    centred = values - average
    spread = jnp.mean(centred * centred, axis=-1, keepdims=True)
    return centred * lax.rsqrt(spread + eps_norm) * gains + offsets


def segment_ids(lengths, row_ids):
    bounds = jnp.cumsum(lengths)
    return jnp.sum((row_ids[:, None] >= bounds[None, :]).astype(jnp.int32), axis=1)


def shards(patches, cotangent, image_lengths, params, first_moment, second_moment):
    local_rows = patches.shape[1]
    seq_len = local_rows * lax.axis_size("blk")
    scale_of = HEAD_DIM ** (-0.5)
    inputs = patches[0].astype(jnp.float32)
    lengths = image_lengths[0]
    query_ids = lax.axis_index("blk") * local_rows + jnp.arange(local_rows, dtype=jnp.int32)
    query_labels = segment_ids(lengths, query_ids)
    weights_low = lax.all_gather(params.astype(jnp.bfloat16), ("dp", "blk"), axis=0, tiled=True)
    (
        gain_one,
        shift_one,
        w_qkv,
        bias_qv,
        w_out,
        bias_out,
        gain_two,
        shift_two,
        w_up,
        bias_up,
        w_down,
        bias_down,
    ) = unpack(weights_low)
    normed_one, pull_one = jax.vjp(
        layer_norm, inputs, gain_one.astype(jnp.float32), shift_one.astype(jnp.float32)
    )
    normed_low = normed_one.astype(jnp.bfloat16)
    bias_all = jnp.concatenate(
        [
            bias_qv[:D].astype(jnp.float32),
            jnp.zeros((D,), jnp.float32),
            bias_qv[D:].astype(jnp.float32),
        ]
    )
    projected = (jnp.dot(normed_low, w_qkv, preferred_element_type=jnp.float32) + bias_all).astype(
        jnp.bfloat16
    )
    queries = projected[:, :D].reshape(local_rows, HEADS, HEAD_DIM)
    key_value = projected[:, D:]

    def attend_block(state, block, block_labels):
        allowed = query_labels[:, None] == block_labels[None, :]
        best_in, total_in, summed_in = state
        raw = jnp.einsum("qhd,khd->hqk", queries, block[:, 0], preferred_element_type=jnp.float32)
        scores = jnp.where(allowed[None], raw * scale_of, neg_big)
        new_best = jnp.maximum(best_in, jnp.max(scores, axis=-1))
        factor = jnp.exp(best_in - new_best)
        weights = jnp.where(allowed[None], jnp.exp(scores - new_best[..., None]), 0.0)
        new_total = total_in * factor + jnp.sum(weights, axis=-1)
        added = jnp.einsum(
            "hqk,khd->qhd",
            weights.astype(jnp.bfloat16),
            block[:, 1],
            preferred_element_type=jnp.float32,
        )
        return (new_best, new_total, summed_in * factor.T[..., None] + added)

    start_state = (
        jnp.full((HEADS, local_rows), neg_big, jnp.float32),
        jnp.zeros((HEADS, local_rows), jnp.float32),
        jnp.zeros((local_rows, HEADS, HEAD_DIM), jnp.float32),
    )
    carry = start_state
    piece = lax.all_gather(key_value, "blk", axis=0, tiled=True)
    count = piece.shape[0]
    size = math.gcd(count, 512)
    blocks = piece.reshape(count // size, size, 2, HEADS, HEAD_DIM)
    labels = segment_ids(lengths, jnp.arange(count, dtype=jnp.int32)).reshape(count // size, size)

    def one_block(state, members):
        return (attend_block(state, members[0], members[1]), None)

    carry, ignored = lax.scan(one_block, carry, (blocks, labels))
    best, total, summed = carry
    attended = summed / total.T[..., None]
    log_total = best + jnp.log(total)
    attended_low = attended.reshape(local_rows, D).astype(jnp.bfloat16)
    branch = jnp.dot(attended_low, w_out, preferred_element_type=jnp.float32) + bias_out.astype(
        jnp.float32
    )
    middle = inputs + branch
    normed_two, pull_two = jax.vjp(
        layer_norm, middle, gain_two.astype(jnp.float32), shift_two.astype(jnp.float32)
    )
    normed_two_low = normed_two.astype(jnp.bfloat16)
    hidden_pre = jnp.dot(normed_two_low, w_up, preferred_element_type=jnp.float32) + bias_up.astype(
        jnp.float32
    )
    activated, pull_gelu = jax.vjp(partial(jax.nn.gelu, approximate=False), hidden_pre)
    activated_low = activated.astype(jnp.bfloat16)
    result = middle + (
        jnp.dot(activated_low, w_down, preferred_element_type=jnp.float32)
        + bias_down.astype(jnp.float32)
    )
    grad_out = cotangent[0]
    grad_down = jnp.dot(activated_low.T, grad_out, preferred_element_type=jnp.float32)
    grad_bias_down = jnp.sum(grad_out.astype(jnp.float32), axis=0)
    grad_act = jnp.dot(grad_out, w_down.T, preferred_element_type=jnp.float32)
    grad_hidden_low = pull_gelu(grad_act)[0].astype(jnp.bfloat16)
    grad_up = jnp.dot(normed_two_low.T, grad_hidden_low, preferred_element_type=jnp.float32)
    grad_bias_up = jnp.sum(grad_hidden_low.astype(jnp.float32), axis=0)
    grad_normed_two = jnp.dot(grad_hidden_low, w_up.T, preferred_element_type=jnp.float32)
    grad_mid_norm, grad_gain_two, grad_shift_two = pull_two(grad_normed_two)
    grad_middle = grad_out.astype(jnp.float32) + grad_mid_norm
    grad_middle_low = grad_middle.astype(jnp.bfloat16)
    grad_w_out = jnp.dot(attended_low.T, grad_middle_low, preferred_element_type=jnp.float32)
    grad_bias_out = jnp.sum(grad_middle_low.astype(jnp.float32), axis=0)
    grad_attended = (
        jnp.dot(grad_middle_low, w_out.T, preferred_element_type=jnp.float32)
        .astype(jnp.bfloat16)
        .reshape(local_rows, HEADS, HEAD_DIM)
    )
    delta_rows = jnp.sum(grad_attended.astype(jnp.float32) * attended, axis=-1).T
    gathered = lax.all_gather(key_value, "blk", axis=0, tiled=True)
    size = math.gcd(seq_len, 512)
    key_blocks = gathered.reshape(seq_len // size, size, 2, HEADS, HEAD_DIM)
    key_labels = segment_ids(lengths, jnp.arange(seq_len, dtype=jnp.int32)).reshape(
        seq_len // size, size
    )

    def back_block(grad_query, members):
        block, block_labels = members
        allowed = query_labels[:, None] == block_labels[None, :]
        raw = jnp.einsum("qhd,khd->hqk", queries, block[:, 0], preferred_element_type=jnp.float32)
        scores = jnp.where(allowed[None], raw * scale_of, neg_big)
        probs = jnp.where(allowed[None], jnp.exp(scores - log_total[..., None]), 0.0)
        grad_probs = jnp.einsum(
            "qhd,khd->hqk", grad_attended, block[:, 1], preferred_element_type=jnp.float32
        )
        grad_raw = (probs * (grad_probs - delta_rows[..., None]) * scale_of).astype(jnp.bfloat16)
        new_grad = grad_query + jnp.einsum(
            "hqk,khd->qhd", grad_raw, block[:, 0], preferred_element_type=jnp.float32
        )
        grad_keys = jnp.einsum(
            "hqk,qhd->khd", grad_raw, queries, preferred_element_type=jnp.float32
        )
        grad_values = jnp.einsum(
            "hqk,qhd->khd",
            probs.astype(jnp.bfloat16),
            grad_attended,
            preferred_element_type=jnp.float32,
        )
        return (new_grad, jnp.stack([grad_keys, grad_values], axis=1))

    grad_query, grad_kv_blocks = lax.scan(
        back_block, jnp.zeros((local_rows, HEADS, HEAD_DIM), jnp.float32), (key_blocks, key_labels)
    )
    grad_kv = lax.psum_scatter(
        grad_kv_blocks.reshape(seq_len, 2 * D).astype(jnp.bfloat16),
        "blk",
        scatter_dimension=0,
        tiled=True,
    ).astype(jnp.float32)
    grad_projected = jnp.concatenate([grad_query.reshape(local_rows, D), grad_kv], axis=1).astype(
        jnp.bfloat16
    )
    grad_w_qkv = jnp.dot(normed_low.T, grad_projected, preferred_element_type=jnp.float32)
    grad_proj_rows = jnp.sum(grad_projected.astype(jnp.float32), axis=0)
    grad_bias_qv = jnp.concatenate([grad_proj_rows[:D], grad_proj_rows[2 * D :]])
    grad_normed_one = jnp.dot(grad_projected, w_qkv.T, preferred_element_type=jnp.float32)
    grad_in_norm, grad_gain_one, grad_shift_one = pull_one(grad_normed_one)
    grad_inputs = grad_middle + grad_in_norm
    shard_len = params.shape[0]
    total_params = shard_len * lax.axis_size(("dp", "blk"))
    flat_grad = jnp.concatenate(
        [
            grad_gain_one,
            grad_shift_one,
            grad_w_qkv.reshape(-1),
            grad_bias_qv,
            grad_w_out.reshape(-1),
            grad_bias_out,
            grad_gain_two,
            grad_shift_two,
            grad_up.reshape(-1),
            grad_bias_up,
            grad_down.reshape(-1),
            grad_bias_down,
            jnp.zeros((total_params - RAW,), jnp.float32),
        ]
    )
    shard_grad = lax.psum_scatter(
        lax.slice_in_dim(flat_grad, 0, lax.axis_size(("dp", "blk")) * shard_len, axis=0),
        ("dp", "blk"),
        scatter_dimension=0,
        tiled=True,
    )
    positions = lax.axis_index(("dp", "blk")) * shard_len + jnp.arange(shard_len, dtype=jnp.int32)
    marks = jnp.array(starts_of(D, FF), dtype=jnp.int32)
    group_of = jnp.sum((positions[:, None] >= marks[None, :]).astype(jnp.int32), axis=1) - 1
    squares = shard_grad * shard_grad
    partials = jnp.sum(
        jnp.where(
            group_of[None, :] == jnp.arange(GROUPS, dtype=jnp.int32)[:, None], squares[None, :], 0.0
        ),
        axis=1,
    )
    norms, bias_total = lax.psum((partials, grad_bias_down), ("dp", "blk"))
    clip_factor = 1.0 / jnp.maximum(jnp.sqrt(jnp.sum(norms)), 1.0)
    decayed = ((group_of == 2) | (group_of == 4) | (group_of == 8) | (group_of == 10)).astype(
        jnp.float32
    )
    scaled = clip_factor * shard_grad
    new_first = 0.9 * first_moment + 0.1 * scaled
    new_second = 0.999 * second_moment + 0.001 * scaled * scaled
    direction = new_first / (1.0 - 0.9**10) / (jnp.sqrt(new_second / (1.0 - 0.999**10)) + 1e-08)
    param_step = -0.001 * 0.9**12 * (direction + 0.05 * decayed * params)
    return (
        result.astype(jnp.bfloat16)[None],
        grad_inputs.astype(jnp.bfloat16)[None],
        norms,
        param_step,
        new_first,
        bias_total,
    )


MESH = pl.DeviceIdType.MESH
LANE = 128


def pick(cond, yes, no):
    return jnp.where(cond, jnp.int32(yes), jnp.int32(no))


def rdma(src, dst, ssem, rsem, dev):
    return pltpu.make_async_remote_copy(src_ref=src, dst_ref=dst, send_sem=ssem, recv_sem=rsem, device_id=dev, device_id_type=MESH)


def rows(ref, start, size, step=128):
    return ref.at[pl.ds(pl.multiple_of(start, step), size)]


def gate(peers):
    sem = pltpu.get_barrier_semaphore()
    for peer in peers:
        pl.semaphore_signal(sem, inc=1, device_id=peer, device_id_type=MESH)
    pl.semaphore_wait(sem, len(peers))


class Place:
    def __init__(self):
        self.dp = lax.axis_index("dp")
        self.blk = lax.axis_index("blk")
        self.d = self.dp * 4 + self.blk
        self.z = self.dp // 2
        self.x = self.dp % 2
        self.y = self.blk // 2
        self.c = self.blk % 2
        self.xpeer = (self.z * 2 + 1 - self.x, self.blk)
        self.zs = [lax.rem(self.z + k, 4) for k in (1, 3, 2)]
        self.zpeers = [(zz * 2 + self.x, self.blk) for zz in self.zs]
        self.quad = [(self.dp, lax.rem(self.blk + k, 4)) for k in (1, 2, 3)]
        up = lax.rem(self.d + 1, 32)
        down = lax.rem(self.d + 31, 32)
        self.above = (self.dp + 2, self.blk)
        self.below = (self.dp - 2, self.blk)
        self.others = self.zpeers + [(zz * 2 + 1 - self.x, self.blk) for zz in self.zs]
        self.near = ((self.dp, self.y * 2 + 1 - self.c), (self.dp, (1 - self.y) * 2 + self.c))
        self.next = (up // 4, up % 4)
        self.prev = (down // 4, down % 4)
        d = self.d
        self.is_qkv = d < 8
        self.is_out = (d == 8) | (d == 9)
        self.is_mix_out = d == 10
        self.is_up = (d >= 11) & (d < 21)
        self.is_mix_down = d == 21
        self.is_down = d >= 22
        self.is_seg = self.is_out | self.is_down
        self.is_mix = self.is_mix_out | self.is_mix_down
        self.base = pick(d < 8, 16, pick(d < 11, 32, pick(d < 21, 56, 88))) - 3 * d
        self.seg0 = pick(d < 11, 3 * (d - 8), jnp.maximum(3 * (d - 21) - 1, 0))
        self.mix_up = pick(self.is_mix_out, 2074, -7)
        self.mix_seg = pick(self.is_mix_out, 2, 1049)

    def seg_home(self, n):
        seg = self.seg0 + n // 4
        panel = n % 4
        out_row = 3072 + 256 * panel + 128 * (seg % 2)
        down_row = 8192 + 1024 * panel + 128 * (seg // 4)
        low = self.d < 11
        return pick(low, seg // 2, seg % 4), pick(low, out_row, down_row)

    def block_home(self, n):
        part, row = self.seg_home(n)
        return pick(self.is_qkv, n % 4, part), pick(self.is_qkv, (n // 4) * 1024 + 128 * self.d, row)

    def up_home(self, n):
        start = pick(self.is_up, 32 + 96 * (self.d - 11), pick(self.is_mix_out, 0, 992))
        return n // 4, 4096 + 1024 * (n % 4) + start


def chunk_row(q, k):
    first = (k // 4) * 1024 + 512 * q + 128 * (k % 4)
    turn = 3 * (q - 2) + k // 4
    panel = k % 4
    other = pick(
        turn < 2,
        3072 + 256 * panel + 128 * turn,
        pick(turn < 10, 4096 + 1024 * panel + 128 * (turn - 2), 8192 + 1024 * panel + 128 * (turn - 10)),
    )
    return pick(q < 2, first, other)


def loop(count, body):
    def step(i, carry):
        body(i)
        return carry

    lax.fori_loop(0, count, step, 0)


def unit_span(start, stride):
    return pl.ds(start, 16, stride=stride)


def for_tiles(me, visit):
    e0 = 24 + me.base

    @pl.when(me.is_qkv)
    def _():
        def body(rb):
            for ct in range(24):
                n = (ct // 8) * 4 + (ct % 8) // 2
                visit(e0 + 384 * rb + ct, 24, n * 128 + 16 * rb, 128 * (ct % 2))

        loop(8, body)

    @pl.when(me.is_up)
    def _():
        def body(rb):
            for ct in range(32):
                n = (ct % 4) * 4 + ct // 8
                visit(e0 + 512 * rb + ct, 32, n * 96 + 16 * rb, 128 * ((ct // 4) % 2))

        loop(6, body)

    def segs(count, first):
        def body(i):
            for ct in range(8):
                visit(first + 128 * i + ct, 8, ((i // 8) * 4 + ct // 2) * 128 + 16 * (i % 8), 128 * (ct % 2))

        loop(count, body)

    @pl.when(me.is_seg)
    def _():
        segs(24, e0)

    @pl.when(me.is_mix)
    def _():
        segs(16, 24 + me.mix_seg)

        def body(rb):
            for ct in range(32):
                n = (ct % 4) * 4 + ct // 8
                visit(24 + me.mix_up + 512 * rb + ct, 32, 1024 + n * 32 + 16 * rb, 128 * ((ct // 4) % 2))

        loop(2, body)


def for_pieces(me, visit):
    @pl.when(me.is_qkv | me.is_seg)
    def _():
        def body(n):
            part, row = me.block_home(n)
            visit(n, n * 128, 128, part, row, 128)

        loop(12, body)

    @pl.when(me.is_up)
    def _():
        def body(n):
            part, row = me.up_home(n)
            visit(n, n * 96, 96, part, row, 32)

        loop(16, body)

    @pl.when(me.is_mix)
    def _():
        def body(n):
            part, row = me.seg_home(n)
            visit(n, n * 128, 128, part, row, 128)

        loop(8, body)

        def body_up(n):
            part, row = me.up_home(n)
            visit(8 + n, 1024 + n * 32, 32, part, row, 32)

        loop(16, body_up)


def vec_spots(me, visit):
    for cond, row, unit, count in (
        (me.d == 0, 0, 0, 16),
        (me.d == 7, 0, 3067, 8),
        (me.d == 8, 0, 0, 8),
        (me.d == 10, 8, 2050, 24),
        (me.d == 21, 0, 1017, 32),
        (me.d == 31, 0, 3067, 8),
    ):

        @pl.when(cond)
        def _(row=row, unit=unit, count=count):
            visit(row, 24 + unit, count)


BF, F32 = jnp.bfloat16, jnp.float32
EPS = 1e-06
OUT0, UP0, DOWN0 = 3072, 4096, 8192


def dot(a, b):
    return lax.dot_general(a, b, (((1,), (0,)), ((), ())), preferred_element_type=F32)


def dot_nt(a, b):
    return lax.dot_general(a, b, (((1,), (1,)), ((), ())), preferred_element_type=F32)


def dot_tn(a, b):
    return lax.dot_general(a, b, (((0,), (0,)), ((), ())), preferred_element_type=F32)


def block_of(i):
    return pl.ds(pl.multiple_of(i * 256, 256), 256)


def wide(r, q, first, count=8):
    return jnp.concatenate([r.XV[q, first + i : first + i + 1, :] for i in range(count)], axis=1)


def narrow(r, q, first):
    return jnp.concatenate([r.XV[q, pl.ds(first + i, 1), :] for i in range(2)], axis=1)


def put_vec(r, q, first, row, add=False):
    for i in range(row.shape[1] // 128):
        part = row[:, i * 128 : i * 128 + 128]
        if add:
            part = part + r.VG[q, first + i : first + i + 1, :]
        r.VG[q, first + i : first + i + 1, :] = part


def normalize(x):
    mean = jnp.mean(x, axis=-1, keepdims=True)
    cen = x - mean
    var = jnp.mean(cen * cen, axis=-1, keepdims=True)
    scale = lax.rsqrt(var + EPS)
    return cen * scale, scale


def norm_back(dy, xhat, scale, gain):
    t = dy * gain
    return scale * (t - jnp.mean(t, axis=-1, keepdims=True) - xhat * jnp.mean(t * xhat, axis=-1, keepdims=True))


def labels_at(r, at):
    total = jnp.zeros_like(at)
    bound = 0
    for k in range(9):
        bound = bound + r.lens[k]
        total = total + (at >= bound).astype(jnp.int32)
    return total


def lane_mask(h, value=1.0):
    lane = lax.broadcasted_iota(jnp.int32, (1, 128), 1)
    return jnp.where((lane // 64) == h, value, 0.0).astype(BF)


def crow(q, k):
    return pick(q < 2, 128 * k, 384 * (k % 4) + 128 * (k // 4))


class Other(Place):
    def __init__(self, me, i):
        d = me.dp * 4 + i
        self.d, self.blk, self.dp = d, i, me.dp
        self.is_qkv = d < 8
        self.is_out = (d == 8) | (d == 9)
        self.is_mix_out = d == 10
        self.is_up = (d >= 11) & (d < 21)
        self.is_mix_down = d == 21
        self.is_down = d >= 22
        self.is_seg = self.is_out | self.is_down
        self.is_mix = self.is_mix_out | self.is_mix_down
        self.seg0 = pick(d < 11, 3 * (d - 8), jnp.maximum(3 * (d - 21) - 1, 0))

    def seg_spot(self, n):
        seg = self.seg0 + n // 4
        low = self.d < 11
        turn = pick(low, seg % 2, 10 + seg // 4 - 3 * (self.dp - 2))
        return pick(low, seg // 2, seg % 4), 384 * (n % 4) + 128 * turn

    def block_spot(self, n):
        part, row = self.seg_spot(n)
        return pick(self.is_qkv, n % 4, part), pick(self.is_qkv, (n // 4) * 512 + 128 * (self.d % 4), row)

    def up_spot(self, n):
        start = pick(self.is_up, 32 + 96 * (self.d - 11), pick(self.is_mix_out, 0, 992))
        return n // 4, 384 * (n % 4) + 256 + start - 384 * (self.dp - 2)

    def pieces(self, visit):
        @pl.when(self.is_qkv | self.is_seg)
        def _():
            loop(12, lambda n: visit(n, n * 128, 128, *self.block_spot(n)))

        @pl.when(self.is_up)
        def _():
            loop(16, lambda n: visit(n, n * 96, 96, *self.up_spot(n)))

        @pl.when(self.is_mix)
        def _():
            loop(8, lambda n: visit(n, n * 128, 128, *self.seg_spot(n)))
            loop(16, lambda n: visit(8 + n, 1024 + n * 32, 32, *self.up_spot(n)))


def arrived(ref, sem):
    pltpu.make_async_copy(ref, ref, sem).wait()


def squares(x):
    s = jnp.sum(x * x, axis=0, keepdims=True)
    return s[:, :128] + s[:, 128:] if x.shape[1] == 256 else s


def by_z(me, values):
    out = jnp.int32(values[0])
    for n in (1, 2, 3):
        out = pick(me.z == n, values[n], out)
    return out


def span(zz, *groups):
    return tuple(zz * 6 + g for g in groups)


ALL = (0, 1, 2, 3, 4, 5)
REST = (24,)
GATHER_ORDER = (
    span(0, *ALL) + span(1, *ALL) + span(2, *ALL) + span(3, *ALL),
    span(1, 0, 1) + span(0, *ALL) + span(1, 2, 3, 4, 5) + span(2, *ALL) + span(3, *ALL),
    span(2, 0, 1, 2, 3) + span(0, *ALL) + span(1, 0, 1, 2, 3)
    + span(3, 0, 1) + span(2, 4, 5) + span(3, 2, 3, 4, 5) + span(1, 4, 5),
    span(3, *ALL) + span(0, *ALL) + span(1, 0, 1, 2, 3) + span(2, *ALL) + span(1, 4, 5),
)
def spots(*by_depth):
    most = max(len(groups) for groups in by_depth)
    return tuple(zip(*(groups + (24,) * (most - len(groups)) for groups in by_depth)))


NONE = ()
SUMS = dict(
    start=spots(span(3, 0, 1, 2, 3), NONE, NONE, span(2, 0)),
    middle0=spots(span(3, 4), span(3, 0), NONE, NONE),
    middle1=spots(span(3, 5), span(3, 1, 2), span(3, 0), span(2, 1)),
    middle2=spots(span(2, 0), span(3, 3), span(3, 1), span(2, 2)),
    middle3=spots(span(2, 1, 2), span(3, 4, 5), span(3, 2, 3), span(2, 3)),
    attended=spots(span(2, 3, 4), span(2, 0, 1), span(3, 4, 5), span(2, 4, 5)),
    rows0=spots(span(2, 5), span(2, 2, 3), NONE, NONE),
    rows1=spots(span(1, 0), span(2, 4), NONE, span(1, 0)),
    rows2=spots(span(1, 1), NONE, NONE, span(1, 1)),
    weights=spots(span(1, 2, 3), span(2, 5), span(1, 0, 1), span(1, 2, 3)),
    last=spots(span(1, 4, 5), NONE, span(1, 2, 3), span(1, 4, 5)),
    last0=spots(NONE, NONE, span(1, 4, 5), span(0, 0)),
    last1=spots(NONE, NONE, span(0, 0), span(0, 1)),
    last2=spots(NONE, NONE, span(0, 1), span(0, 2)),
    last3=spots(NONE, span(0, 0), span(0, 2), span(0, 3)),
    end=spots(NONE, span(0, 1, 2, 3, 4, 5), span(0, 3, 4, 5), span(0, 4, 5)),
)


def prepare(me, r):
    r.tail[...] = r.par[3051:3075, :]
    up = rdma(r.tail, r.hp, r.hsem.at[0], r.hsem.at[1], me.next)
    down = rdma(r.par.at[0:24], r.hn, r.hsem.at[2], r.hsem.at[3], me.prev)
    up.start()
    down.start()

    def put(i):
        r.E[pl.ds(pl.multiple_of(24 + 64 * i, 8), 64), :] = r.par[pl.ds(pl.multiple_of(64 * i, 8), 64), :]

    loop(48, put)
    r.E[3096:3099, :] = r.par[3072:3075, :]
    r.VS[...] = jnp.zeros_like(r.VS)

    def vec(row, unit, count):
        r.VS[row : row + count, :] = r.E[unit : unit + count, :].astype(BF).astype(F32)

    vec_spots(me, vec)
    vq = [rdma(r.VS, r.VQ.at[me.blk], r.vsem.at[0], r.vsem.at[1], peer) for peer in me.quad]
    for v in vq:
        v.start()
    r.VQ[me.blk] = r.VS[...]
    up.wait()
    down.wait()
    r.E[0:24, :] = r.hp[...]
    r.E[3099:3123, :] = r.hn[...]

    def tile(unit, stride, row, lane):
        r.S[pl.ds(pl.multiple_of(row, 16), 16), lane : lane + 128] = r.E[unit_span(unit, stride), :].astype(BF)

    for_tiles(me, tile)

    def which(i):
        return pick(me.is_qkv, jnp.minimum(i // 4, 2), 0)

    def visit(i, srow, size, part, frow, step):
        src, dst = rows(r.S, srow, size, 32), rows(r.F, frow, size, step)

        @pl.when(part != me.blk)
        def _():
            rdma(src, dst, r.qsem.at[i], r.csem.at[which(i)], (me.dp, part)).start()

        @pl.when(part == me.blk)
        def _():
            pltpu.make_async_copy(src, dst, r.csem.at[which(i)]).start()

    for_pieces(me, visit)
    arrived(r.VQ.at[0:3], r.vsem.at[0])
    arrived(r.VQ.at[0:3], r.vsem.at[1])
    r.XV[me.dp] = r.VQ[0] + r.VQ[1] + r.VQ[2] + r.VQ[3]
    for peer in me.others + [me.xpeer]:
        rdma(r.XV.at[me.dp], r.XV.at[me.dp], r.vxs, r.vxr.at[me.dp], peer).start()


def chunk_here(me, r, panel):
    @pl.when(me.is_qkv)
    def _():
        arrived(r.F.at[0:512], r.csem.at[panel])

    if panel == 0:

        @pl.when(jnp.logical_not(me.is_qkv))
        def _():
            arrived(r.F.at[0:1536], r.csem.at[0])


def prepare_drain(me, r):
    def visit(i, srow, size, part, frow, step):
        @pl.when(part != me.blk)
        def _():
            arrived(rows(r.S, srow, size, 32), r.qsem.at[i])

    for_pieces(me, visit)
    arrived(r.XV.at[0:7], r.vxs)


def own_down(me, r):
    @pl.when(me.z > 0)
    def _():
        def body(k):
            ref = rows(r.F, chunk_row(me.dp, k), 128)
            rdma(ref, ref, r.zsd.at[me.z], r.zr.at[me.z * 6 + k // 2], me.below).start()

        loop(12, body)


def gather_step(me, r, s):
    e = by_z(me, [order[s] for order in GATHER_ORDER])
    zz, g = e // 6, e % 6

    @pl.when(zz != me.z)
    def _():
        arrived(r.F.at[0:256], r.zr.at[e])

    def block(i):
        return rows(r.F, chunk_row(zz * 2 + me.x, g * 2 + i), 128)

    @pl.when((zz <= me.z) & (me.z < 3))
    def _():
        for i in range(2):
            rdma(block(i), block(i), r.zsu.at[zz], r.zr.at[e], me.above).start()

    @pl.when((zz > me.z) & (me.z > 0))
    def _():
        for i in range(2):
            rdma(block(i), block(i), r.zsd.at[zz], r.zr.at[e], me.below).start()

    for i in range(2):
        rdma(block(i), block(i), r.xs, r.xr.at[e], me.xpeer).start()


def gather_steps(me, r, *numbers):
    for s in numbers:
        gather_step(me, r, s)


def gathered(me, r, zz, groups=ALL):
    for g in groups:
        arrived(r.F.at[0:256], r.xr.at[zz * 6 + g])


def gather_drain(me, r):
    arrived(r.F.at[0:6144], r.xs)
    for zz in range(4):
        @pl.when((zz <= me.z) & (me.z < 3))
        def _():
            arrived(r.F.at[0:1536], r.zsu.at[zz])

        @pl.when((zz >= me.z) & (me.z > 0))
        def _():
            arrived(r.F.at[0:1536], r.zsd.at[zz])


def swap_send(me, r, src, dst, ssem, rsem):
    mine = block_of(me.blk)
    for n, peer in enumerate(me.near):
        rdma(src, dst.at[mine], ssem.at[n], rsem.at[n], peer).start()
    dst[mine, :] = src[...]


def swap_pass(me, r, dst, ssem, rsem):
    far = dst.at[block_of((1 - me.y) * 2 + me.c)]
    arrived(far, rsem.at[1])
    rdma(far, far, ssem.at[2], rsem.at[2], me.near[0]).start()


def swap_drain(me, r, dst, ssem):
    for n in range(3):
        arrived(dst.at[0:256], ssem.at[n])


def nothing(n):
    pass


class QuadSum:
    def __init__(self, me, r, term, make, sems, finish, slot, out=None):
        self.me, self.r, self.term, self.make, self.finish, self.slot, self.out = me, r, term, make, finish, slot, out
        self.ssem, self.rsem = sems
        y, c = me.y, me.c
        self.far_sib, self.far, self.near_sib, self.own = (1 - y) * 2 + 1 - c, (1 - y) * 2 + c, y * 2 + 1 - c, me.blk
        self.sib, self.yp = me.near
        self.over = []

    def copy(self, src, dst, n, dev):
        return rdma(src, dst, self.ssem.at[n], self.rsem.at[n], dev)

    def at(self, dev, i):
        return pl.ds(pl.multiple_of(dev * 256 + 64 * i, 64), 64)

    def send_far_sib(self):
        self.a = self.copy(self.term.at[block_of(self.far_sib)], self.r.RB.at[0], 0, self.sib)
        self.a.start()

    def send_near_sib(self):
        self.d = self.copy(self.term.at[block_of(self.near_sib)], self.r.RB.at[1], 1, self.sib)
        self.d.start()

    def cross(self):
        r = self.r
        self.a.wait_recv()
        for i in range(4):
            lo = pl.ds(64 * i, 64)
            r.RB[3, lo, :] = (self.term[self.at(self.far, i), :].astype(F32) + r.RB[0, lo, :].astype(F32)).astype(BF)
            self.over.append(self.copy(r.RB.at[3, lo], r.RB.at[self.slot, lo], 2 + i, self.yp))
            self.over[i].start()

    def begin(self):
        self.make(self.far_sib)
        self.send_far_sib()
        self.make(self.far)
        self.cross()
        self.make(self.near_sib)
        self.send_near_sib()
        self.make(self.own)

    def end(self, idle=nothing):
        r = self.r
        self.d.wait_recv()
        out, near, on = [], [], []
        for i in range(4):
            self.over[i].wait_recv()
            lo = slice(64 * i, 64 * i + 64)
            total = self.term[self.at(self.own, i), :].astype(F32) + r.RB[1, lo, :].astype(F32)
            self.finish(lo, total + r.RB[self.slot, lo, :].astype(F32))
            if self.out is not None:
                part, passed = self.out.at[self.at(self.own, i)], self.out.at[self.at(self.far, i)]
                out.append(self.copy(part, part, 6 + i, self.yp))
                near.append(self.copy(part, part, 10 + i, self.sib))
                on.append(self.copy(passed, passed, 14 + i, self.sib))
                out[i].start()
                near[i].start()
            idle(i)
        for i in range(len(out)):
            out[i].wait_recv()
            on[i].start()
        for cp in near + on:
            cp.wait()
        for cp in [self.a, self.d] + self.over + out:
            cp.wait_send()


def first_norm(me, r, half):
    gain, shift = wide(r, 0, 0), wide(r, 0, 8)

    def ln(i):
        at = pl.ds(pl.multiple_of(half * 512 + i * 64, 64), 64)
        xhat, _ = normalize(r.PA[at, :].astype(F32))
        r.PA[at, :] = (xhat * gain + shift).astype(BF)

    loop(8, ln)


def attention(me, r, idle):
    bias = [narrow(r, 1, 2 * me.blk), None, narrow(r, 2, 2 * me.blk)]

    def proj(i):
        at = block_of(i)
        for j in range(3):
            out = dot(r.PA[at, :], r.F[j * 1024 : j * 1024 + 1024, :])
            if bias[j] is not None:
                out = out + bias[j]
            r.QKV[j, at, :] = out.astype(BF)

    loop(4, proj)
    idle(0)
    key_labels = labels_at(r, lax.broadcasted_iota(jnp.int32, (1, 1024), 1))

    def attend(i):
        at = block_of(i)
        row_labels = labels_at(r, lax.broadcasted_iota(jnp.int32, (256, 1), 0) + i * 256)
        allowed = row_labels == key_labels
        for t in range(2):
            lanes = slice(128 * t, 128 * t + 128)
            q = r.QKV[0, at, lanes]
            k = r.QKV[1, :, lanes]
            v = r.QKV[2, :, lanes]
            out = jnp.zeros((256, 128), F32)
            inverse = []
            for h in range(2):
                s = jnp.where(allowed, dot_nt(q * lane_mask(h, 0.125), k), -1e30)
                w = jnp.exp(s - jnp.max(s, axis=-1, keepdims=True))
                inverse.append(1.0 / jnp.sum(w, axis=-1, keepdims=True))
                p = w.astype(BF)
                r.P[2 * t + h, at, :] = p
                out = out + dot(p, v * lane_mask(h))
            low_lanes = lax.broadcasted_iota(jnp.int32, (256, 128), 1) < 64
            scale = jnp.where(low_lanes, inverse[0], inverse[1])
            r.RL[at, lanes] = scale
            r.AT[at, lanes] = (out * scale).astype(BF)

    loop(2, attend)
    idle(1)
    loop(2, lambda i: attend(i + 2))


def second_norm(me, r):
    def term(i):
        at = block_of(i)
        for p in range(4):
            r.PB[at, 256 * p : 256 * p + 256] = dot(r.AT[at, :], r.F[OUT0 + 256 * p : OUT0 + 256 * p + 256, :]).astype(BF)

    bias_out = wide(r, 2, 8)
    gain, shift = wide(r, 2, 16), wide(r, 2, 24)

    def finish(lo, total):
        x = r.pat[lo, :].astype(F32) + (total + bias_out)
        r.MID[lo, :] = x
        xhat, _ = normalize(x)
        r.NT[pl.ds(pl.multiple_of(me.blk * 256 + lo.start, 64), 64), :] = (xhat * gain + shift).astype(BF)

    return QuadSum(me, r, r.PB, term, (r.s1s, r.s1r), finish, 2, r.NT)


def hidden(me, r):
    biases = [jnp.concatenate([r.XV[5, pl.ds(4 * (2 * p + i) + me.blk, 1), :] for i in range(2)], axis=1) for p in range(4)]

    def up(i):
        at = pl.ds(pl.multiple_of(i * 128, 128), 128)
        for p in range(4):
            h = dot(r.NT[at, :], r.F[UP0 + 1024 * p : UP0 + 1024 * p + 1024, :]) + biases[p]
            phi = 0.5 + 0.5 * lax.erf(h * 0.7071067811865476)
            lanes = slice(256 * p, 256 * p + 256)
            r.AC[at, lanes] = (h * phi).astype(BF)
            r.GP[at, lanes] = (phi + h * (jnp.exp(-0.5 * h * h) * 0.3989422804014327)).astype(BF)

    loop(8, up)


def hidden_grad(me, r):
    def body(i):
        at = block_of(i)
        for p in range(4):
            lanes = slice(256 * p, 256 * p + 256)
            acc = jnp.zeros((256, 256), F32)
            for k in range(4):
                down = r.F[DOWN0 + 1024 * k + 256 * p : DOWN0 + 1024 * k + 256 * p + 256, :]
                acc = acc + dot_nt(r.CA[at, 256 * k : 256 * k + 256], down)
            r.GH[at, lanes] = (acc * r.GP[at, lanes].astype(F32)).astype(BF)

    loop(4, body)


def hidden_sums(me, r):
    for p in range(4):
        sums = jnp.sum(r.GH[:, 256 * p : 256 * p + 256].astype(F32), axis=0, keepdims=True)
        for i in range(2):
            r.VG[5, pl.ds(4 * (2 * p + i) + me.blk, 1), :] = sums[:, 128 * i : 128 * i + 128]
    put_vec(r, 7, 0, jnp.sum(r.cot[...].astype(F32), axis=0, keepdims=True))


def weight_grad(r, left, right, base, height):
    def body(i):
        cols = pl.ds(pl.multiple_of(i * 256, 256), 256)
        lt = left[:, cols].T
        for p in range(right.shape[1] // 256):
            out = dot(lt, right[:, 256 * p : 256 * p + 256])
            r.G[pl.ds(pl.multiple_of(base + p * height + i * 256, 256), 256), :] = out.astype(BF)

    loop(height // 256, body)


def middle_grad(me, r, sums):
    def term(i):
        at = block_of(i)
        for n in range(4):
            acc = jnp.zeros((256, 256), F32)
            for p in range(4):
                up = r.F[UP0 + 1024 * p + 256 * n : UP0 + 1024 * p + 256 * n + 256, :]
                acc = acc + dot_nt(r.GH[at, 256 * p : 256 * p + 256], up)
            r.PB[at, 256 * n : 256 * n + 256] = acc.astype(BF)

    gain = wide(r, 2, 16)
    sums[:] = [jnp.zeros((1, 1024), F32)] * 3

    def finish(lo, dy):
        xhat, scale = normalize(r.MID[lo, :])
        gm = r.cot[lo, :].astype(F32) + norm_back(dy, xhat, scale, gain)
        r.GMID[lo, :] = gm
        low = gm.astype(BF)
        r.GM[pl.ds(pl.multiple_of(me.blk * 256 + lo.start, 64), 64), :] = low
        for n, term_of in enumerate((low.astype(F32), dy * xhat, dy)):
            sums[n] = sums[n] + jnp.sum(term_of, axis=0, keepdims=True)

    return QuadSum(me, r, r.PB, term, (r.s2s, r.s2r), finish, 4, r.GM)


def attended_grad(me, r):
    def body(i):
        at = block_of(i)
        acc = jnp.zeros((256, 256), F32)
        for p in range(4):
            acc = acc + dot_nt(r.GM[at, 256 * p : 256 * p + 256], r.F[OUT0 + 256 * p : OUT0 + 256 * p + 256, :])
        r.GP[at, 768:1024] = acc.astype(BF)

    loop(4, body)


def attention_grad(me, r, idle):
    r.E[...] = jnp.zeros_like(r.E)

    def attend(i):
        at = block_of(i)
        for t in range(2):
            lanes = slice(128 * t, 128 * t + 128)
            q = r.QKV[0, at, lanes]
            k = r.QKV[1, :, lanes]
            v = r.QKV[2, :, lanes]
            da = (r.GP[at, 768 + 128 * t : 896 + 128 * t].astype(F32) * r.RL[at, lanes]).astype(BF)
            overlap = da.astype(F32) * r.AT[at, lanes].astype(F32)
            dq = jnp.zeros((256, 128), F32)
            for h in range(2):
                m, m8 = lane_mask(h), lane_mask(h, 0.125)
                p = r.P[2 * t + h, at, :]
                delta = jnp.sum(overlap * m.astype(F32), axis=-1, keepdims=True)
                ds = (p.astype(F32) * (dot_nt(da * m, v) - delta)).astype(BF)
                dq = dq + dot(ds, k * m8)
                r.E[1024 * t : 1024 * t + 1024, :] += dot_tn(ds, q * m8)
                r.E[2048 + 1024 * t : 3072 + 1024 * t, :] += dot_tn(p, da * m)
            r.GP[at, lanes] = dq.astype(BF)

    for i in range(4):
        attend(i)
        if i < 3:
            idle(i)
    for n in range(4):
        r.GP[:, 256 + 128 * n : 384 + 128 * n] = r.E[1024 * n : 1024 * n + 1024, :].astype(BF)


def projection_sums(me, r):
    for j, q in ((0, 1), (2, 2)):
        sums = jnp.sum(r.GP[:, 256 * j : 256 * j + 256].astype(F32), axis=0, keepdims=True)
        for i in range(2):
            r.VG[q, pl.ds(2 * me.blk + i, 1), :] = sums[:, 128 * i : 128 * i + 128]


def projection_grad(me, r):
    def body(i):
        cols = pl.ds(pl.multiple_of(i * 256, 256), 256)
        lt = r.PA[:, cols].T
        for j in range(3):
            r.G[pl.ds(pl.multiple_of(j * 1024 + i * 256, 256), 256), :] = dot(lt, r.GP[:, 256 * j : 256 * j + 256]).astype(BF)

    loop(4, body)


def input_grad(me, r, sums):
    def term(i):
        at = block_of(i)
        for n in range(4):
            acc = jnp.zeros((256, 256), F32)
            for j in range(3):
                acc = acc + dot_nt(r.GP[at, 256 * j : 256 * j + 256], r.F[1024 * j + 256 * n : 1024 * j + 256 * n + 256, :])
            r.PB[at, 256 * n : 256 * n + 256] = acc.astype(BF)

    gain = wide(r, 0, 0)
    sums[:] = [jnp.zeros((1, 1024), F32)] * 2

    def finish(lo, dy):
        xhat, scale = normalize(r.pat[lo, :].astype(F32))
        r.ing[lo, :] = (r.GMID[lo, :] + norm_back(dy, xhat, scale, gain)).astype(BF)
        for n, term_of in enumerate((dy * xhat, dy)):
            sums[n] = sums[n] + jnp.sum(term_of, axis=0, keepdims=True)

    return QuadSum(me, r, r.PB, term, (r.s4s, r.s4r), finish, 4)


def layer_out(me, r):
    def term(i):
        at = block_of(i)
        for p in range(4):
            r.CA[at, 256 * p : 256 * p + 256] = dot(r.AC[at, :], r.F[DOWN0 + 1024 * p : DOWN0 + 1024 * p + 1024, :]).astype(BF)

    bias_down = wide(r, 7, 0)

    def finish(lo, total):
        r.act[lo, :] = (r.MID[lo, :] + (total + bias_down)).astype(BF)

    return QuadSum(me, r, r.CA, term, (r.s3s, r.s3r), finish, 2)


def reduce_send(me, r, zz, first=0, count=12):
    q = zz * 2 + 1 - me.x

    def body(i):
        k = first + i
        rdma(rows(r.G, chunk_row(q, k), 128), rows(r.XR.at[zz], crow(q, k), 128), r.rxs, r.rxr.at[zz * 6 + k // 2], me.xpeer).start()

    loop(count, body)


def reduce_step(me, r, groups):
    e = by_z(me, groups)

    @pl.when(e < 24)
    def _():
        zz, g = e // 6, e % 6
        q = zz * 2 + me.x
        down = zz < me.z
        arrived(r.G.at[0:256], r.rxr.at[e])

        @pl.when((me.z > 0) & (me.z < 3))
        def _():
            arrived(r.G.at[0:256], r.rzr.at[e])

        def body(i):
            k = g * 2 + i
            src, at = pl.ds(pl.multiple_of(chunk_row(q, k), 128), 128), pl.ds(pl.multiple_of(crow(q, k), 128), 128)
            total = r.G[src, :].astype(F32) + r.XR[zz, at, :].astype(F32) + r.ZR[zz, at, :].astype(F32)
            r.XR[zz, at, :] = total.astype(BF)
            sent = rows(r.XR.at[zz], crow(q, k), 128)

            @pl.when(down)
            def _():
                rdma(sent, rows(r.ZR.at[zz], crow(q, k), 128), r.rzs.at[zz], r.rzr.at[e], me.below).start()

            @pl.when(jnp.logical_not(down))
            def _():
                last = zz == me.z + 1
                slot, sem = pick(last, 4, zz), pick(last, 24 + g, e)
                rdma(sent, rows(r.ZR.at[slot], crow(q, k), 128), r.rzs.at[zz], r.rzr.at[sem], me.above).start()

        loop(2, body)


def sums_at(me, r, place):
    for groups in SUMS[place]:
        reduce_step(me, r, groups)


def reduce_last(me, r):
    first_tensor = pick(me.dp < 2, 2, pick(me.dp == 2, 4, pick(me.dp < 6, 8, 10)))

    def group(g):
        e = me.z * 6 + g
        arrived(r.G.at[0:256], r.rxr.at[e])

        @pl.when(me.z < 3)
        def _():
            arrived(r.G.at[0:256], r.rzr.at[e])

        @pl.when(me.z > 0)
        def _():
            arrived(r.G.at[0:256], r.rzr.at[24 + g])

        part = jnp.zeros((1, 128), F32)
        for i in range(2):
            k = g * 2 + i
            src, at = pl.ds(pl.multiple_of(chunk_row(me.dp, k), 128), 128), pl.ds(pl.multiple_of(crow(me.dp, k), 128), 128)
            total = r.G[src, :].astype(F32) + r.XR[me.z, at, :].astype(F32)
            total = total + (r.ZR[me.z, at, :].astype(F32) + r.ZR[4, at, :].astype(F32))
            part = part + squares(total)
            r.XR[me.z, at, :] = total.astype(BF)
        tensor = pick((g >= 4) & (me.dp == 2), 8, pick((g >= 2) & (me.dp == 5), 10, first_tensor))
        r.NB[0, pl.ds(tensor, 1), :] += part

    def pair(j):
        group(2 * j)
        group(2 * j + 1)

        @pl.when(me.is_qkv)
        def _():
            for i in range(4):
                src = rows(r.XR.at[me.z], j * 512 + 128 * i, 128)
                dst = rows(r.S, (j * 4 + me.blk) * 128, 128)

                @pl.when(me.blk != i)
                def _():
                    rdma(src, dst, r.qsem2.at[i * 24 + j * 4 + me.blk], r.csem2, (me.dp, i)).start()

                @pl.when(me.blk == i)
                def _():
                    pltpu.make_async_copy(src, dst, r.csem2).start()

    loop(3, pair)

    @pl.when(jnp.logical_not(me.is_qkv))
    def _():
        for i in range(4):
            def visit(n, srow, size, part, row, i=i):
                src, dst = rows(r.XR.at[me.z], row, size, 32), rows(r.S, srow, size, 32)

                @pl.when((part == me.blk) & (me.blk != i))
                def _():
                    rdma(src, dst, r.qsem2.at[i * 24 + n], r.csem2, (me.dp, i)).start()

                @pl.when((part == me.blk) & (me.blk == i))
                def _():
                    pltpu.make_async_copy(src, dst, r.csem2).start()

            Other(me, i).pieces(visit)


def column(me):
    return [(lax.rem(me.dp + k, 8), me.blk) for k in range(1, 8)]


def vectors_send(me, r):
    for q, blk in column(me):
        rdma(r.VG.at[q], r.VX.at[me.dp], r.wxs, r.wxr.at[me.dp], (q, blk)).start()
    r.VX[me.dp] = r.VG[me.dp]


def vectors_sum(me, r):
    for q, _ in column(me):
        arrived(r.VX.at[0], r.wxr.at[q])
    total = r.VX[0]
    for q in range(1, 8):
        total = total + r.VX[q]
    r.VT[me.blk] = total
    for peer in me.quad:
        rdma(r.VT.at[me.blk], r.VT.at[me.blk], r.wqs, r.wqr.at[me.blk], peer).start()


def vectors_end(me, r):
    for k in (1, 2, 3):
        arrived(r.VT.at[0], r.wqr.at[lax.rem(me.blk + k, 4)])
    r.VS[...] = r.VT[0] + r.VT[1] + r.VT[2] + r.VT[3]
    vector_squares(me, r)


def norms_send(me, r):
    for peer in column(me):
        rdma(r.NB.at[0], r.NR.at[me.dp], r.nsem, r.nrsem.at[me.dp], peer).start()
    r.NR[me.dp] = r.NB[0]


def norms_sum(me, r):
    for q, _ in column(me):
        arrived(r.NR.at[0], r.nrsem.at[q])
    total = r.NR[0]
    for q in range(1, 8):
        total = total + r.NR[q]
    r.NQ[me.blk] = total
    for peer in me.quad:
        rdma(r.NQ.at[me.blk], r.NQ.at[me.blk], r.nqs, r.nqr.at[me.blk], peer).start()


def norms_end(me, r):
    for k in (1, 2, 3):
        arrived(r.NQ.at[0], r.nqr.at[lax.rem(me.blk + k, 4)])
    r.norms[...] = r.NQ[0] + r.NQ[1] + r.NQ[2] + r.NQ[3]
    arrived(r.NR.at[0:7], r.nsem)
    arrived(r.NQ.at[0:3], r.nqs)


def vector_squares(me, r):
    for q, tensors in ((0, (0, 1, None, None)), (1, (3, None, None, None)), (2, (3, 5, 6, 7)), (5, (9, 9, 9, 9)), (7, (11, None, None, None))):
        @pl.when((me.dp == q) & (me.blk == 0))
        def _(q=q, tensors=tensors):
            for g, tensor in enumerate(tensors):
                if tensor is not None:
                    r.NB[0, tensor : tensor + 1, :] += squares(r.VS[8 * g : 8 * g + 8, :])
            if q == 7:
                r.NB[0, 16:24, :] = r.VS[0:8, :]


def reduce_drain(me, r):
    arrived(r.G.at[0:6144], r.rxs)
    arrived(r.VX.at[0:3], r.wqs)
    arrived(r.VX.at[0:7], r.wxs)
    for i in range(4):
        @pl.when(me.z != i)
        def _(i=i):
            arrived(r.G.at[0:1536], r.rzs.at[i])

        def visit(n, srow, size, part, row, i=i):
            @pl.when((part == me.blk) & (me.blk != i))
            def _():
                arrived(rows(r.XR.at[me.z], row, size, 32), r.qsem2.at[i * 24 + n])

        Other(me, i).pieces(visit)


def units_send(me, r):
    arrived(r.S, r.csem2)
    for lo, hi in ((0, 48), (3072, 3128)):
        r.E[lo:hi, :] = jnp.zeros((hi - lo, 128), F32)

    def tile(unit, stride, row, lane):
        r.E[unit_span(unit, stride), :] = r.S[pl.ds(pl.multiple_of(row, 16), 16), lane : lane + 128].astype(F32)

    for_tiles(me, tile)

    def vec(row, unit, count):
        r.E[unit : unit + count, :] = r.VS[row : row + count, :]

    vec_spots(me, vec)
    r.tail[...] = r.E[3099:3123, :]
    rdma(r.tail, r.hp2, r.hsem2.at[0], r.hsem2.at[1], me.next).start()
    rdma(r.E.at[0:24], r.hn2, r.hsem2.at[2], r.hsem2.at[3], me.prev).start()


def units_end(me, r):
    def put(i):
        r.grad[pl.ds(pl.multiple_of(64 * i, 8), 64), :] = r.E[pl.ds(pl.multiple_of(24 + 64 * i, 8), 64), :]

    loop(48, put)
    r.grad[3072:3075, :] = r.E[3096:3099, :]
    for n in range(4):
        arrived(r.tail, r.hsem2.at[n])
    r.grad[0:24, :] += r.hp2[...]
    r.grad[3051:3075, :] += r.hn2[...]


def whole_layer(me, r):
    r.VG[...] = jnp.zeros_like(r.VG)
    r.NB[0] = jnp.zeros((24, 128), F32)

    def clear(slot):
        r.ZR[slot] = jnp.zeros((1536, 256), BF)

    @pl.when(me.z == 0)
    def _():
        loop(4, lambda i: clear(i + 1))

    @pl.when(me.z == 3)
    def _():
        loop(4, clear)

    gate(me.quad + me.others + [me.xpeer, me.next, me.prev])
    prepare(me, r)
    chunk_here(me, r, 0)
    own_down(me, r)
    gather_steps(me, r, 0, 1)
    chunk_here(me, r, 1)
    gather_steps(me, r, 2, 3)
    chunk_here(me, r, 2)
    swap_send(me, r, r.pat, r.PA, r.pas, r.par_in)
    gather_steps(me, r, 4, 5, 6)
    swap_pass(me, r, r.PA, r.pas, r.par_in)
    for peer in range(1, 8):
        arrived(r.XV.at[0], r.vxr.at[lax.rem(me.dp + peer, 8)])
    gather_steps(me, r, 7)
    arrived(r.PA.at[0:256], r.par_in.at[0])
    first_norm(me, r, me.y)
    gather_steps(me, r, 8, 9)
    arrived(r.PA.at[0:256], r.par_in.at[2])
    swap_drain(me, r, r.PA, r.pas)
    first_norm(me, r, 1 - me.y)
    gather_steps(me, r, 10, 11)
    swap_send(me, r, r.cot, r.CA, r.cas, r.car)
    prepare_drain(me, r)
    gathered(me, r, 0)
    attention(me, r, lambda n: gather_steps(me, r, 12 + 2 * n, 13 + 2 * n))
    swap_pass(me, r, r.CA, r.cas, r.car)
    gather_steps(me, r, 16, 17, 18, 19)
    gathered(me, r, 1, (0, 1, 2, 3))
    second = second_norm(me, r)
    second.begin()
    gather_steps(me, r, 20, 21)
    second.end(lambda n: gather_steps(me, r, 22 + n) if n < 2 else None)
    gathered(me, r, 1, (4, 5))
    gathered(me, r, 2)
    hidden(me, r)
    gathered(me, r, 3)
    gather_drain(me, r)
    arrived(r.CA.at[0:256], r.car.at[0])
    arrived(r.CA.at[0:256], r.car.at[2])
    swap_drain(me, r, r.CA, r.cas)
    hidden_grad(me, r)
    weight_grad(r, r.AC, r.CA, DOWN0, 1024)
    reduce_send(me, r, 3, 0, 6)

    @pl.when(me.z < 3)
    def _():
        reduce_send(me, r, 3, 6, 6)

    middle_sums, input_sums = [], []
    middle = middle_grad(me, r, middle_sums)
    middle.begin()
    weight_grad(r, r.NT, r.GH, UP0, 1024)
    reduce_send(me, r, 2)

    @pl.when(me.z == 3)
    def _():
        reduce_send(me, r, 3, 6, 6)

    result = layer_out(me, r)
    loop(4, result.make)
    sums_at(me, r, "start")
    middle.end(lambda n: sums_at(me, r, "middle%d" % n))
    for n in range(3):
        put_vec(r, 2, 8 + 8 * n, middle_sums[n])
    result.send_far_sib()
    weight_grad(r, r.AT, r.GM, OUT0, 256)
    reduce_send(me, r, 1)
    attended_grad(me, r)
    result.cross()
    result.send_near_sib()
    sums_at(me, r, "attended")
    attention_grad(me, r, lambda n: sums_at(me, r, "rows%d" % n))
    projection_grad(me, r)
    reduce_send(me, r, 0)
    last = input_grad(me, r, input_sums)
    sums_at(me, r, "weights")
    result.end()
    last.begin()
    sums_at(me, r, "last")
    hidden_sums(me, r)
    projection_sums(me, r)
    last.end(lambda n: sums_at(me, r, "last%d" % n))
    for n in range(2):
        put_vec(r, 0, 8 * n, input_sums[n])
    vectors_send(me, r)
    sums_at(me, r, "end")
    vectors_sum(me, r)
    reduce_last(me, r)
    vectors_end(me, r)
    norms_send(me, r)
    units_send(me, r)
    norms_sum(me, r)
    units_end(me, r)
    norms_end(me, r)
    reduce_drain(me, r)


DMA = pltpu.SemaphoreType.DMA
VMEM = pltpu.VMEM
SCRATCH = dict(
    F=VMEM((12288, 256), BF),
    G=VMEM((12288, 256), BF),
    XV=VMEM((8, 32, 128), F32),
    PA=VMEM((1024, 1024), BF),
    CA=VMEM((1024, 1024), BF),
    E=VMEM((4096, 128), F32),
    S=VMEM((1536, 256), BF),
    VS=VMEM((32, 128), F32),
    VQ=VMEM((4, 32, 128), F32),
    VG=VMEM((8, 32, 128), F32),
    VX=VMEM((8, 32, 128), F32),
    VT=VMEM((4, 32, 128), F32),
    NB=VMEM((1, 24, 128), F32),
    NR=VMEM((8, 24, 128), F32),
    NQ=VMEM((4, 24, 128), F32),
    tail=VMEM((24, 128), F32),
    hp=VMEM((24, 128), F32),
    hn=VMEM((24, 128), F32),
    hp2=VMEM((24, 128), F32),
    hn2=VMEM((24, 128), F32),
    XR=VMEM((4, 1536, 256), BF),
    ZR=VMEM((5, 1536, 256), BF),
    QKV=VMEM((3, 1024, 256), BF),
    P=VMEM((4, 1024, 1024), BF),
    AT=VMEM((1024, 256), BF),
    RL=VMEM((1024, 256), F32),
    PB=VMEM((1024, 1024), BF),
    RB=VMEM((5, 256, 1024), BF),
    MID=VMEM((256, 1024), F32),
    GMID=VMEM((256, 1024), F32),
    NT=VMEM((1024, 1024), BF),
    GM=VMEM((1024, 1024), BF),
    AC=VMEM((1024, 1024), BF),
    GP=VMEM((1024, 1024), BF),
    GH=VMEM((1024, 1024), BF),
    hsem=DMA((4,)), pas=DMA((3,)), par_in=DMA((3,)), cas=DMA((3,)), car=DMA((3,)), qsem=DMA((24,)), csem=DMA((3,)), vsem=DMA((2,)), vxs=DMA, vxr=DMA((8,)),
    xs=DMA, xr=DMA((24,)), zsu=DMA((4,)), zsd=DMA((4,)), zr=DMA((24,)),
    s1s=DMA((18,)), s1r=DMA((18,)), s2s=DMA((18,)), s2r=DMA((18,)),
    s3s=DMA((18,)), s3r=DMA((18,)), s4s=DMA((18,)), s4r=DMA((18,)),
    hsem2=DMA((4,)), rxs=DMA, rxr=DMA((24,)), rzs=DMA((4,)), rzr=DMA((30,)),
    wxs=DMA, wxr=DMA((8,)), wqs=DMA, wqr=DMA((4,)),
    qsem2=DMA((96,)), csem2=DMA, nsem=DMA, nrsem=DMA((8,)), nqs=DMA, nqr=DMA((4,)),
)


class Refs:
    pass


def fast_layer(lens, pat, cot, par):
    outs = dict(
        act=((256, 1024), BF), ing=((256, 1024), BF), grad=((3075, 128), F32), norms=((24, 128), F32)
    )
    names = ["lens", "pat", "cot", "par"] + list(outs) + list(SCRATCH)

    def kernel(*refs):
        r = Refs()
        for name, ref in zip(names, refs):
            setattr(r, name, ref)
        whole_layer(Place(), r)

    whole = pl.BlockSpec(memory_space=pltpu.VMEM)
    return pl.pallas_call(
        kernel,
        out_shape=[jax.ShapeDtypeStruct(*o) for o in outs.values()],
        in_specs=[pl.BlockSpec(memory_space=pltpu.SMEM)] + [whole] * 3,
        out_specs=[whole] * len(outs),
        scratch_shapes=list(SCRATCH.values()),
        compiler_params=pltpu.CompilerParams(collective_id=0, has_side_effects=True, vmem_limit_bytes=VMEM_LIMIT),
    )(lens, pat, cot, par)


VMEM_LIMIT = 63 * 2**20
PLAIN_UNITS = ((0, 16), (24592, 24608), (32800, 32824), (65592, 65624), (98392, 98400))


def fast_shards(pat, cot, lens, params, m, v):
    def units(a):
        return a.reshape(-1, LANE)

    par = units(params)
    act, ing, grad, nb = fast_layer(lens[0], pat[0], cot[0], par)
    norms = jnp.sum(nb[:GROUPS], axis=1)
    clip = 1.0 / jnp.maximum(jnp.sqrt(jnp.sum(norms)), 1.0)
    start = lax.axis_index(("dp", "blk")) * par.shape[0]
    unit = start + lax.broadcasted_iota(jnp.int32, par.shape, 0)
    plain = jnp.zeros(par.shape, jnp.bool_)
    for lo, hi in PLAIN_UNITS:
        plain = plain | ((unit >= lo) & (unit < hi))
    scaled = clip * grad
    first = 0.9 * units(m) + 0.1 * scaled
    second = 0.999 * units(v) + 0.001 * scaled * scaled
    direction = first / (1.0 - 0.9**10) / (jnp.sqrt(second / (1.0 - 0.999**10)) + 1e-08)
    step = -0.001 * 0.9**12 * (direction + jnp.where(plain, 0.0, 0.05 * par))
    return act[None], ing[None], norms, step.reshape(-1), first.reshape(-1), nb[16:24].reshape(-1)


def solution(mesh):
    act, flat = P("dp", "blk", None), P(("dp", "blk"))
    specs = dict(
        in_specs=(act, act, P("dp", None), flat, flat, flat), out_specs=(act, act, P(), flat, flat, P()), check_vma=False
    )

    def layer(patches, cotangent, image_lengths, params, first_moment, second_moment):
        fits = (dict(mesh.shape), patches.shape, params.shape) == (dict(dp=8, blk=4), (8, 1024, D), (RAW,))
        step = jax.shard_map(fast_shards if fits else shards, mesh=mesh, **specs)
        return step(patches, cotangent, image_lengths, params, first_moment, second_moment)

    return layer
```

```python
from functools import partial
import math

import jax
import jax.numpy as jnp
from jax import lax
from jax.experimental import pallas as pl
from jax.experimental.pallas import tpu as pltpu
from jax.sharding import PartitionSpec as P

D = 1024
FF = 4096
HEADS = 16
HEAD_DIM = 64
GROUPS = 12
RAW = 12595200


eps_norm = 1e-06
neg_big = -1e30


def starts_of(model_width, hidden):
    square = model_width * model_width
    mlp_start = 7 * model_width + 4 * square
    return [
        0,
        model_width,
        2 * model_width,
        2 * model_width + 3 * square,
        4 * model_width + 3 * square,
        4 * model_width + 4 * square,
        5 * model_width + 4 * square,
        6 * model_width + 4 * square,
        mlp_start,
        mlp_start + model_width * hidden,
        mlp_start + model_width * hidden + hidden,
        mlp_start + 2 * model_width * hidden + hidden,
        mlp_start + 2 * model_width * hidden + hidden + model_width,
    ]


def unpack(flat_params):
    marks = starts_of(D, FF)
    pieces = [flat_params[marks[member] : marks[member + 1]] for member in range(12)]
    return (
        pieces[0],
        pieces[1],
        pieces[2].reshape(D, 3 * D),
        pieces[3],
        pieces[4].reshape(D, D),
        pieces[5],
        pieces[6],
        pieces[7],
        pieces[8].reshape(D, FF),
        pieces[9],
        pieces[10].reshape(FF, D),
        pieces[11],
    )


def layer_norm(values, gains, offsets):
    average = jnp.mean(values, axis=-1, keepdims=True)
    centred = values - average
    spread = jnp.mean(centred * centred, axis=-1, keepdims=True)
    return centred * lax.rsqrt(spread + eps_norm) * gains + offsets


def segment_ids(lengths, row_ids):
    bounds = jnp.cumsum(lengths)
    return jnp.sum((row_ids[:, None] >= bounds[None, :]).astype(jnp.int32), axis=1)


def shards(patches, cotangent, image_lengths, params, first_moment, second_moment):
    local_rows = patches.shape[1]
    seq_len = local_rows * lax.axis_size("blk")
    scale_of = HEAD_DIM ** (-0.5)
    inputs = patches[0].astype(jnp.float32)
    lengths = image_lengths[0]
    query_ids = lax.axis_index("blk") * local_rows + jnp.arange(local_rows, dtype=jnp.int32)
    query_labels = segment_ids(lengths, query_ids)
    weights_low = lax.all_gather(params.astype(jnp.bfloat16), ("dp", "blk"), axis=0, tiled=True)
    (
        gain_one,
        shift_one,
        w_qkv,
        bias_qv,
        w_out,
        bias_out,
        gain_two,
        shift_two,
        w_up,
        bias_up,
        w_down,
        bias_down,
    ) = unpack(weights_low)
    normed_one, pull_one = jax.vjp(
        layer_norm, inputs, gain_one.astype(jnp.float32), shift_one.astype(jnp.float32)
    )
    normed_low = normed_one.astype(jnp.bfloat16)
    bias_all = jnp.concatenate(
        [
            bias_qv[:D].astype(jnp.float32),
            jnp.zeros((D,), jnp.float32),
            bias_qv[D:].astype(jnp.float32),
        ]
    )
    projected = (jnp.dot(normed_low, w_qkv, preferred_element_type=jnp.float32) + bias_all).astype(
        jnp.bfloat16
    )
    queries = projected[:, :D].reshape(local_rows, HEADS, HEAD_DIM)
    key_value = projected[:, D:]

    def attend_block(state, block, block_labels):
        allowed = query_labels[:, None] == block_labels[None, :]
        best_in, total_in, summed_in = state
        raw = jnp.einsum("qhd,khd->hqk", queries, block[:, 0], preferred_element_type=jnp.float32)
        scores = jnp.where(allowed[None], raw * scale_of, neg_big)
        new_best = jnp.maximum(best_in, jnp.max(scores, axis=-1))
        factor = jnp.exp(best_in - new_best)
        weights = jnp.where(allowed[None], jnp.exp(scores - new_best[..., None]), 0.0)
        new_total = total_in * factor + jnp.sum(weights, axis=-1)
        added = jnp.einsum(
            "hqk,khd->qhd",
            weights.astype(jnp.bfloat16),
            block[:, 1],
            preferred_element_type=jnp.float32,
        )
        return (new_best, new_total, summed_in * factor.T[..., None] + added)

    start_state = (
        jnp.full((HEADS, local_rows), neg_big, jnp.float32),
        jnp.zeros((HEADS, local_rows), jnp.float32),
        jnp.zeros((local_rows, HEADS, HEAD_DIM), jnp.float32),
    )
    carry = start_state
    piece = lax.all_gather(key_value, "blk", axis=0, tiled=True)
    count = piece.shape[0]
    size = math.gcd(count, 512)
    blocks = piece.reshape(count // size, size, 2, HEADS, HEAD_DIM)
    labels = segment_ids(lengths, jnp.arange(count, dtype=jnp.int32)).reshape(count // size, size)

    def one_block(state, members):
        return (attend_block(state, members[0], members[1]), None)

    carry, ignored = lax.scan(one_block, carry, (blocks, labels))
    best, total, summed = carry
    attended = summed / total.T[..., None]
    log_total = best + jnp.log(total)
    attended_low = attended.reshape(local_rows, D).astype(jnp.bfloat16)
    branch = jnp.dot(attended_low, w_out, preferred_element_type=jnp.float32) + bias_out.astype(
        jnp.float32
    )
    middle = inputs + branch
    normed_two, pull_two = jax.vjp(
        layer_norm, middle, gain_two.astype(jnp.float32), shift_two.astype(jnp.float32)
    )
    normed_two_low = normed_two.astype(jnp.bfloat16)
    hidden_pre = jnp.dot(normed_two_low, w_up, preferred_element_type=jnp.float32) + bias_up.astype(
        jnp.float32
    )
    activated, pull_gelu = jax.vjp(partial(jax.nn.gelu, approximate=False), hidden_pre)
    activated_low = activated.astype(jnp.bfloat16)
    result = middle + (
        jnp.dot(activated_low, w_down, preferred_element_type=jnp.float32)
        + bias_down.astype(jnp.float32)
    )
    grad_out = cotangent[0]
    grad_down = jnp.dot(activated_low.T, grad_out, preferred_element_type=jnp.float32)
    grad_bias_down = jnp.sum(grad_out.astype(jnp.float32), axis=0)
    grad_act = jnp.dot(grad_out, w_down.T, preferred_element_type=jnp.float32)
    grad_hidden_low = pull_gelu(grad_act)[0].astype(jnp.bfloat16)
    grad_up = jnp.dot(normed_two_low.T, grad_hidden_low, preferred_element_type=jnp.float32)
    grad_bias_up = jnp.sum(grad_hidden_low.astype(jnp.float32), axis=0)
    grad_normed_two = jnp.dot(grad_hidden_low, w_up.T, preferred_element_type=jnp.float32)
    grad_mid_norm, grad_gain_two, grad_shift_two = pull_two(grad_normed_two)
    grad_middle = grad_out.astype(jnp.float32) + grad_mid_norm
    grad_middle_low = grad_middle.astype(jnp.bfloat16)
    grad_w_out = jnp.dot(attended_low.T, grad_middle_low, preferred_element_type=jnp.float32)
    grad_bias_out = jnp.sum(grad_middle_low.astype(jnp.float32), axis=0)
    grad_attended = (
        jnp.dot(grad_middle_low, w_out.T, preferred_element_type=jnp.float32)
        .astype(jnp.bfloat16)
        .reshape(local_rows, HEADS, HEAD_DIM)
    )
    delta_rows = jnp.sum(grad_attended.astype(jnp.float32) * attended, axis=-1).T
    gathered = lax.all_gather(key_value, "blk", axis=0, tiled=True)
    size = math.gcd(seq_len, 512)
    key_blocks = gathered.reshape(seq_len // size, size, 2, HEADS, HEAD_DIM)
    key_labels = segment_ids(lengths, jnp.arange(seq_len, dtype=jnp.int32)).reshape(
        seq_len // size, size
    )

    def back_block(grad_query, members):
        block, block_labels = members
        allowed = query_labels[:, None] == block_labels[None, :]
        raw = jnp.einsum("qhd,khd->hqk", queries, block[:, 0], preferred_element_type=jnp.float32)
        scores = jnp.where(allowed[None], raw * scale_of, neg_big)
        probs = jnp.where(allowed[None], jnp.exp(scores - log_total[..., None]), 0.0)
        grad_probs = jnp.einsum(
            "qhd,khd->hqk", grad_attended, block[:, 1], preferred_element_type=jnp.float32
        )
        grad_raw = (probs * (grad_probs - delta_rows[..., None]) * scale_of).astype(jnp.bfloat16)
        new_grad = grad_query + jnp.einsum(
            "hqk,khd->qhd", grad_raw, block[:, 0], preferred_element_type=jnp.float32
        )
        grad_keys = jnp.einsum(
            "hqk,qhd->khd", grad_raw, queries, preferred_element_type=jnp.float32
        )
        grad_values = jnp.einsum(
            "hqk,qhd->khd",
            probs.astype(jnp.bfloat16),
            grad_attended,
            preferred_element_type=jnp.float32,
        )
        return (new_grad, jnp.stack([grad_keys, grad_values], axis=1))

    grad_query, grad_kv_blocks = lax.scan(
        back_block, jnp.zeros((local_rows, HEADS, HEAD_DIM), jnp.float32), (key_blocks, key_labels)
    )
    grad_kv = lax.psum_scatter(
        grad_kv_blocks.reshape(seq_len, 2 * D).astype(jnp.bfloat16),
        "blk",
        scatter_dimension=0,
        tiled=True,
    ).astype(jnp.float32)
    grad_projected = jnp.concatenate([grad_query.reshape(local_rows, D), grad_kv], axis=1).astype(
        jnp.bfloat16
    )
    grad_w_qkv = jnp.dot(normed_low.T, grad_projected, preferred_element_type=jnp.float32)
    grad_proj_rows = jnp.sum(grad_projected.astype(jnp.float32), axis=0)
    grad_bias_qv = jnp.concatenate([grad_proj_rows[:D], grad_proj_rows[2 * D :]])
    grad_normed_one = jnp.dot(grad_projected, w_qkv.T, preferred_element_type=jnp.float32)
    grad_in_norm, grad_gain_one, grad_shift_one = pull_one(grad_normed_one)
    grad_inputs = grad_middle + grad_in_norm
    shard_len = params.shape[0]
    total_params = shard_len * lax.axis_size(("dp", "blk"))
    flat_grad = jnp.concatenate(
        [
            grad_gain_one,
            grad_shift_one,
            grad_w_qkv.reshape(-1),
            grad_bias_qv,
            grad_w_out.reshape(-1),
            grad_bias_out,
            grad_gain_two,
            grad_shift_two,
            grad_up.reshape(-1),
            grad_bias_up,
            grad_down.reshape(-1),
            grad_bias_down,
            jnp.zeros((total_params - RAW,), jnp.float32),
        ]
    )
    shard_grad = lax.psum_scatter(
        lax.slice_in_dim(flat_grad, 0, lax.axis_size(("dp", "blk")) * shard_len, axis=0),
        ("dp", "blk"),
        scatter_dimension=0,
        tiled=True,
    )
    positions = lax.axis_index(("dp", "blk")) * shard_len + jnp.arange(shard_len, dtype=jnp.int32)
    marks = jnp.array(starts_of(D, FF), dtype=jnp.int32)
    group_of = jnp.sum((positions[:, None] >= marks[None, :]).astype(jnp.int32), axis=1) - 1
    squares = shard_grad * shard_grad
    partials = jnp.sum(
        jnp.where(
            group_of[None, :] == jnp.arange(GROUPS, dtype=jnp.int32)[:, None], squares[None, :], 0.0
        ),
        axis=1,
    )
    norms, bias_total = lax.psum((partials, grad_bias_down), ("dp", "blk"))
    clip_factor = 1.0 / jnp.maximum(jnp.sqrt(jnp.sum(norms)), 1.0)
    decayed = ((group_of == 2) | (group_of == 4) | (group_of == 8) | (group_of == 10)).astype(
        jnp.float32
    )
    scaled = clip_factor * shard_grad
    new_first = 0.9 * first_moment + 0.1 * scaled
    new_second = 0.999 * second_moment + 0.001 * scaled * scaled
    direction = new_first / (1.0 - 0.9**10) / (jnp.sqrt(new_second / (1.0 - 0.999**10)) + 1e-08)
    param_step = -0.001 * 0.9**12 * (direction + 0.05 * decayed * params)
    return (
        result.astype(jnp.bfloat16)[None],
        grad_inputs.astype(jnp.bfloat16)[None],
        norms,
        param_step,
        new_first,
        bias_total,
    )


MESH = pl.DeviceIdType.MESH
LANE = 128


def pick(cond, yes, no):
    return jnp.where(cond, jnp.int32(yes), jnp.int32(no))


def rdma(src, dst, ssem, rsem, dev):
    return pltpu.make_async_remote_copy(src_ref=src, dst_ref=dst, send_sem=ssem, recv_sem=rsem, device_id=dev, device_id_type=MESH)


def rows(ref, start, size, step=128):
    return ref.at[pl.ds(pl.multiple_of(start, step), size)]


def gate(peers):
    sem = pltpu.get_barrier_semaphore()
    for peer in peers:
        pl.semaphore_signal(sem, inc=1, device_id=peer, device_id_type=MESH)
    pl.semaphore_wait(sem, len(peers))


class Place:
    def __init__(self):
        self.dp = lax.axis_index("dp")
        self.blk = lax.axis_index("blk")
        self.d = self.dp * 4 + self.blk
        self.z = self.dp // 2
        self.x = self.dp % 2
        self.y = self.blk // 2
        self.c = self.blk % 2
        self.xpeer = (self.z * 2 + 1 - self.x, self.blk)
        self.zs = [lax.rem(self.z + k, 4) for k in (1, 3, 2)]
        self.zpeers = [(zz * 2 + self.x, self.blk) for zz in self.zs]
        self.quad = [(self.dp, lax.rem(self.blk + k, 4)) for k in (1, 2, 3)]
        up = lax.rem(self.d + 1, 32)
        down = lax.rem(self.d + 31, 32)
        self.above = (self.dp + 2, self.blk)
        self.below = (self.dp - 2, self.blk)
        self.others = self.zpeers + [(zz * 2 + 1 - self.x, self.blk) for zz in self.zs]
        self.near = ((self.dp, self.y * 2 + 1 - self.c), (self.dp, (1 - self.y) * 2 + self.c))
        self.far = (1 - self.y) * 2 + self.c
        self.next = (up // 4, up % 4)
        self.prev = (down // 4, down % 4)
        d = self.d
        self.is_qkv = d < 8
        self.is_out = (d == 8) | (d == 9)
        self.is_mix_out = d == 10
        self.is_up = (d >= 11) & (d < 21)
        self.is_mix_down = d == 21
        self.is_down = d >= 22
        self.is_seg = self.is_out | self.is_down
        self.is_mix = self.is_mix_out | self.is_mix_down
        self.base = pick(d < 8, 16, pick(d < 11, 32, pick(d < 21, 56, 88))) - 3 * d
        self.seg0 = pick(d < 11, 3 * (d - 8), jnp.maximum(3 * (d - 21) - 1, 0))
        self.mix_up = pick(self.is_mix_out, 2074, -7)
        self.mix_seg = pick(self.is_mix_out, 2, 1049)

    def seg_home(self, n):
        seg = self.seg0 + n // 4
        panel = n % 4
        out_row = 3072 + 256 * panel + 128 * (seg % 2)
        down_row = 8192 + 1024 * panel + 128 * (seg // 4)
        low = self.d < 11
        return pick(low, seg // 2, seg % 4), pick(low, out_row, down_row)

    def block_home(self, n):
        part, row = self.seg_home(n)
        return pick(self.is_qkv, n % 4, part), pick(self.is_qkv, (n // 4) * 1024 + 128 * self.d, row)

    def up_home(self, n):
        start = pick(self.is_up, 32 + 96 * (self.d - 11), pick(self.is_mix_out, 0, 992))
        return n // 4, 4096 + 1024 * (n % 4) + start


def chunk_row(q, k):
    first = (k // 4) * 1024 + 512 * q + 128 * (k % 4)
    turn = 3 * (q - 2) + k // 4
    panel = k % 4
    other = pick(
        turn < 2,
        3072 + 256 * panel + 128 * turn,
        pick(turn < 10, 4096 + 1024 * panel + 128 * (turn - 2), 8192 + 1024 * panel + 128 * (turn - 10)),
    )
    return pick(q < 2, first, other)


def loop(count, body):
    def step(i, carry):
        body(i)
        return carry

    lax.fori_loop(0, count, step, 0)


def unit_span(start, stride):
    return pl.ds(start, 16, stride=stride)


def for_tiles(me, visit):
    e0 = 24 + me.base

    @pl.when(me.is_qkv)
    def _():
        def body(rb):
            for ct in range(24):
                n = (ct // 8) * 4 + (ct % 8) // 2
                visit(e0 + 384 * rb + ct, 24, n * 128 + 16 * rb, 128 * (ct % 2))

        loop(8, body)

    @pl.when(me.is_up)
    def _():
        def body(rb):
            for ct in range(32):
                n = (ct % 4) * 4 + ct // 8
                visit(e0 + 512 * rb + ct, 32, n * 96 + 16 * rb, 128 * ((ct // 4) % 2))

        loop(6, body)

    def segs(count, first):
        def body(i):
            for ct in range(8):
                visit(first + 128 * i + ct, 8, ((i // 8) * 4 + ct // 2) * 128 + 16 * (i % 8), 128 * (ct % 2))

        loop(count, body)

    @pl.when(me.is_seg)
    def _():
        segs(24, e0)

    @pl.when(me.is_mix)
    def _():
        segs(16, 24 + me.mix_seg)

        def body(rb):
            for ct in range(32):
                n = (ct % 4) * 4 + ct // 8
                visit(24 + me.mix_up + 512 * rb + ct, 32, 1024 + n * 32 + 16 * rb, 128 * ((ct // 4) % 2))

        loop(2, body)


def for_pieces(me, visit):
    @pl.when(me.is_qkv | me.is_seg)
    def _():
        def body(n):
            part, row = me.block_home(n)
            visit(n, n * 128, 128, part, row, 128)

        loop(12, body)

    @pl.when(me.is_up)
    def _():
        def body(n):
            part, row = me.up_home(n)
            visit(n, n * 96, 96, part, row, 32)

        loop(16, body)

    @pl.when(me.is_mix)
    def _():
        def body(n):
            part, row = me.seg_home(n)
            visit(n, n * 128, 128, part, row, 128)

        loop(8, body)

        def body_up(n):
            part, row = me.up_home(n)
            visit(8 + n, 1024 + n * 32, 32, part, row, 32)

        loop(16, body_up)


def vec_spots(me, visit):
    for cond, row, unit, count in (
        (me.d == 0, 0, 0, 16),
        (me.d == 7, 0, 3067, 8),
        (me.d == 8, 0, 0, 8),
        (me.d == 10, 8, 2050, 24),
        (me.d == 21, 0, 1017, 32),
        (me.d == 31, 0, 3067, 8),
    ):

        @pl.when(cond)
        def _(row=row, unit=unit, count=count):
            visit(row, 24 + unit, count)


BF, F32 = jnp.bfloat16, jnp.float32
EPS = 1e-06
OUT0, UP0, DOWN0 = 3072, 4096, 8192


def dot(a, b):
    return lax.dot_general(a, b, (((1,), (0,)), ((), ())), preferred_element_type=F32)


def dot_nt(a, b):
    return lax.dot_general(a, b, (((1,), (1,)), ((), ())), preferred_element_type=F32)


def dot_tn(a, b):
    return lax.dot_general(a, b, (((0,), (0,)), ((), ())), preferred_element_type=F32)


def block_of(i):
    return pl.ds(pl.multiple_of(i * 256, 256), 256)


def wide(r, q, first, count=8):
    return jnp.concatenate([r.XV[q, first + i : first + i + 1, :] for i in range(count)], axis=1)


def narrow(r, q, first):
    return jnp.concatenate([r.XV[q, pl.ds(first + i, 1), :] for i in range(2)], axis=1)


def put_vec(r, q, first, row, add=False):
    for i in range(row.shape[1] // 128):
        part = row[:, i * 128 : i * 128 + 128]
        if add:
            part = part + r.VG[q, first + i : first + i + 1, :]
        r.VG[q, first + i : first + i + 1, :] = part


def normalize(x):
    mean = jnp.mean(x, axis=-1, keepdims=True)
    cen = x - mean
    var = jnp.mean(cen * cen, axis=-1, keepdims=True)
    scale = lax.rsqrt(var + EPS)
    return cen * scale, scale


def norm_back(dy, xhat, scale, gain):
    t = dy * gain
    return scale * (t - jnp.mean(t, axis=-1, keepdims=True) - xhat * jnp.mean(t * xhat, axis=-1, keepdims=True))


def labels_at(r, at):
    total = jnp.zeros_like(at)
    bound = 0
    for k in range(9):
        bound = bound + r.lens[k]
        total = total + (at >= bound).astype(jnp.int32)
    return total


def lane_mask(h, value=1.0):
    lane = lax.broadcasted_iota(jnp.int32, (1, 128), 1)
    return jnp.where((lane // 64) == h, value, 0.0).astype(BF)


def crow(q, k):
    return pick(q < 2, 128 * k, 384 * (k % 4) + 128 * (k // 4))


class Other(Place):
    def __init__(self, me, i):
        d = me.dp * 4 + i
        self.d, self.blk, self.dp = d, i, me.dp
        self.is_qkv = d < 8
        self.is_out = (d == 8) | (d == 9)
        self.is_mix_out = d == 10
        self.is_up = (d >= 11) & (d < 21)
        self.is_mix_down = d == 21
        self.is_down = d >= 22
        self.is_seg = self.is_out | self.is_down
        self.is_mix = self.is_mix_out | self.is_mix_down
        self.seg0 = pick(d < 11, 3 * (d - 8), jnp.maximum(3 * (d - 21) - 1, 0))

    def seg_spot(self, n):
        seg = self.seg0 + n // 4
        low = self.d < 11
        turn = pick(low, seg % 2, 10 + seg // 4 - 3 * (self.dp - 2))
        return pick(low, seg // 2, seg % 4), 384 * (n % 4) + 128 * turn

    def block_spot(self, n):
        part, row = self.seg_spot(n)
        return pick(self.is_qkv, n % 4, part), pick(self.is_qkv, (n // 4) * 512 + 128 * (self.d % 4), row)

    def up_spot(self, n):
        start = pick(self.is_up, 32 + 96 * (self.d - 11), pick(self.is_mix_out, 0, 992))
        return n // 4, 384 * (n % 4) + 256 + start - 384 * (self.dp - 2)

    def pieces(self, visit):
        @pl.when(self.is_qkv | self.is_seg)
        def _():
            loop(12, lambda n: visit(n, n * 128, 128, *self.block_spot(n)))

        @pl.when(self.is_up)
        def _():
            loop(16, lambda n: visit(n, n * 96, 96, *self.up_spot(n)))

        @pl.when(self.is_mix)
        def _():
            loop(8, lambda n: visit(n, n * 128, 128, *self.seg_spot(n)))
            loop(16, lambda n: visit(8 + n, 1024 + n * 32, 32, *self.up_spot(n)))


def arrived(ref, sem):
    pltpu.make_async_copy(ref, ref, sem).wait()


def squares(x):
    s = jnp.sum(x * x, axis=0, keepdims=True)
    return s[:, :128] + s[:, 128:] if x.shape[1] == 256 else s


def by_z(me, values):
    out = jnp.int32(values[0])
    for n in (1, 2, 3):
        out = pick(me.z == n, values[n], out)
    return out


def span(zz, *groups):
    return tuple(zz * 6 + g for g in groups)


ALL = (0, 1, 2, 3, 4, 5)
def spots(*by_depth):
    most = max(len(groups) for groups in by_depth)
    return tuple(zip(*(groups + (24,) * (most - len(groups)) for groups in by_depth)))


NONE = ()
GATHER = dict(
    first=spots(span(0, 0, 1), span(1, 0, 1), span(2, 0, 1), span(3, 0, 1)),
    second=spots(span(0, 2, 3), span(0, 0, 1), span(2, 2, 3), span(3, 2, 3)),
    third=spots(span(0, 4, 5) + span(1, 0), span(0, 2, 3, 4), span(0, 0, 1, 2), span(3, 4, 5) + span(0, 0)),
    fourth=spots(span(1, 1), NONE, NONE, span(0, 1)),
    fifth=spots(span(1, 2, 3), span(0, 5), span(0, 3, 4), span(0, 2, 3)),
    sixth=spots(span(1, 4, 5), span(1, 2, 3), span(0, 5) + span(1, 0), span(0, 4, 5)),
    rows0=spots(NONE, span(1, 4, 5), span(1, 1) + span(3, 0), span(2, 0)),
    rows1=spots(NONE, span(2, 0, 1), span(1, 2) + span(3, 1), span(1, 0) + span(2, 1)),
    rows2=spots(span(2, 0), span(2, 2, 3), span(1, 3) + span(3, 2), span(1, 1) + span(2, 2)),
    rows3=spots(span(2, 1, 2), span(2, 4, 5), span(1, 4, 5) + span(3, 3), span(1, 2, 3)),
    out0=spots(span(2, 3, 4), span(3, 0, 1), span(2, 4, 5) + span(3, 4), span(1, 4, 5) + span(2, 3)),
    out1=spots(span(2, 5), span(3, 2, 3), span(3, 5), span(2, 4)),
    shared=spots(span(3, 0, 1, 2), span(3, 4, 5), NONE, span(2, 5)),
    normed=spots(span(3, 3, 4, 5), NONE, NONE, NONE),
)
SUMS = dict(
    start=spots(span(3, 0, 1, 2, 3), NONE, NONE, span(2, 0)),
    middle0=spots(span(3, 4), span(3, 0), NONE, NONE),
    middle1=spots(span(3, 5), span(3, 1, 2), span(3, 0), span(2, 1)),
    middle2=spots(span(2, 0), span(3, 3), span(3, 1), span(2, 2)),
    middle3=spots(span(2, 1, 2), span(3, 4, 5), span(3, 2, 3), span(2, 3)),
    attended=spots(span(2, 3, 4), span(2, 0, 1), span(3, 4, 5), span(2, 4, 5)),
    rows0=spots(span(2, 5), span(2, 2, 3), NONE, span(1, 0)),
    rows1=spots(span(1, 0), span(2, 4), NONE, span(1, 1)),
    rows2=spots(span(1, 1), NONE, span(1, 0), span(1, 2)),
    weights=spots(span(1, 2, 3), span(2, 5), span(1, 1, 2), span(1, 3, 4)),
    last=spots(span(1, 4, 5), NONE, span(1, 3), span(1, 5) + span(0, 0)),
    last0=spots(NONE, NONE, span(1, 4), span(0, 1)),
    last1=spots(NONE, NONE, span(1, 5) + span(0, 0), span(0, 2)),
    last2=spots(NONE, NONE, span(0, 1), span(0, 3)),
    last3=spots(NONE, span(0, 0), span(0, 2), span(0, 4)),
    end=spots(NONE, span(0, 1, 2, 3, 4, 5), span(0, 3, 4, 5), span(0, 5)),
)


def prepare(me, r):
    r.tail[...] = r.par[3051:3075, :]
    up = rdma(r.tail, r.hp, r.hsem.at[0], r.hsem.at[1], me.next)
    down = rdma(r.par.at[0:24], r.hn, r.hsem.at[2], r.hsem.at[3], me.prev)
    up.start()
    down.start()

    def put(i):
        r.E[pl.ds(pl.multiple_of(24 + 64 * i, 8), 64), :] = r.par[pl.ds(pl.multiple_of(64 * i, 8), 64), :]

    loop(48, put)
    r.E[3096:3099, :] = r.par[3072:3075, :]
    r.VS[...] = jnp.zeros_like(r.VS)

    def vec(row, unit, count):
        r.VS[row : row + count, :] = r.E[unit : unit + count, :].astype(BF).astype(F32)

    vec_spots(me, vec)
    vq = [rdma(r.VS, r.VQ.at[me.blk], r.vsem.at[0], r.vsem.at[1], peer) for peer in me.quad]
    for v in vq:
        v.start()
    r.VQ[me.blk] = r.VS[...]
    up.wait()
    down.wait()
    r.E[0:24, :] = r.hp[...]
    r.E[3099:3123, :] = r.hn[...]

    def tile(unit, stride, row, lane):
        r.S[pl.ds(pl.multiple_of(row, 16), 16), lane : lane + 128] = r.E[unit_span(unit, stride), :].astype(BF)

    for_tiles(me, tile)

    def which(i):
        return pick(me.is_qkv, jnp.minimum(i // 4, 2), 0)

    def visit(i, srow, size, part, frow, step):
        src, dst = rows(r.S, srow, size, 32), rows(r.F, frow, size, step)

        @pl.when(part != me.blk)
        def _():
            rdma(src, dst, r.qsem.at[i], r.csem.at[which(i)], (me.dp, part)).start()

        @pl.when(part == me.blk)
        def _():
            pltpu.make_async_copy(src, dst, r.csem.at[which(i)]).start()

    for_pieces(me, visit)
    arrived(r.VQ.at[0:3], r.vsem.at[0])
    arrived(r.VQ.at[0:3], r.vsem.at[1])
    r.XV[me.dp] = r.VQ[0] + r.VQ[1] + r.VQ[2] + r.VQ[3]
    for peer in me.others + [me.xpeer]:
        rdma(r.XV.at[me.dp], r.XV.at[me.dp], r.vxs, r.vxr.at[me.dp], peer).start()


def chunk_here(me, r, panel):
    @pl.when(me.is_qkv)
    def _():
        arrived(r.F.at[0:512], r.csem.at[panel])

    if panel == 0:

        @pl.when(jnp.logical_not(me.is_qkv))
        def _():
            arrived(r.F.at[0:1536], r.csem.at[0])


def prepare_drain(me, r):
    def visit(i, srow, size, part, frow, step):
        @pl.when(part != me.blk)
        def _():
            arrived(rows(r.S, srow, size, 32), r.qsem.at[i])

    for_pieces(me, visit)
    arrived(r.XV.at[0:7], r.vxs)


def own_down(me, r):
    @pl.when(me.z > 0)
    def _():
        def body(k):
            ref = rows(r.F, chunk_row(me.dp, k), 128)
            rdma(ref, ref, r.zsd.at[me.z], r.zr.at[me.z * 12 + k], me.below).start()

        loop(12, body)


def gather_step(me, r, groups):
    e = by_z(me, groups)
    if 24 in groups:

        @pl.when(e < 24)
        def _():
            gather_group(me, r, e)

    else:
        gather_group(me, r, e)


def gather_group(me, r, e):
    zz, g = e // 6, e % 6
    for i in range(2):
        n = 2 * e + i

        @pl.when(zz != me.z)
        def _(n=n):
            arrived(r.F.at[0:128], r.zr.at[n])

        ref = rows(r.F, chunk_row(zz * 2 + me.x, g * 2 + i), 128)

        @pl.when((zz <= me.z) & (me.z < 3))
        def _(n=n, ref=ref):
            rdma(ref, ref, r.zsu.at[zz], r.zr.at[n], me.above).start()

        @pl.when((zz > me.z) & (me.z > 0))
        def _(n=n, ref=ref):
            rdma(ref, ref, r.zsd.at[zz], r.zr.at[n], me.below).start()

        rdma(ref, ref, r.xs, r.xr.at[n], me.xpeer).start()


def gather_at(me, r, place):
    for groups in GATHER[place]:
        gather_step(me, r, groups)


def gathered(me, r, zz, groups=ALL):
    for g in groups:
        for i in range(2):
            arrived(r.F.at[0:128], r.xr.at[zz * 12 + 2 * g + i])


def gather_drain(me, r):
    arrived(r.F.at[0:6144], r.xs)
    for zz in range(4):
        @pl.when((zz <= me.z) & (me.z < 3))
        def _():
            arrived(r.F.at[0:1536], r.zsu.at[zz])

        @pl.when((zz >= me.z) & (me.z > 0))
        def _():
            arrived(r.F.at[0:1536], r.zsd.at[zz])


def swap_send(me, r, src, dst, ssem, rsem):
    mine = block_of(me.blk)
    for n, peer in enumerate(me.near):
        rdma(src, dst.at[mine], ssem.at[n], rsem.at[n], peer).start()
    dst[mine, :] = src[...]


def swap_pass(me, r, dst, ssem, rsem):
    far = dst.at[block_of((1 - me.y) * 2 + me.c)]
    arrived(far, rsem.at[1])
    rdma(far, far, ssem.at[2], rsem.at[2], me.near[0]).start()


def swap_drain(me, r, dst, ssem):
    for n in range(3):
        arrived(dst.at[0:256], ssem.at[n])


def nothing(n):
    pass


class QuadSum:
    def __init__(self, me, r, term, make, sems, finish, slot, out=None):
        self.me, self.r, self.term, self.make, self.finish, self.slot, self.out = me, r, term, make, finish, slot, out
        self.ssem, self.rsem = sems
        y, c = me.y, me.c
        self.far_sib, self.far, self.near_sib, self.own = (1 - y) * 2 + 1 - c, (1 - y) * 2 + c, y * 2 + 1 - c, me.blk
        self.sib, self.yp = me.near
        self.over = []

    def copy(self, src, dst, n, dev):
        return rdma(src, dst, self.ssem.at[n], self.rsem.at[n], dev)

    def at(self, dev, i):
        return pl.ds(pl.multiple_of(dev * 256 + 64 * i, 64), 64)

    def send_far_sib(self):
        self.a = self.copy(self.term.at[block_of(self.far_sib)], self.r.RB.at[0], 0, self.sib)
        self.a.start()

    def send_near_sib(self):
        self.d = self.copy(self.term.at[block_of(self.near_sib)], self.r.RB.at[1], 1, self.sib)
        self.d.start()

    def cross(self):
        r = self.r
        self.a.wait_recv()
        for i in range(4):
            lo = pl.ds(64 * i, 64)
            r.RB[3, lo, :] = (self.term[self.at(self.far, i), :].astype(F32) + r.RB[0, lo, :].astype(F32)).astype(BF)
            self.over.append(self.copy(r.RB.at[3, lo], r.RB.at[self.slot, lo], 2 + i, self.yp))
            self.over[i].start()

    def begin(self):
        self.make(self.far_sib)
        self.send_far_sib()
        self.make(self.far)
        self.cross()
        self.make(self.near_sib)
        self.send_near_sib()
        self.make(self.own)

    def end(self, idle=nothing):
        r = self.r
        self.d.wait_recv()
        out, near, on = [], [], []
        for i in range(4):
            self.over[i].wait_recv()
            lo = slice(64 * i, 64 * i + 64)
            total = self.term[self.at(self.own, i), :].astype(F32) + r.RB[1, lo, :].astype(F32)
            self.finish(lo, total + r.RB[self.slot, lo, :].astype(F32))
            if self.out is not None:
                part, passed = self.out.at[self.at(self.own, i)], self.out.at[self.at(self.far, i)]
                out.append(self.copy(part, part, 6 + i, self.yp))
                near.append(self.copy(part, part, 10 + i, self.sib))
                on.append(self.copy(passed, passed, 14 + i, self.sib))
                out[i].start()
                near[i].start()
            idle(i)
        for i in range(len(out)):
            out[i].wait_recv()
            on[i].start()
        for cp in near + on:
            cp.wait()
        for cp in [self.a, self.d] + self.over + out:
            cp.wait_send()


def first_norm(me, r, half):
    gain, shift = wide(r, 0, 0), wide(r, 0, 8)

    def ln(i):
        at = pl.ds(pl.multiple_of(half * 512 + i * 64, 64), 64)
        x = r.PA[at, :]
        for p in range(4):
            row = pl.multiple_of(PATCH0 + 1024 * p + half * 512 + i * 64, 64)
            r.G[pl.ds(row, 64), :] = x[:, 256 * p : 256 * p + 256]
        xhat, _ = normalize(x.astype(F32))
        r.PA[at, :] = (xhat * gain + shift).astype(BF)

    loop(8, ln)


def attention(me, r, idle):
    bias = [narrow(r, 1, 2 * me.blk), None, narrow(r, 2, 2 * me.blk)]

    def proj(i):
        at = block_of(i)
        for j in range(3):
            out = dot(r.PA[at, :], r.F[j * 1024 : j * 1024 + 1024, :])
            if bias[j] is not None:
                out = out + bias[j]
            r.QKV[j, at, :] = out.astype(BF)

    loop(4, proj)
    key_labels = labels_at(r, lax.broadcasted_iota(jnp.int32, (1, 1024), 1))

    def attend(i):
        at = block_of(i)
        row_labels = labels_at(r, lax.broadcasted_iota(jnp.int32, (256, 1), 0) + i * 256)
        allowed = row_labels == key_labels
        for t in range(2):
            lanes = slice(128 * t, 128 * t + 128)
            q = r.QKV[0, at, lanes]
            k = r.QKV[1, :, lanes]
            v = r.QKV[2, :, lanes]
            out = jnp.zeros((256, 128), F32)
            inverse = []
            for h in range(2):
                s = jnp.where(allowed, dot_nt(q * lane_mask(h, 0.125), k), -1e30)
                w = jnp.exp(s - jnp.max(s, axis=-1, keepdims=True))
                inverse.append(1.0 / jnp.sum(w, axis=-1, keepdims=True))
                p = w.astype(BF)
                r.P[2 * t + h, at, :] = p
                out = out + dot(p, v * lane_mask(h))
            low_lanes = lax.broadcasted_iota(jnp.int32, (256, 128), 1) < 64
            scale = jnp.where(low_lanes, inverse[0], inverse[1])
            r.RL[at, lanes] = scale
            r.AT[at, lanes] = (out * scale).astype(BF)

    for i in range(4):
        attend(i)
        attended_send(me, r, i)
        if i > 0:
            attended_pass(me, r, i - 1)
        idle(i)


ATTENDED0, WHOLE_OUT0, PATCH0 = 0, 4096, 8192


def attended_send(me, r, i):
    dst = rows(r.G, ATTENDED0 + 1024 * me.blk + 256 * i, 256)
    for n in range(2):
        rdma(r.AT.at[256 * i : 256 * i + 256], dst, r.ats.at[2 * i + n], r.atr.at[2 * i + n], me.near[n]).start()


def attended_pass(me, r, i):
    ref = rows(r.G, ATTENDED0 + 1024 * me.far + 256 * i, 256)
    arrived(ref, r.atr.at[2 * i + 1])
    rdma(ref, ref, r.ats.at[8 + i], r.atr.at[8 + i], me.near[0]).start()


def out_send(me, r, half):
    @pl.when(me.x == 1)
    def _():
        gathered(me, r, 1, (0, 1) if half == 0 else (2, 3))

    for p in range(4):
        at = 256 * p + 128 * half
        src, dst = r.F.at[OUT0 + at : OUT0 + at + 128], rows(r.G, WHOLE_OUT0 + 1024 * me.blk + at, 128)
        for n in range(2):
            rdma(src, dst, r.wos.at[2 * half + n], r.wor.at[2 * half + n], me.near[n]).start()


def out_pass(me, r, half):
    arrived(r.G.at[0:512], r.wor.at[2 * half + 1])
    for p in range(4):
        ref = rows(r.G, WHOLE_OUT0 + 1024 * me.far + 256 * p + 128 * half, 128)
        rdma(ref, ref, r.wos.at[4 + half], r.wor.at[4 + half], me.near[0]).start()


def shared_here(me, r):
    for i in range(4):
        arrived(r.G.at[0:256], r.atr.at[2 * i])
        arrived(r.G.at[0:256], r.atr.at[8 + i])
    for half in range(2):
        arrived(r.G.at[0:512], r.wor.at[2 * half])
        arrived(r.G.at[0:512], r.wor.at[4 + half])
    for i in range(12):
        arrived(r.G.at[0:256], r.ats.at[i])
    for i in range(6):
        arrived(r.G.at[0:512], r.wos.at[i])
    r.G[pl.ds(pl.multiple_of(ATTENDED0 + 1024 * me.blk, 1024), 1024), :] = r.AT[...]
    r.G[pl.ds(pl.multiple_of(WHOLE_OUT0 + 1024 * me.blk, 1024), 1024), :] = r.F[OUT0 : OUT0 + 1024, :]


def second_norm(me, r):
    bias_out = wide(r, 2, 8)
    gain, shift = wide(r, 2, 16), wide(r, 2, 24)

    def body(i):
        for p in range(4):
            lanes = slice(256 * p, 256 * p + 256)
            acc = r.G[pl.ds(pl.multiple_of(PATCH0 + 1024 * p + 256 * i, 256), 256), :].astype(F32) + bias_out[:, lanes]
            for part in range(4):
                weights = r.G[WHOLE_OUT0 + 1024 * part + 256 * p : WHOLE_OUT0 + 1024 * part + 256 * p + 256, :]
                acc = acc + dot(r.G[pl.ds(pl.multiple_of(ATTENDED0 + 1024 * part + 256 * i, 256), 256), :], weights)
            r.GMID[:, lanes] = acc

        def ln(n):
            at = pl.ds(pl.multiple_of(n * 64, 64), 64)
            xhat, _ = normalize(r.GMID[at, :])
            r.NT[pl.ds(pl.multiple_of(i * 256 + n * 64, 64), 64), :] = (xhat * gain + shift).astype(BF)

        loop(4, ln)

        @pl.when(i == me.blk)
        def _():
            r.MID[...] = r.GMID[...]

    loop(4, body)


def hidden(me, r):
    biases = [jnp.concatenate([r.XV[5, pl.ds(4 * (2 * p + i) + me.blk, 1), :] for i in range(2)], axis=1) for p in range(4)]

    def up(i):
        at = pl.ds(pl.multiple_of(i * 128, 128), 128)
        for p in range(4):
            h = dot(r.NT[at, :], r.F[UP0 + 1024 * p : UP0 + 1024 * p + 1024, :]) + biases[p]
            phi = 0.5 + 0.5 * lax.erf(h * 0.7071067811865476)
            lanes = slice(256 * p, 256 * p + 256)
            r.AC[at, lanes] = (h * phi).astype(BF)
            r.GP[at, lanes] = (phi + h * (jnp.exp(-0.5 * h * h) * 0.3989422804014327)).astype(BF)

    loop(8, up)


def hidden_grad(me, r):
    def body(i):
        at = block_of(i)
        for p in range(4):
            lanes = slice(256 * p, 256 * p + 256)
            acc = jnp.zeros((256, 256), F32)
            for k in range(4):
                down = r.F[DOWN0 + 1024 * k + 256 * p : DOWN0 + 1024 * k + 256 * p + 256, :]
                acc = acc + dot_nt(r.CA[at, 256 * k : 256 * k + 256], down)
            r.GH[at, lanes] = (acc * r.GP[at, lanes].astype(F32)).astype(BF)

    loop(4, body)


def hidden_sums(me, r):
    for p in range(4):
        sums = jnp.sum(r.GH[:, 256 * p : 256 * p + 256].astype(F32), axis=0, keepdims=True)
        for i in range(2):
            r.VG[5, pl.ds(4 * (2 * p + i) + me.blk, 1), :] = sums[:, 128 * i : 128 * i + 128]
    put_vec(r, 7, 0, jnp.sum(r.cot[...].astype(F32), axis=0, keepdims=True))


def weight_grad(r, left, right, base, height):
    def body(i):
        cols = pl.ds(pl.multiple_of(i * 256, 256), 256)
        lt = left[:, cols].T
        for p in range(right.shape[1] // 256):
            out = dot(lt, right[:, 256 * p : 256 * p + 256])
            r.G[pl.ds(pl.multiple_of(base + p * height + i * 256, 256), 256), :] = out.astype(BF)

    loop(height // 256, body)


def middle_grad(me, r, sums):
    def term(i):
        at = block_of(i)
        for n in range(4):
            acc = jnp.zeros((256, 256), F32)
            for p in range(4):
                up = r.F[UP0 + 1024 * p + 256 * n : UP0 + 1024 * p + 256 * n + 256, :]
                acc = acc + dot_nt(r.GH[at, 256 * p : 256 * p + 256], up)
            r.PB[at, 256 * n : 256 * n + 256] = acc.astype(BF)

    gain = wide(r, 2, 16)
    sums[:] = [jnp.zeros((1, 1024), F32)] * 3

    def finish(lo, dy):
        xhat, scale = normalize(r.MID[lo, :])
        gm = r.cot[lo, :].astype(F32) + norm_back(dy, xhat, scale, gain)
        r.GMID[lo, :] = gm
        low = gm.astype(BF)
        r.GM[pl.ds(pl.multiple_of(me.blk * 256 + lo.start, 64), 64), :] = low
        for n, term_of in enumerate((low.astype(F32), dy * xhat, dy)):
            sums[n] = sums[n] + jnp.sum(term_of, axis=0, keepdims=True)

    return QuadSum(me, r, r.PB, term, (r.s2s, r.s2r), finish, 4, r.GM)


def attended_grad(me, r):
    def body(i):
        at = block_of(i)
        acc = jnp.zeros((256, 256), F32)
        for p in range(4):
            acc = acc + dot_nt(r.GM[at, 256 * p : 256 * p + 256], r.F[OUT0 + 256 * p : OUT0 + 256 * p + 256, :])
        r.GP[at, 768:1024] = acc.astype(BF)

    loop(4, body)


def attention_grad(me, r, idle):
    r.E[...] = jnp.zeros_like(r.E)

    def attend(i):
        at = block_of(i)
        for t in range(2):
            lanes = slice(128 * t, 128 * t + 128)
            q = r.QKV[0, at, lanes]
            k = r.QKV[1, :, lanes]
            v = r.QKV[2, :, lanes]
            da = (r.GP[at, 768 + 128 * t : 896 + 128 * t].astype(F32) * r.RL[at, lanes]).astype(BF)
            overlap = da.astype(F32) * r.AT[at, lanes].astype(F32)
            dq = jnp.zeros((256, 128), F32)
            for h in range(2):
                m, m8 = lane_mask(h), lane_mask(h, 0.125)
                p = r.P[2 * t + h, at, :]
                delta = jnp.sum(overlap * m.astype(F32), axis=-1, keepdims=True)
                ds = (p.astype(F32) * (dot_nt(da * m, v) - delta)).astype(BF)
                dq = dq + dot(ds, k * m8)
                r.E[1024 * t : 1024 * t + 1024, :] += dot_tn(ds, q * m8)
                r.E[2048 + 1024 * t : 3072 + 1024 * t, :] += dot_tn(p, da * m)
            r.GP[at, lanes] = dq.astype(BF)

    for i in range(4):
        attend(i)
        if i < 3:
            idle(i)
    for n in range(4):
        r.GP[:, 256 + 128 * n : 384 + 128 * n] = r.E[1024 * n : 1024 * n + 1024, :].astype(BF)


def projection_sums(me, r):
    for j, q in ((0, 1), (2, 2)):
        sums = jnp.sum(r.GP[:, 256 * j : 256 * j + 256].astype(F32), axis=0, keepdims=True)
        for i in range(2):
            r.VG[q, pl.ds(2 * me.blk + i, 1), :] = sums[:, 128 * i : 128 * i + 128]


def projection_grad(me, r):
    def body(i):
        cols = pl.ds(pl.multiple_of(i * 256, 256), 256)
        lt = r.PA[:, cols].T
        for j in range(3):
            r.G[pl.ds(pl.multiple_of(j * 1024 + i * 256, 256), 256), :] = dot(lt, r.GP[:, 256 * j : 256 * j + 256]).astype(BF)

    loop(4, body)


def input_grad(me, r, sums):
    def term(i):
        at = block_of(i)
        for n in range(4):
            acc = jnp.zeros((256, 256), F32)
            for j in range(3):
                acc = acc + dot_nt(r.GP[at, 256 * j : 256 * j + 256], r.F[1024 * j + 256 * n : 1024 * j + 256 * n + 256, :])
            r.PB[at, 256 * n : 256 * n + 256] = acc.astype(BF)

    gain = wide(r, 0, 0)
    sums[:] = [jnp.zeros((1, 1024), F32)] * 2

    def finish(lo, dy):
        xhat, scale = normalize(r.pat[lo, :].astype(F32))
        r.ing[lo, :] = (r.GMID[lo, :] + norm_back(dy, xhat, scale, gain)).astype(BF)
        for n, term_of in enumerate((dy * xhat, dy)):
            sums[n] = sums[n] + jnp.sum(term_of, axis=0, keepdims=True)

    return QuadSum(me, r, r.PB, term, (r.s4s, r.s4r), finish, 4)


def layer_out(me, r):
    def term(i):
        at = block_of(i)
        for p in range(4):
            r.CA[at, 256 * p : 256 * p + 256] = dot(r.AC[at, :], r.F[DOWN0 + 1024 * p : DOWN0 + 1024 * p + 1024, :]).astype(BF)

    bias_down = wide(r, 7, 0)

    def finish(lo, total):
        r.act[lo, :] = (r.MID[lo, :] + (total + bias_down)).astype(BF)

    return QuadSum(me, r, r.CA, term, (r.s3s, r.s3r), finish, 2)


def reduce_send(me, r, zz, first=0, count=12):
    q = zz * 2 + 1 - me.x

    def body(i):
        k = first + i
        rdma(rows(r.G, chunk_row(q, k), 128), rows(r.XR.at[zz], crow(q, k), 128), r.rxs, r.rxr.at[zz * 12 + k], me.xpeer).start()

    loop(count, body)


def reduce_step(me, r, groups):
    e = by_z(me, groups)

    @pl.when(e < 24)
    def _():
        zz, g = e // 6, e % 6
        q = zz * 2 + me.x
        down = zz < me.z

        def body(i):
            k = g * 2 + i
            n = zz * 12 + k
            arrived(r.G.at[0:128], r.rxr.at[n])

            @pl.when((me.z > 0) & (me.z < 3))
            def _():
                arrived(r.G.at[0:128], r.rzr.at[n])

            src, at = pl.ds(pl.multiple_of(chunk_row(q, k), 128), 128), pl.ds(pl.multiple_of(crow(q, k), 128), 128)
            total = r.G[src, :].astype(F32) + r.XR[zz, at, :].astype(F32) + r.ZR[zz, at, :].astype(F32)
            r.XR[zz, at, :] = total.astype(BF)
            sent = rows(r.XR.at[zz], crow(q, k), 128)

            @pl.when(down)
            def _():
                rdma(sent, rows(r.ZR.at[zz], crow(q, k), 128), r.rzs.at[zz], r.rzr.at[n], me.below).start()

            @pl.when(jnp.logical_not(down))
            def _():
                last = zz == me.z + 1
                slot, sem = pick(last, 4, zz), pick(last, 48 + k, n)
                rdma(sent, rows(r.ZR.at[slot], crow(q, k), 128), r.rzs.at[zz], r.rzr.at[sem], me.above).start()

        loop(2, body)


def sums_at(me, r, place):
    for groups in SUMS[place]:
        reduce_step(me, r, groups)


def reduce_last(me, r):
    first_tensor = pick(me.dp < 2, 2, pick(me.dp == 2, 4, pick(me.dp < 6, 8, 10)))

    def group(g):
        part = jnp.zeros((1, 128), F32)
        for i in range(2):
            k = g * 2 + i
            n = me.z * 12 + k
            arrived(r.G.at[0:128], r.rxr.at[n])

            @pl.when(me.z < 3)
            def _(n=n):
                arrived(r.G.at[0:128], r.rzr.at[n])

            @pl.when(me.z > 0)
            def _(k=k):
                arrived(r.G.at[0:128], r.rzr.at[48 + k])

            src, at = pl.ds(pl.multiple_of(chunk_row(me.dp, k), 128), 128), pl.ds(pl.multiple_of(crow(me.dp, k), 128), 128)
            total = r.G[src, :].astype(F32) + r.XR[me.z, at, :].astype(F32)
            total = total + (r.ZR[me.z, at, :].astype(F32) + r.ZR[4, at, :].astype(F32))
            part = part + squares(total)
            r.XR[me.z, at, :] = total.astype(BF)
        tensor = pick((g >= 4) & (me.dp == 2), 8, pick((g >= 2) & (me.dp == 5), 10, first_tensor))
        r.NB[0, pl.ds(tensor, 1), :] += part

    def pair(j):
        group(2 * j)
        group(2 * j + 1)

        @pl.when(me.is_qkv)
        def _():
            for i in range(4):
                src = rows(r.XR.at[me.z], j * 512 + 128 * i, 128)
                dst = rows(r.S, (j * 4 + me.blk) * 128, 128)

                @pl.when(me.blk != i)
                def _():
                    rdma(src, dst, r.qsem2.at[i * 24 + j * 4 + me.blk], r.csem2, (me.dp, i)).start()

                @pl.when(me.blk == i)
                def _():
                    pltpu.make_async_copy(src, dst, r.csem2).start()

    loop(3, pair)

    @pl.when(jnp.logical_not(me.is_qkv))
    def _():
        for i in range(4):
            def visit(n, srow, size, part, row, i=i):
                src, dst = rows(r.XR.at[me.z], row, size, 32), rows(r.S, srow, size, 32)

                @pl.when((part == me.blk) & (me.blk != i))
                def _():
                    rdma(src, dst, r.qsem2.at[i * 24 + n], r.csem2, (me.dp, i)).start()

                @pl.when((part == me.blk) & (me.blk == i))
                def _():
                    pltpu.make_async_copy(src, dst, r.csem2).start()

            Other(me, i).pieces(visit)


def column(me):
    return [(lax.rem(me.dp + k, 8), me.blk) for k in range(1, 8)]


VECTORS = ((0, 16), (1, 8), (2, 32), (5, 32), (7, 8))


def vectors_send(me, r, early):
    for q, count in VECTORS:
        if early == (q > 0):
            @pl.when(me.dp != q)
            def _(q=q, count=count):
                rdma(r.VG.at[q, 0:count], r.VX.at[me.dp, 0:count], r.wxs.at[q], r.wxr.at[me.dp], (q, me.blk)).start()


def vectors_sum(me, r):
    for q, count in VECTORS:
        @pl.when(me.dp == q)
        def _(q=q, count=count):
            total = r.VG[q, 0:count, :]
            for other in range(8):
                if other != q:
                    arrived(r.VX.at[0, 0:count], r.wxr.at[other])
                    total = total + r.VX[other, 0:count, :]
            r.VT[me.blk, 0:count, :] = total
            for peer in me.quad:
                rdma(r.VT.at[me.blk, 0:count], r.VT.at[me.blk, 0:count], r.wqs, r.wqr.at[me.blk], peer).start()


def vectors_end(me, r):
    for q, count in VECTORS:
        @pl.when(me.dp == q)
        def _(q=q, count=count):
            for k in (1, 2, 3):
                arrived(r.VT.at[0, 0:count], r.wqr.at[lax.rem(me.blk + k, 4)])
            r.VS[0:count, :] = r.VT[0, 0:count, :] + r.VT[1, 0:count, :] + r.VT[2, 0:count, :] + r.VT[3, 0:count, :]
            arrived(r.VT.at[0:3, 0:count], r.wqs)

        @pl.when(me.dp != q)
        def _(q=q, count=count):
            arrived(r.VG.at[q, 0:count], r.wxs.at[q])

    vector_squares(me, r)


def norms_pack(me, r):
    sums = jnp.sum(r.NB[0, 0:16, :], axis=1, keepdims=True)
    tensor = lax.broadcasted_iota(jnp.int32, (16, 128), 0)
    lane = lax.broadcasted_iota(jnp.int32, (16, 128), 1)
    line = jnp.sum(jnp.where(tensor == lane, sums, 0.0), axis=0, keepdims=True)
    r.NM[0:8, :] = jnp.broadcast_to(line, (8, 128))
    r.NM[8:16, :] = r.NB[0, 16:24, :]


def norms_send(me, r):
    norms_pack(me, r)
    for peer in column(me):
        rdma(r.NM, r.NR.at[me.dp], r.nsem, r.nrsem.at[me.dp], peer).start()
    r.NR[me.dp] = r.NM[...]


def norms_sum(me, r):
    for q, _ in column(me):
        arrived(r.NR.at[0], r.nrsem.at[q])
    total = r.NR[0]
    for q in range(1, 8):
        total = total + r.NR[q]
    r.NQ[me.blk] = total
    for peer in me.quad:
        rdma(r.NQ.at[me.blk], r.NQ.at[me.blk], r.nqs, r.nqr.at[me.blk], peer).start()


def norms_end(me, r):
    for k in (1, 2, 3):
        arrived(r.NQ.at[0], r.nqr.at[lax.rem(me.blk + k, 4)])
    r.norms[...] = r.NQ[0] + r.NQ[1] + r.NQ[2] + r.NQ[3]
    arrived(r.NR.at[0:7], r.nsem)
    arrived(r.NQ.at[0:3], r.nqs)


def vector_squares(me, r):
    for q, tensors in ((0, (0, 1, None, None)), (1, (3, None, None, None)), (2, (3, 5, 6, 7)), (5, (9, 9, 9, 9)), (7, (11, None, None, None))):
        @pl.when((me.dp == q) & (me.blk == 0))
        def _(q=q, tensors=tensors):
            for g, tensor in enumerate(tensors):
                if tensor is not None:
                    r.NB[0, tensor : tensor + 1, :] += squares(r.VS[8 * g : 8 * g + 8, :])
            if q == 7:
                r.NB[0, 16:24, :] = r.VS[0:8, :]


def reduce_drain(me, r):
    arrived(r.G.at[0:6144], r.rxs)
    for i in range(4):
        @pl.when(me.z != i)
        def _(i=i):
            arrived(r.G.at[0:1536], r.rzs.at[i])

        def visit(n, srow, size, part, row, i=i):
            @pl.when((part == me.blk) & (me.blk != i))
            def _():
                arrived(rows(r.XR.at[me.z], row, size, 32), r.qsem2.at[i * 24 + n])

        Other(me, i).pieces(visit)


def units_send(me, r):
    arrived(r.S, r.csem2)
    for lo, hi in ((0, 48), (3072, 3128)):
        r.E[lo:hi, :] = jnp.zeros((hi - lo, 128), F32)

    def tile(unit, stride, row, lane):
        r.E[unit_span(unit, stride), :] = r.S[pl.ds(pl.multiple_of(row, 16), 16), lane : lane + 128].astype(F32)

    for_tiles(me, tile)

    def vec(row, unit, count):
        r.E[unit : unit + count, :] = r.VS[row : row + count, :]

    vec_spots(me, vec)
    r.tail[...] = r.E[3099:3123, :]
    rdma(r.tail, r.hp2, r.hsem2.at[0], r.hsem2.at[1], me.next).start()
    rdma(r.E.at[0:24], r.hn2, r.hsem2.at[2], r.hsem2.at[3], me.prev).start()


def units_end(me, r):
    def put(i):
        r.grad[pl.ds(pl.multiple_of(64 * i, 8), 64), :] = r.E[pl.ds(pl.multiple_of(24 + 64 * i, 8), 64), :]

    loop(48, put)
    r.grad[3072:3075, :] = r.E[3096:3099, :]
    for n in range(4):
        arrived(r.tail, r.hsem2.at[n])
    r.grad[0:24, :] += r.hp2[...]
    r.grad[3051:3075, :] += r.hn2[...]


def whole_layer(me, r):
    r.VG[...] = jnp.zeros_like(r.VG)
    r.NB[0] = jnp.zeros((24, 128), F32)

    def clear(slot):
        r.ZR[slot] = jnp.zeros((1536, 256), BF)

    @pl.when(me.z == 0)
    def _():
        loop(4, lambda i: clear(i + 1))

    @pl.when(me.z == 3)
    def _():
        loop(4, clear)

    gate(me.quad + me.others + [me.xpeer, me.next, me.prev])
    prepare(me, r)
    chunk_here(me, r, 0)
    own_down(me, r)
    gather_at(me, r, "first")
    chunk_here(me, r, 1)
    gather_at(me, r, "second")
    chunk_here(me, r, 2)
    swap_send(me, r, r.pat, r.PA, r.pas, r.par_in)
    gather_at(me, r, "third")
    swap_pass(me, r, r.PA, r.pas, r.par_in)
    swap_send(me, r, r.cot, r.CA, r.cas, r.car)
    for peer in range(1, 8):
        arrived(r.XV.at[0], r.vxr.at[lax.rem(me.dp + peer, 8)])
    gather_at(me, r, "fourth")
    arrived(r.PA.at[0:256], r.par_in.at[0])
    first_norm(me, r, me.y)
    gather_at(me, r, "fifth")
    arrived(r.PA.at[0:256], r.par_in.at[2])
    swap_drain(me, r, r.PA, r.pas)
    first_norm(me, r, 1 - me.y)
    gather_at(me, r, "sixth")
    prepare_drain(me, r)
    gathered(me, r, 0)

    def between(n):
        if n == 1:
            swap_pass(me, r, r.CA, r.cas, r.car)
        gather_at(me, r, "rows%d" % n)

    attention(me, r, between)
    out_send(me, r, 0)
    out_send(me, r, 1)
    attended_pass(me, r, 3)
    gather_at(me, r, "out0")
    out_pass(me, r, 0)
    gather_at(me, r, "out1")
    out_pass(me, r, 1)
    shared_here(me, r)
    gather_at(me, r, "shared")
    second_norm(me, r)
    gather_at(me, r, "normed")

    @pl.when(me.x == 0)
    def _():
        gathered(me, r, 1, (0, 1, 2, 3))

    gathered(me, r, 1, (4, 5))
    gathered(me, r, 2)
    hidden(me, r)
    arrived(r.CA.at[0:256], r.car.at[0])
    arrived(r.CA.at[0:256], r.car.at[2])
    swap_drain(me, r, r.CA, r.cas)
    weight_grad(r, r.AC, r.CA, DOWN0, 1024)
    reduce_send(me, r, 3, 0, 6)

    @pl.when(me.z < 3)
    def _():
        reduce_send(me, r, 3, 6, 6)

    gathered(me, r, 3)
    gather_drain(me, r)
    hidden_grad(me, r)
    middle_sums, input_sums = [], []
    middle = middle_grad(me, r, middle_sums)
    middle.begin()
    weight_grad(r, r.NT, r.GH, UP0, 1024)
    reduce_send(me, r, 2)

    @pl.when(me.z == 3)
    def _():
        reduce_send(me, r, 3, 6, 6)

    result = layer_out(me, r)
    loop(4, result.make)
    sums_at(me, r, "start")
    middle.end(lambda n: sums_at(me, r, "middle%d" % n))
    for n in range(3):
        put_vec(r, 2, 8 + 8 * n, middle_sums[n])
    result.send_far_sib()
    weight_grad(r, r.AT, r.GM, OUT0, 256)
    reduce_send(me, r, 1)
    attended_grad(me, r)
    result.cross()
    result.send_near_sib()
    sums_at(me, r, "attended")
    attention_grad(me, r, lambda n: sums_at(me, r, "rows%d" % n))
    projection_grad(me, r)
    reduce_send(me, r, 0)
    last = input_grad(me, r, input_sums)
    sums_at(me, r, "weights")
    result.end()
    last.begin()
    sums_at(me, r, "last")
    hidden_sums(me, r)
    projection_sums(me, r)
    vectors_send(me, r, True)
    last.end(lambda n: sums_at(me, r, "last%d" % n))
    for n in range(2):
        put_vec(r, 0, 8 * n, input_sums[n])
    vectors_send(me, r, False)
    sums_at(me, r, "end")
    vectors_sum(me, r)
    reduce_last(me, r)
    vectors_end(me, r)
    norms_send(me, r)
    units_send(me, r)
    norms_sum(me, r)
    units_end(me, r)
    norms_end(me, r)
    reduce_drain(me, r)


DMA = pltpu.SemaphoreType.DMA
VMEM = pltpu.VMEM
SCRATCH = dict(
    F=VMEM((12288, 256), BF),
    G=VMEM((12288, 256), BF),
    XV=VMEM((8, 32, 128), F32),
    PA=VMEM((1024, 1024), BF),
    CA=VMEM((1024, 1024), BF),
    E=VMEM((4096, 128), F32),
    S=VMEM((1536, 256), BF),
    VS=VMEM((32, 128), F32),
    VQ=VMEM((4, 32, 128), F32),
    VG=VMEM((8, 32, 128), F32),
    VX=VMEM((8, 32, 128), F32),
    VT=VMEM((4, 32, 128), F32),
    NB=VMEM((1, 24, 128), F32),
    NM=VMEM((16, 128), F32),
    NR=VMEM((8, 16, 128), F32),
    NQ=VMEM((4, 16, 128), F32),
    tail=VMEM((24, 128), F32),
    hp=VMEM((24, 128), F32),
    hn=VMEM((24, 128), F32),
    hp2=VMEM((24, 128), F32),
    hn2=VMEM((24, 128), F32),
    XR=VMEM((4, 1536, 256), BF),
    ZR=VMEM((5, 1536, 256), BF),
    QKV=VMEM((3, 1024, 256), BF),
    P=VMEM((4, 1024, 1024), BF),
    AT=VMEM((1024, 256), BF),
    RL=VMEM((1024, 256), F32),
    PB=VMEM((1024, 1024), BF),
    RB=VMEM((5, 256, 1024), BF),
    MID=VMEM((256, 1024), F32),
    GMID=VMEM((256, 1024), F32),
    NT=VMEM((1024, 1024), BF),
    GM=VMEM((1024, 1024), BF),
    AC=VMEM((1024, 1024), BF),
    GP=VMEM((1024, 1024), BF),
    GH=VMEM((1024, 1024), BF),
    hsem=DMA((4,)), pas=DMA((3,)), par_in=DMA((3,)), cas=DMA((3,)), car=DMA((3,)), qsem=DMA((24,)), csem=DMA((3,)), vsem=DMA((2,)), vxs=DMA, vxr=DMA((8,)),
    xs=DMA, xr=DMA((48,)), ats=DMA((12,)), atr=DMA((12,)), wos=DMA((6,)), wor=DMA((6,)), zsu=DMA((4,)), zsd=DMA((4,)), zr=DMA((48,)),
    s2s=DMA((18,)), s2r=DMA((18,)),
    s3s=DMA((18,)), s3r=DMA((18,)), s4s=DMA((18,)), s4r=DMA((18,)),
    hsem2=DMA((4,)), rxs=DMA, rxr=DMA((48,)), rzs=DMA((4,)), rzr=DMA((60,)),
    wxs=DMA((8,)), wxr=DMA((8,)), wqs=DMA, wqr=DMA((4,)),
    qsem2=DMA((96,)), csem2=DMA, nsem=DMA, nrsem=DMA((8,)), nqs=DMA, nqr=DMA((4,)),
)


class Refs:
    pass


def fast_layer(lens, pat, cot, par):
    outs = dict(
        act=((256, 1024), BF), ing=((256, 1024), BF), grad=((3075, 128), F32), norms=((16, 128), F32)
    )
    names = ["lens", "pat", "cot", "par"] + list(outs) + list(SCRATCH)

    def kernel(*refs):
        r = Refs()
        for name, ref in zip(names, refs):
            setattr(r, name, ref)
        whole_layer(Place(), r)

    whole = pl.BlockSpec(memory_space=pltpu.VMEM)
    return pl.pallas_call(
        kernel,
        out_shape=[jax.ShapeDtypeStruct(*o) for o in outs.values()],
        in_specs=[pl.BlockSpec(memory_space=pltpu.SMEM)] + [whole] * 3,
        out_specs=[whole] * len(outs),
        scratch_shapes=list(SCRATCH.values()),
        compiler_params=pltpu.CompilerParams(collective_id=0, has_side_effects=True, vmem_limit_bytes=VMEM_LIMIT),
    )(lens, pat, cot, par)


VMEM_LIMIT = 63 * 2**20
PLAIN_UNITS = ((0, 16), (24592, 24608), (32800, 32824), (65592, 65624), (98392, 98400))


def fast_shards(pat, cot, lens, params, m, v):
    def units(a):
        return a.reshape(-1, LANE)

    par = units(params)
    act, ing, grad, nb = fast_layer(lens[0], pat[0], cot[0], par)
    norms = nb[0, :GROUPS]
    clip = 1.0 / jnp.maximum(jnp.sqrt(jnp.sum(norms)), 1.0)
    start = lax.axis_index(("dp", "blk")) * par.shape[0]
    unit = start + lax.broadcasted_iota(jnp.int32, par.shape, 0)
    plain = jnp.zeros(par.shape, jnp.bool_)
    for lo, hi in PLAIN_UNITS:
        plain = plain | ((unit >= lo) & (unit < hi))
    scaled = clip * grad
    first = 0.9 * units(m) + 0.1 * scaled
    second = 0.999 * units(v) + 0.001 * scaled * scaled
    direction = first / (1.0 - 0.9**10) / (jnp.sqrt(second / (1.0 - 0.999**10)) + 1e-08)
    step = -0.001 * 0.9**12 * (direction + jnp.where(plain, 0.0, 0.05 * par))
    return act[None], ing[None], norms, step.reshape(-1), first.reshape(-1), nb[8:16].reshape(-1)


def solution(mesh):
    act, flat = P("dp", "blk", None), P(("dp", "blk"))
    specs = dict(
        in_specs=(act, act, P("dp", None), flat, flat, flat), out_specs=(act, act, P(), flat, flat, P()), check_vma=False
    )

    def layer(patches, cotangent, image_lengths, params, first_moment, second_moment):
        fits = (dict(mesh.shape), patches.shape, params.shape) == (dict(dp=8, blk=4), (8, 1024, D), (RAW,))
        step = jax.shard_map(fast_shards if fits else shards, mesh=mesh, **specs)
        return step(patches, cotangent, image_lengths, params, first_moment, second_moment)

    return layer
```

```python
from functools import partial
import math

import jax
import jax.numpy as jnp
from jax import lax
from jax.experimental import pallas as pl
from jax.experimental.pallas import tpu as pltpu
from jax.sharding import PartitionSpec as P

D = 1024
FF = 4096
HEADS = 16
HEAD_DIM = 64
GROUPS = 12
RAW = 12595200


eps_norm = 1e-06
neg_big = -1e30


def starts_of(model_width, hidden):
    square = model_width * model_width
    mlp_start = 7 * model_width + 4 * square
    return [
        0,
        model_width,
        2 * model_width,
        2 * model_width + 3 * square,
        4 * model_width + 3 * square,
        4 * model_width + 4 * square,
        5 * model_width + 4 * square,
        6 * model_width + 4 * square,
        mlp_start,
        mlp_start + model_width * hidden,
        mlp_start + model_width * hidden + hidden,
        mlp_start + 2 * model_width * hidden + hidden,
        mlp_start + 2 * model_width * hidden + hidden + model_width,
    ]


def unpack(flat_params):
    marks = starts_of(D, FF)
    pieces = [flat_params[marks[member] : marks[member + 1]] for member in range(12)]
    return (
        pieces[0],
        pieces[1],
        pieces[2].reshape(D, 3 * D),
        pieces[3],
        pieces[4].reshape(D, D),
        pieces[5],
        pieces[6],
        pieces[7],
        pieces[8].reshape(D, FF),
        pieces[9],
        pieces[10].reshape(FF, D),
        pieces[11],
    )


def layer_norm(values, gains, offsets):
    average = jnp.mean(values, axis=-1, keepdims=True)
    centred = values - average
    spread = jnp.mean(centred * centred, axis=-1, keepdims=True)
    return centred * lax.rsqrt(spread + eps_norm) * gains + offsets


def segment_ids(lengths, row_ids):
    bounds = jnp.cumsum(lengths)
    return jnp.sum((row_ids[:, None] >= bounds[None, :]).astype(jnp.int32), axis=1)


def shards(patches, cotangent, image_lengths, params, first_moment, second_moment):
    local_rows = patches.shape[1]
    seq_len = local_rows * lax.axis_size("blk")
    scale_of = HEAD_DIM ** (-0.5)
    inputs = patches[0].astype(jnp.float32)
    lengths = image_lengths[0]
    query_ids = lax.axis_index("blk") * local_rows + jnp.arange(local_rows, dtype=jnp.int32)
    query_labels = segment_ids(lengths, query_ids)
    weights_low = lax.all_gather(params.astype(jnp.bfloat16), ("dp", "blk"), axis=0, tiled=True)
    (
        gain_one,
        shift_one,
        w_qkv,
        bias_qv,
        w_out,
        bias_out,
        gain_two,
        shift_two,
        w_up,
        bias_up,
        w_down,
        bias_down,
    ) = unpack(weights_low)
    normed_one, pull_one = jax.vjp(
        layer_norm, inputs, gain_one.astype(jnp.float32), shift_one.astype(jnp.float32)
    )
    normed_low = normed_one.astype(jnp.bfloat16)
    bias_all = jnp.concatenate(
        [
            bias_qv[:D].astype(jnp.float32),
            jnp.zeros((D,), jnp.float32),
            bias_qv[D:].astype(jnp.float32),
        ]
    )
    projected = (jnp.dot(normed_low, w_qkv, preferred_element_type=jnp.float32) + bias_all).astype(
        jnp.bfloat16
    )
    queries = projected[:, :D].reshape(local_rows, HEADS, HEAD_DIM)
    key_value = projected[:, D:]

    def attend_block(state, block, block_labels):
        allowed = query_labels[:, None] == block_labels[None, :]
        best_in, total_in, summed_in = state
        raw = jnp.einsum("qhd,khd->hqk", queries, block[:, 0], preferred_element_type=jnp.float32)
        scores = jnp.where(allowed[None], raw * scale_of, neg_big)
        new_best = jnp.maximum(best_in, jnp.max(scores, axis=-1))
        factor = jnp.exp(best_in - new_best)
        weights = jnp.where(allowed[None], jnp.exp(scores - new_best[..., None]), 0.0)
        new_total = total_in * factor + jnp.sum(weights, axis=-1)
        added = jnp.einsum(
            "hqk,khd->qhd",
            weights.astype(jnp.bfloat16),
            block[:, 1],
            preferred_element_type=jnp.float32,
        )
        return (new_best, new_total, summed_in * factor.T[..., None] + added)

    start_state = (
        jnp.full((HEADS, local_rows), neg_big, jnp.float32),
        jnp.zeros((HEADS, local_rows), jnp.float32),
        jnp.zeros((local_rows, HEADS, HEAD_DIM), jnp.float32),
    )
    carry = start_state
    piece = lax.all_gather(key_value, "blk", axis=0, tiled=True)
    count = piece.shape[0]
    size = math.gcd(count, 512)
    blocks = piece.reshape(count // size, size, 2, HEADS, HEAD_DIM)
    labels = segment_ids(lengths, jnp.arange(count, dtype=jnp.int32)).reshape(count // size, size)

    def one_block(state, members):
        return (attend_block(state, members[0], members[1]), None)

    carry, ignored = lax.scan(one_block, carry, (blocks, labels))
    best, total, summed = carry
    attended = summed / total.T[..., None]
    log_total = best + jnp.log(total)
    attended_low = attended.reshape(local_rows, D).astype(jnp.bfloat16)
    branch = jnp.dot(attended_low, w_out, preferred_element_type=jnp.float32) + bias_out.astype(
        jnp.float32
    )
    middle = inputs + branch
    normed_two, pull_two = jax.vjp(
        layer_norm, middle, gain_two.astype(jnp.float32), shift_two.astype(jnp.float32)
    )
    normed_two_low = normed_two.astype(jnp.bfloat16)
    hidden_pre = jnp.dot(normed_two_low, w_up, preferred_element_type=jnp.float32) + bias_up.astype(
        jnp.float32
    )
    activated, pull_gelu = jax.vjp(partial(jax.nn.gelu, approximate=False), hidden_pre)
    activated_low = activated.astype(jnp.bfloat16)
    result = middle + (
        jnp.dot(activated_low, w_down, preferred_element_type=jnp.float32)
        + bias_down.astype(jnp.float32)
    )
    grad_out = cotangent[0]
    grad_down = jnp.dot(activated_low.T, grad_out, preferred_element_type=jnp.float32)
    grad_bias_down = jnp.sum(grad_out.astype(jnp.float32), axis=0)
    grad_act = jnp.dot(grad_out, w_down.T, preferred_element_type=jnp.float32)
    grad_hidden_low = pull_gelu(grad_act)[0].astype(jnp.bfloat16)
    grad_up = jnp.dot(normed_two_low.T, grad_hidden_low, preferred_element_type=jnp.float32)
    grad_bias_up = jnp.sum(grad_hidden_low.astype(jnp.float32), axis=0)
    grad_normed_two = jnp.dot(grad_hidden_low, w_up.T, preferred_element_type=jnp.float32)
    grad_mid_norm, grad_gain_two, grad_shift_two = pull_two(grad_normed_two)
    grad_middle = grad_out.astype(jnp.float32) + grad_mid_norm
    grad_middle_low = grad_middle.astype(jnp.bfloat16)
    grad_w_out = jnp.dot(attended_low.T, grad_middle_low, preferred_element_type=jnp.float32)
    grad_bias_out = jnp.sum(grad_middle_low.astype(jnp.float32), axis=0)
    grad_attended = (
        jnp.dot(grad_middle_low, w_out.T, preferred_element_type=jnp.float32)
        .astype(jnp.bfloat16)
        .reshape(local_rows, HEADS, HEAD_DIM)
    )
    delta_rows = jnp.sum(grad_attended.astype(jnp.float32) * attended, axis=-1).T
    gathered = lax.all_gather(key_value, "blk", axis=0, tiled=True)
    size = math.gcd(seq_len, 512)
    key_blocks = gathered.reshape(seq_len // size, size, 2, HEADS, HEAD_DIM)
    key_labels = segment_ids(lengths, jnp.arange(seq_len, dtype=jnp.int32)).reshape(
        seq_len // size, size
    )

    def back_block(grad_query, members):
        block, block_labels = members
        allowed = query_labels[:, None] == block_labels[None, :]
        raw = jnp.einsum("qhd,khd->hqk", queries, block[:, 0], preferred_element_type=jnp.float32)
        scores = jnp.where(allowed[None], raw * scale_of, neg_big)
        probs = jnp.where(allowed[None], jnp.exp(scores - log_total[..., None]), 0.0)
        grad_probs = jnp.einsum(
            "qhd,khd->hqk", grad_attended, block[:, 1], preferred_element_type=jnp.float32
        )
        grad_raw = (probs * (grad_probs - delta_rows[..., None]) * scale_of).astype(jnp.bfloat16)
        new_grad = grad_query + jnp.einsum(
            "hqk,khd->qhd", grad_raw, block[:, 0], preferred_element_type=jnp.float32
        )
        grad_keys = jnp.einsum(
            "hqk,qhd->khd", grad_raw, queries, preferred_element_type=jnp.float32
        )
        grad_values = jnp.einsum(
            "hqk,qhd->khd",
            probs.astype(jnp.bfloat16),
            grad_attended,
            preferred_element_type=jnp.float32,
        )
        return (new_grad, jnp.stack([grad_keys, grad_values], axis=1))

    grad_query, grad_kv_blocks = lax.scan(
        back_block, jnp.zeros((local_rows, HEADS, HEAD_DIM), jnp.float32), (key_blocks, key_labels)
    )
    grad_kv = lax.psum_scatter(
        grad_kv_blocks.reshape(seq_len, 2 * D).astype(jnp.bfloat16),
        "blk",
        scatter_dimension=0,
        tiled=True,
    ).astype(jnp.float32)
    grad_projected = jnp.concatenate([grad_query.reshape(local_rows, D), grad_kv], axis=1).astype(
        jnp.bfloat16
    )
    grad_w_qkv = jnp.dot(normed_low.T, grad_projected, preferred_element_type=jnp.float32)
    grad_proj_rows = jnp.sum(grad_projected.astype(jnp.float32), axis=0)
    grad_bias_qv = jnp.concatenate([grad_proj_rows[:D], grad_proj_rows[2 * D :]])
    grad_normed_one = jnp.dot(grad_projected, w_qkv.T, preferred_element_type=jnp.float32)
    grad_in_norm, grad_gain_one, grad_shift_one = pull_one(grad_normed_one)
    grad_inputs = grad_middle + grad_in_norm
    shard_len = params.shape[0]
    total_params = shard_len * lax.axis_size(("dp", "blk"))
    flat_grad = jnp.concatenate(
        [
            grad_gain_one,
            grad_shift_one,
            grad_w_qkv.reshape(-1),
            grad_bias_qv,
            grad_w_out.reshape(-1),
            grad_bias_out,
            grad_gain_two,
            grad_shift_two,
            grad_up.reshape(-1),
            grad_bias_up,
            grad_down.reshape(-1),
            grad_bias_down,
            jnp.zeros((total_params - RAW,), jnp.float32),
        ]
    )
    shard_grad = lax.psum_scatter(
        lax.slice_in_dim(flat_grad, 0, lax.axis_size(("dp", "blk")) * shard_len, axis=0),
        ("dp", "blk"),
        scatter_dimension=0,
        tiled=True,
    )
    positions = lax.axis_index(("dp", "blk")) * shard_len + jnp.arange(shard_len, dtype=jnp.int32)
    marks = jnp.array(starts_of(D, FF), dtype=jnp.int32)
    group_of = jnp.sum((positions[:, None] >= marks[None, :]).astype(jnp.int32), axis=1) - 1
    squares = shard_grad * shard_grad
    partials = jnp.sum(
        jnp.where(
            group_of[None, :] == jnp.arange(GROUPS, dtype=jnp.int32)[:, None], squares[None, :], 0.0
        ),
        axis=1,
    )
    norms, bias_total = lax.psum((partials, grad_bias_down), ("dp", "blk"))
    clip_factor = 1.0 / jnp.maximum(jnp.sqrt(jnp.sum(norms)), 1.0)
    decayed = ((group_of == 2) | (group_of == 4) | (group_of == 8) | (group_of == 10)).astype(
        jnp.float32
    )
    scaled = clip_factor * shard_grad
    new_first = 0.9 * first_moment + 0.1 * scaled
    new_second = 0.999 * second_moment + 0.001 * scaled * scaled
    direction = new_first / (1.0 - 0.9**10) / (jnp.sqrt(new_second / (1.0 - 0.999**10)) + 1e-08)
    param_step = -0.001 * 0.9**12 * (direction + 0.05 * decayed * params)
    return (
        result.astype(jnp.bfloat16)[None],
        grad_inputs.astype(jnp.bfloat16)[None],
        norms,
        param_step,
        new_first,
        bias_total,
    )


MESH = pl.DeviceIdType.MESH
LANE = 128


def pick(cond, yes, no):
    return jnp.where(cond, jnp.int32(yes), jnp.int32(no))


def rdma(src, dst, ssem, rsem, dev):
    return pltpu.make_async_remote_copy(src_ref=src, dst_ref=dst, send_sem=ssem, recv_sem=rsem, device_id=dev, device_id_type=MESH)


def rows(ref, start, size, step=128):
    return ref.at[pl.ds(pl.multiple_of(start, step), size)]


def gate(peers):
    sem = pltpu.get_barrier_semaphore()
    for peer in peers:
        pl.semaphore_signal(sem, inc=1, device_id=peer, device_id_type=MESH)
    pl.semaphore_wait(sem, len(peers))


class Place:
    def __init__(self):
        self.dp = lax.axis_index("dp")
        self.blk = lax.axis_index("blk")
        self.d = self.dp * 4 + self.blk
        self.z = self.dp // 2
        self.x = self.dp % 2
        self.y = self.blk // 2
        self.c = self.blk % 2
        self.xpeer = (self.z * 2 + 1 - self.x, self.blk)
        self.zs = [lax.rem(self.z + k, 4) for k in (1, 3, 2)]
        self.zpeers = [(zz * 2 + self.x, self.blk) for zz in self.zs]
        self.quad = [(self.dp, lax.rem(self.blk + k, 4)) for k in (1, 2, 3)]
        up = lax.rem(self.d + 1, 32)
        down = lax.rem(self.d + 31, 32)
        self.above = (self.dp + 2, self.blk)
        self.below = (self.dp - 2, self.blk)
        self.others = self.zpeers + [(zz * 2 + 1 - self.x, self.blk) for zz in self.zs]
        self.near = ((self.dp, self.y * 2 + 1 - self.c), (self.dp, (1 - self.y) * 2 + self.c))
        self.far = (1 - self.y) * 2 + self.c
        self.next = (up // 4, up % 4)
        self.prev = (down // 4, down % 4)
        d = self.d
        self.is_qkv = d < 8
        self.is_out = (d == 8) | (d == 9)
        self.is_mix_out = d == 10
        self.is_up = (d >= 11) & (d < 21)
        self.is_mix_down = d == 21
        self.is_down = d >= 22
        self.is_seg = self.is_out | self.is_down
        self.is_mix = self.is_mix_out | self.is_mix_down
        self.base = pick(d < 8, 16, pick(d < 11, 32, pick(d < 21, 56, 88))) - 3 * d
        self.seg0 = pick(d < 11, 3 * (d - 8), jnp.maximum(3 * (d - 21) - 1, 0))
        self.mix_up = pick(self.is_mix_out, 2074, -7)
        self.mix_seg = pick(self.is_mix_out, 2, 1049)

    def seg_home(self, n):
        seg = self.seg0 + n // 4
        panel = n % 4
        out_row = 3072 + 256 * panel + 128 * (seg % 2)
        down_row = 8192 + 1024 * panel + 128 * (seg // 4)
        low = self.d < 11
        return pick(low, seg // 2, seg % 4), pick(low, out_row, down_row)

    def block_home(self, n):
        part, row = self.seg_home(n)
        return pick(self.is_qkv, n % 4, part), pick(self.is_qkv, (n // 4) * 1024 + 128 * self.d, row)

    def up_home(self, n):
        start = pick(self.is_up, 32 + 96 * (self.d - 11), pick(self.is_mix_out, 0, 992))
        return n // 4, 4096 + 1024 * (n % 4) + start


def chunk_row(q, k):
    first = (k // 4) * 1024 + 512 * q + 128 * (k % 4)
    turn = 3 * (q - 2) + k // 4
    panel = k % 4
    other = pick(
        turn < 2,
        3072 + 256 * panel + 128 * turn,
        pick(turn < 10, 4096 + 1024 * panel + 128 * (turn - 2), 8192 + 1024 * panel + 128 * (turn - 10)),
    )
    return pick(q < 2, first, other)


def loop(count, body):
    def step(i, carry):
        body(i)
        return carry

    lax.fori_loop(0, count, step, 0)


def unit_span(start, stride):
    return pl.ds(start, 16, stride=stride)


def for_tiles(me, visit):
    e0 = 24 + me.base

    @pl.when(me.is_qkv)
    def _():
        def body(rb):
            for ct in range(24):
                n = (ct // 8) * 4 + (ct % 8) // 2
                visit(e0 + 384 * rb + ct, 24, n * 128 + 16 * rb, 128 * (ct % 2))

        loop(8, body)

    @pl.when(me.is_up)
    def _():
        def body(rb):
            for ct in range(32):
                n = (ct % 4) * 4 + ct // 8
                visit(e0 + 512 * rb + ct, 32, n * 96 + 16 * rb, 128 * ((ct // 4) % 2))

        loop(6, body)

    def segs(count, first):
        def body(i):
            for ct in range(8):
                visit(first + 128 * i + ct, 8, ((i // 8) * 4 + ct // 2) * 128 + 16 * (i % 8), 128 * (ct % 2))

        loop(count, body)

    @pl.when(me.is_seg)
    def _():
        segs(24, e0)

    @pl.when(me.is_mix)
    def _():
        segs(16, 24 + me.mix_seg)

        def body(rb):
            for ct in range(32):
                n = (ct % 4) * 4 + ct // 8
                visit(24 + me.mix_up + 512 * rb + ct, 32, 1024 + n * 32 + 16 * rb, 128 * ((ct // 4) % 2))

        loop(2, body)


def for_pieces(me, visit):
    @pl.when(me.is_qkv | me.is_seg)
    def _():
        def body(n):
            part, row = me.block_home(n)
            visit(n, n * 128, 128, part, row, 128)

        loop(12, body)

    @pl.when(me.is_up)
    def _():
        def body(n):
            part, row = me.up_home(n)
            visit(n, n * 96, 96, part, row, 32)

        loop(16, body)

    @pl.when(me.is_mix)
    def _():
        def body(n):
            part, row = me.seg_home(n)
            visit(n, n * 128, 128, part, row, 128)

        loop(8, body)

        def body_up(n):
            part, row = me.up_home(n)
            visit(8 + n, 1024 + n * 32, 32, part, row, 32)

        loop(16, body_up)


def vec_spots(me, visit):
    for cond, row, unit, count in (
        (me.d == 0, 0, 0, 16),
        (me.d == 7, 0, 3067, 8),
        (me.d == 8, 0, 0, 8),
        (me.d == 10, 8, 2050, 24),
        (me.d == 21, 0, 1017, 32),
        (me.d == 31, 0, 3067, 8),
    ):

        @pl.when(cond)
        def _(row=row, unit=unit, count=count):
            visit(row, 24 + unit, count)


BF, F32 = jnp.bfloat16, jnp.float32
EPS = 1e-06
OUT0, UP0, DOWN0 = 3072, 4096, 8192


def dot(a, b):
    return lax.dot_general(a, b, (((1,), (0,)), ((), ())), preferred_element_type=F32)


def dot_nt(a, b):
    return lax.dot_general(a, b, (((1,), (1,)), ((), ())), preferred_element_type=F32)


def dot_tn(a, b):
    return lax.dot_general(a, b, (((0,), (0,)), ((), ())), preferred_element_type=F32)


def block_of(i):
    return pl.ds(pl.multiple_of(i * 256, 256), 256)


def wide(r, q, first, count=8):
    return jnp.concatenate([r.XV[q, first + i : first + i + 1, :] for i in range(count)], axis=1)


def narrow(r, q, first):
    return jnp.concatenate([r.XV[q, pl.ds(first + i, 1), :] for i in range(2)], axis=1)


def put_vec(r, q, first, row, add=False):
    for i in range(row.shape[1] // 128):
        part = row[:, i * 128 : i * 128 + 128]
        if add:
            part = part + r.VG[q, first + i : first + i + 1, :]
        r.VG[q, first + i : first + i + 1, :] = part


def normalize(x):
    mean = jnp.mean(x, axis=-1, keepdims=True)
    cen = x - mean
    var = jnp.mean(cen * cen, axis=-1, keepdims=True)
    scale = lax.rsqrt(var + EPS)
    return cen * scale, scale


def norm_back(dy, xhat, scale, gain):
    t = dy * gain
    return scale * (t - jnp.mean(t, axis=-1, keepdims=True) - xhat * jnp.mean(t * xhat, axis=-1, keepdims=True))


def labels_at(r, at):
    total = jnp.zeros_like(at)
    bound = 0
    for k in range(9):
        bound = bound + r.lens[k]
        total = total + (at >= bound).astype(jnp.int32)
    return total


def lane_mask(h, value=1.0):
    lane = lax.broadcasted_iota(jnp.int32, (1, 128), 1)
    return jnp.where((lane // 64) == h, value, 0.0).astype(BF)


def crow(q, k):
    return pick(q < 2, 128 * k, 384 * (k % 4) + 128 * (k // 4))


class Other(Place):
    def __init__(self, me, i):
        d = me.dp * 4 + i
        self.d, self.blk, self.dp = d, i, me.dp
        self.is_qkv = d < 8
        self.is_out = (d == 8) | (d == 9)
        self.is_mix_out = d == 10
        self.is_up = (d >= 11) & (d < 21)
        self.is_mix_down = d == 21
        self.is_down = d >= 22
        self.is_seg = self.is_out | self.is_down
        self.is_mix = self.is_mix_out | self.is_mix_down
        self.seg0 = pick(d < 11, 3 * (d - 8), jnp.maximum(3 * (d - 21) - 1, 0))

    def seg_spot(self, n):
        seg = self.seg0 + n // 4
        low = self.d < 11
        turn = pick(low, seg % 2, 10 + seg // 4 - 3 * (self.dp - 2))
        return pick(low, seg // 2, seg % 4), 384 * (n % 4) + 128 * turn

    def block_spot(self, n):
        part, row = self.seg_spot(n)
        return pick(self.is_qkv, n % 4, part), pick(self.is_qkv, (n // 4) * 512 + 128 * (self.d % 4), row)

    def up_spot(self, n):
        start = pick(self.is_up, 32 + 96 * (self.d - 11), pick(self.is_mix_out, 0, 992))
        return n // 4, 384 * (n % 4) + 256 + start - 384 * (self.dp - 2)

    def pieces(self, visit):
        @pl.when(self.is_qkv | self.is_seg)
        def _():
            loop(12, lambda n: visit(n, n * 128, 128, *self.block_spot(n)))

        @pl.when(self.is_up)
        def _():
            loop(16, lambda n: visit(n, n * 96, 96, *self.up_spot(n)))

        @pl.when(self.is_mix)
        def _():
            loop(8, lambda n: visit(n, n * 128, 128, *self.seg_spot(n)))
            loop(16, lambda n: visit(8 + n, 1024 + n * 32, 32, *self.up_spot(n)))


def arrived(ref, sem):
    pltpu.make_async_copy(ref, ref, sem).wait()


def squares(x):
    s = jnp.sum(x * x, axis=0, keepdims=True)
    return s[:, :128] + s[:, 128:] if x.shape[1] == 256 else s


def by_z(me, values):
    out = jnp.int32(values[0])
    for n in (1, 2, 3):
        out = pick(me.z == n, values[n], out)
    return out


def span(zz, *groups):
    return tuple(zz * 6 + g for g in groups)


ALL = (0, 1, 2, 3, 4, 5)
def spots(*by_depth):
    most = max(len(groups) for groups in by_depth)
    return tuple(zip(*(groups + (24,) * (most - len(groups)) for groups in by_depth)))


NONE = ()
GATHER = dict(
    first=spots(span(0, 0, 1), span(1, 0, 1), span(2, 0, 1), span(3, 0, 1)),
    second=spots(span(0, 2, 3), span(0, 0, 1), span(2, 2, 3), span(3, 2, 3)),
    third=spots(span(0, 4, 5) + span(1, 0), span(0, 2, 3, 4), span(0, 0, 1, 2), span(3, 4, 5) + span(0, 0)),
    fourth=spots(span(1, 1), NONE, NONE, span(0, 1)),
    fifth=spots(span(1, 2, 3), span(0, 5), span(0, 3, 4), span(0, 2, 3)),
    sixth=spots(span(1, 4, 5), span(1, 2, 3), span(0, 5) + span(1, 0), span(0, 4, 5)),
    rows0=spots(NONE, span(1, 4, 5), span(1, 1) + span(3, 0), span(2, 0)),
    rows1=spots(NONE, span(2, 0, 1), span(1, 2) + span(3, 1), span(1, 0) + span(2, 1)),
    rows2=spots(span(2, 0), span(2, 2, 3), span(1, 3) + span(3, 2), span(1, 1) + span(2, 2)),
    rows3=spots(span(2, 1, 2), span(2, 4, 5), span(1, 4, 5) + span(3, 3), span(1, 2, 3)),
    out0=spots(span(2, 3, 4), span(3, 0, 1), span(2, 4, 5) + span(3, 4), span(1, 4, 5) + span(2, 3)),
    out1=spots(span(2, 5), span(3, 2, 3), span(3, 5), span(2, 4)),
    shared=spots(span(3, 0, 1, 2), span(3, 4, 5), NONE, span(2, 5)),
    normed=spots(span(3, 3, 4, 5), NONE, NONE, NONE),
)
SUMS = dict(
    start=spots(span(3, 0, 1, 2, 3), NONE, NONE, span(2, 0)),
    middle0=spots(span(3, 4), span(3, 0), NONE, NONE),
    middle1=spots(span(3, 5), span(3, 1, 2), span(3, 0), span(2, 1)),
    middle2=spots(span(2, 0), span(3, 3), span(3, 1), span(2, 2)),
    middle3=spots(span(2, 1, 2), span(3, 4, 5), span(3, 2, 3), span(2, 3)),
    attended=spots(span(2, 3, 4), span(2, 0, 1), span(3, 4, 5), span(2, 4, 5)),
    rows0=spots(span(2, 5), span(2, 2, 3), NONE, span(1, 0)),
    rows1=spots(span(1, 0), span(2, 4), NONE, span(1, 1)),
    rows2=spots(span(1, 1), NONE, span(1, 0), span(1, 2)),
    weights=spots(span(1, 2, 3), span(2, 5), span(1, 1, 2), span(1, 3, 4)),
    last=spots(span(1, 4, 5), NONE, span(1, 3), span(1, 5) + span(0, 0)),
    last0=spots(NONE, NONE, span(1, 4), span(0, 1)),
    last1=spots(NONE, NONE, span(1, 5) + span(0, 0), span(0, 2)),
    last2=spots(NONE, NONE, span(0, 1), span(0, 3)),
    last3=spots(NONE, span(0, 0), span(0, 2), span(0, 4)),
    end=spots(NONE, span(0, 1, 2, 3, 4, 5), span(0, 3, 4, 5), span(0, 5)),
)


def prepare(me, r):
    r.tail[...] = r.par[3051:3075, :]
    up = rdma(r.tail, r.hp, r.hsem.at[0], r.hsem.at[1], me.next)
    down = rdma(r.par.at[0:24], r.hn, r.hsem.at[2], r.hsem.at[3], me.prev)
    up.start()
    down.start()

    def put(i):
        r.E[pl.ds(pl.multiple_of(24 + 64 * i, 8), 64), :] = r.par[pl.ds(pl.multiple_of(64 * i, 8), 64), :]

    loop(48, put)
    r.E[3096:3099, :] = r.par[3072:3075, :]
    r.VS[...] = jnp.zeros_like(r.VS)

    def vec(row, unit, count):
        r.VS[row : row + count, :] = r.E[unit : unit + count, :].astype(BF).astype(F32)

    vec_spots(me, vec)
    vq = [rdma(r.VS, r.VQ.at[me.blk], r.vsem.at[0], r.vsem.at[1], peer) for peer in me.quad]
    for v in vq:
        v.start()
    r.VQ[me.blk] = r.VS[...]
    up.wait()
    down.wait()
    r.E[0:24, :] = r.hp[...]
    r.E[3099:3123, :] = r.hn[...]

    def tile(unit, stride, row, lane):
        r.S[pl.ds(pl.multiple_of(row, 16), 16), lane : lane + 128] = r.E[unit_span(unit, stride), :].astype(BF)

    for_tiles(me, tile)

    def which(i):
        return pick(me.is_qkv, jnp.minimum(i // 4, 2), 0)

    def visit(i, srow, size, part, frow, step):
        src, dst = rows(r.S, srow, size, 32), rows(r.F, frow, size, step)

        @pl.when(part != me.blk)
        def _():
            rdma(src, dst, r.qsem.at[i], r.csem.at[which(i)], (me.dp, part)).start()

        @pl.when(part == me.blk)
        def _():
            pltpu.make_async_copy(src, dst, r.csem.at[which(i)]).start()

    for_pieces(me, visit)
    arrived(r.VQ.at[0:3], r.vsem.at[0])
    arrived(r.VQ.at[0:3], r.vsem.at[1])
    r.XV[me.dp] = r.VQ[0] + r.VQ[1] + r.VQ[2] + r.VQ[3]
    for peer in me.others + [me.xpeer]:
        rdma(r.XV.at[me.dp], r.XV.at[me.dp], r.vxs, r.vxr.at[me.dp], peer).start()


def chunk_here(me, r, panel):
    @pl.when(me.is_qkv)
    def _():
        arrived(r.F.at[0:512], r.csem.at[panel])

    if panel == 0:

        @pl.when(jnp.logical_not(me.is_qkv))
        def _():
            arrived(r.F.at[0:1536], r.csem.at[0])


def prepare_drain(me, r):
    def visit(i, srow, size, part, frow, step):
        @pl.when(part != me.blk)
        def _():
            arrived(rows(r.S, srow, size, 32), r.qsem.at[i])

    for_pieces(me, visit)
    arrived(r.XV.at[0:7], r.vxs)


def own_down(me, r):
    @pl.when(me.z > 0)
    def _():
        def body(k):
            ref = rows(r.F, chunk_row(me.dp, k), 128)
            rdma(ref, ref, r.zsd.at[me.z], r.zr.at[me.z * 12 + k], me.below).start()

        loop(12, body)


def gather_step(me, r, groups):
    e = by_z(me, groups)
    if 24 in groups:

        @pl.when(e < 24)
        def _():
            gather_group(me, r, e)

    else:
        gather_group(me, r, e)


def gather_group(me, r, e):
    zz, g = e // 6, e % 6
    for i in range(2):
        n = 2 * e + i

        @pl.when(zz != me.z)
        def _(n=n):
            arrived(r.F.at[0:128], r.zr.at[n])

        ref = rows(r.F, chunk_row(zz * 2 + me.x, g * 2 + i), 128)

        @pl.when((zz <= me.z) & (me.z < 3))
        def _(n=n, ref=ref):
            rdma(ref, ref, r.zsu.at[zz], r.zr.at[n], me.above).start()

        @pl.when((zz > me.z) & (me.z > 0))
        def _(n=n, ref=ref):
            rdma(ref, ref, r.zsd.at[zz], r.zr.at[n], me.below).start()

        rdma(ref, ref, r.xs, r.xr.at[n], me.xpeer).start()


def gather_at(me, r, place):
    for groups in GATHER[place]:
        gather_step(me, r, groups)


def gathered(me, r, zz, groups=ALL):
    for g in groups:
        for i in range(2):
            arrived(r.F.at[0:128], r.xr.at[zz * 12 + 2 * g + i])


def gather_drain(me, r):
    arrived(r.F.at[0:6144], r.xs)
    for zz in range(4):
        @pl.when((zz <= me.z) & (me.z < 3))
        def _():
            arrived(r.F.at[0:1536], r.zsu.at[zz])

        @pl.when((zz >= me.z) & (me.z > 0))
        def _():
            arrived(r.F.at[0:1536], r.zsd.at[zz])


def swap_send(me, r, src, dst, ssem, rsem):
    mine = block_of(me.blk)
    for n, peer in enumerate(me.near):
        rdma(src, dst.at[mine], ssem.at[n], rsem.at[n], peer).start()
    dst[mine, :] = src[...]


def swap_pass(me, r, dst, ssem, rsem):
    far = dst.at[block_of((1 - me.y) * 2 + me.c)]
    arrived(far, rsem.at[1])
    rdma(far, far, ssem.at[2], rsem.at[2], me.near[0]).start()


def swap_drain(me, r, dst, ssem):
    for n in range(3):
        arrived(dst.at[0:256], ssem.at[n])


def nothing(n):
    pass


class QuadSum:
    def __init__(self, me, r, term, make, sems, finish, slot, out=None):
        self.me, self.r, self.term, self.make, self.finish, self.slot, self.out = me, r, term, make, finish, slot, out
        self.ssem, self.rsem = sems
        y, c = me.y, me.c
        self.far_sib, self.far, self.near_sib, self.own = (1 - y) * 2 + 1 - c, (1 - y) * 2 + c, y * 2 + 1 - c, me.blk
        self.sib, self.yp = me.near
        self.over = []

    def copy(self, src, dst, n, dev):
        return rdma(src, dst, self.ssem.at[n], self.rsem.at[n], dev)

    def at(self, dev, i):
        return pl.ds(pl.multiple_of(dev * 256 + 64 * i, 64), 64)

    def send_far_sib(self):
        self.a = self.copy(self.term.at[block_of(self.far_sib)], self.r.RB.at[0], 0, self.sib)
        self.a.start()

    def send_near_sib(self):
        self.d = self.copy(self.term.at[block_of(self.near_sib)], self.r.RB.at[1], 1, self.sib)
        self.d.start()

    def cross(self):
        r = self.r
        self.a.wait_recv()
        for i in range(4):
            lo = pl.ds(64 * i, 64)
            r.RB[3, lo, :] = (self.term[self.at(self.far, i), :].astype(F32) + r.RB[0, lo, :].astype(F32)).astype(BF)
            self.over.append(self.copy(r.RB.at[3, lo], r.RB.at[self.slot, lo], 2 + i, self.yp))
            self.over[i].start()

    def begin(self):
        self.make(self.far_sib)
        self.send_far_sib()
        self.make(self.far)
        self.cross()
        self.make(self.near_sib)
        self.send_near_sib()
        self.make(self.own)

    def end(self, idle=nothing):
        r = self.r
        self.d.wait_recv()
        out, near, on = [], [], []
        for i in range(4):
            self.over[i].wait_recv()
            lo = slice(64 * i, 64 * i + 64)
            total = self.term[self.at(self.own, i), :].astype(F32) + r.RB[1, lo, :].astype(F32)
            self.finish(lo, total + r.RB[self.slot, lo, :].astype(F32))
            if self.out is not None:
                part, passed = self.out.at[self.at(self.own, i)], self.out.at[self.at(self.far, i)]
                out.append(self.copy(part, part, 6 + i, self.yp))
                near.append(self.copy(part, part, 10 + i, self.sib))
                on.append(self.copy(passed, passed, 14 + i, self.sib))
                out[i].start()
                near[i].start()
            idle(i)
        for i in range(len(out)):
            out[i].wait_recv()
            on[i].start()
        for cp in near + on:
            cp.wait()
        for cp in [self.a, self.d] + self.over + out:
            cp.wait_send()


def first_norm(me, r, half):
    gain, shift = wide(r, 0, 0), wide(r, 0, 8)

    def ln(i):
        at = pl.ds(pl.multiple_of(half * 512 + i * 64, 64), 64)
        x = r.PA[at, :]
        for p in range(4):
            row = pl.multiple_of(PATCH0 + 1024 * p + half * 512 + i * 64, 64)
            r.G[pl.ds(row, 64), :] = x[:, 256 * p : 256 * p + 256]
        xhat, _ = normalize(x.astype(F32))
        r.PA[at, :] = (xhat * gain + shift).astype(BF)

    loop(8, ln)


def attention(me, r, idle):
    bias = [narrow(r, 1, 2 * me.blk), None, narrow(r, 2, 2 * me.blk)]

    def proj(i):
        at = block_of(i)
        for j in range(3):
            out = dot(r.PA[at, :], r.F[j * 1024 : j * 1024 + 1024, :])
            if bias[j] is not None:
                out = out + bias[j]
            r.QKV[j, at, :] = out.astype(BF)

    loop(4, proj)
    key_labels = labels_at(r, lax.broadcasted_iota(jnp.int32, (1, 1024), 1))

    def attend(i):
        at = block_of(i)
        row_labels = labels_at(r, lax.broadcasted_iota(jnp.int32, (256, 1), 0) + i * 256)
        allowed = row_labels == key_labels
        for t in range(2):
            lanes = slice(128 * t, 128 * t + 128)
            q = r.QKV[0, at, lanes]
            k = r.QKV[1, :, lanes]
            v = r.QKV[2, :, lanes]
            out = jnp.zeros((256, 128), F32)
            inverse = []
            for h in range(2):
                s = jnp.where(allowed, dot_nt(q * lane_mask(h, 0.125), k), -1e30)
                w = jnp.exp(s - jnp.max(s, axis=-1, keepdims=True))
                inverse.append(1.0 / jnp.sum(w, axis=-1, keepdims=True))
                p = w.astype(BF)
                r.P[2 * t + h, at, :] = p
                out = out + dot(p, v * lane_mask(h))
            low_lanes = lax.broadcasted_iota(jnp.int32, (256, 128), 1) < 64
            scale = jnp.where(low_lanes, inverse[0], inverse[1])
            r.RL[at, lanes] = scale
            r.AT[at, lanes] = (out * scale).astype(BF)

    for i in range(4):
        attend(i)
        attended_send(me, r, i)
        if i > 0:
            attended_pass(me, r, i - 1)
        idle(i)


ATTENDED0, WHOLE_OUT0, PATCH0 = 0, 4096, 8192


def attended_send(me, r, i):
    dst = rows(r.G, ATTENDED0 + 1024 * me.blk + 256 * i, 256)
    for n in range(2):
        rdma(r.AT.at[256 * i : 256 * i + 256], dst, r.ats.at[2 * i + n], r.atr.at[2 * i + n], me.near[n]).start()


def attended_pass(me, r, i):
    ref = rows(r.G, ATTENDED0 + 1024 * me.far + 256 * i, 256)
    arrived(ref, r.atr.at[2 * i + 1])
    rdma(ref, ref, r.ats.at[8 + i], r.atr.at[8 + i], me.near[0]).start()


def out_send(me, r, half):
    @pl.when(me.x == 1)
    def _():
        gathered(me, r, 1, (0, 1) if half == 0 else (2, 3))

    for p in range(4):
        at = 256 * p + 128 * half
        src, dst = r.F.at[OUT0 + at : OUT0 + at + 128], rows(r.G, WHOLE_OUT0 + 1024 * me.blk + at, 128)
        for n in range(2):
            rdma(src, dst, r.wos.at[2 * half + n], r.wor.at[2 * half + n], me.near[n]).start()


def out_pass(me, r, half):
    arrived(r.G.at[0:512], r.wor.at[2 * half + 1])
    for p in range(4):
        ref = rows(r.G, WHOLE_OUT0 + 1024 * me.far + 256 * p + 128 * half, 128)
        rdma(ref, ref, r.wos.at[4 + half], r.wor.at[4 + half], me.near[0]).start()


def shared_here(me, r):
    for i in range(4):
        arrived(r.G.at[0:256], r.atr.at[2 * i])
        arrived(r.G.at[0:256], r.atr.at[8 + i])
    for half in range(2):
        arrived(r.G.at[0:512], r.wor.at[2 * half])
        arrived(r.G.at[0:512], r.wor.at[4 + half])
    for i in range(12):
        arrived(r.G.at[0:256], r.ats.at[i])
    for i in range(6):
        arrived(r.G.at[0:512], r.wos.at[i])
    r.G[pl.ds(pl.multiple_of(ATTENDED0 + 1024 * me.blk, 1024), 1024), :] = r.AT[...]
    r.G[pl.ds(pl.multiple_of(WHOLE_OUT0 + 1024 * me.blk, 1024), 1024), :] = r.F[OUT0 : OUT0 + 1024, :]


def second_norm(me, r):
    bias_out = wide(r, 2, 8)
    gain, shift = wide(r, 2, 16), wide(r, 2, 24)

    def body(i):
        for p in range(4):
            lanes = slice(256 * p, 256 * p + 256)
            acc = r.G[pl.ds(pl.multiple_of(PATCH0 + 1024 * p + 256 * i, 256), 256), :].astype(F32) + bias_out[:, lanes]
            for part in range(4):
                weights = r.G[WHOLE_OUT0 + 1024 * part + 256 * p : WHOLE_OUT0 + 1024 * part + 256 * p + 256, :]
                acc = acc + dot(r.G[pl.ds(pl.multiple_of(ATTENDED0 + 1024 * part + 256 * i, 256), 256), :], weights)
            r.GMID[:, lanes] = acc

        def ln(n):
            at = pl.ds(pl.multiple_of(n * 64, 64), 64)
            xhat, _ = normalize(r.GMID[at, :])
            r.NT[pl.ds(pl.multiple_of(i * 256 + n * 64, 64), 64), :] = (xhat * gain + shift).astype(BF)

        loop(4, ln)

        @pl.when(i == me.blk)
        def _():
            r.MID[...] = r.GMID[...]

    loop(4, body)


def hidden(me, r):
    biases = [jnp.concatenate([r.XV[5, pl.ds(4 * (2 * p + i) + me.blk, 1), :] for i in range(2)], axis=1) for p in range(4)]

    def up(i):
        at = pl.ds(pl.multiple_of(i * 128, 128), 128)
        for p in range(4):
            h = dot(r.NT[at, :], r.F[UP0 + 1024 * p : UP0 + 1024 * p + 1024, :]) + biases[p]
            phi = 0.5 + 0.5 * lax.erf(h * 0.7071067811865476)
            lanes = slice(256 * p, 256 * p + 256)
            r.AC[at, lanes] = (h * phi).astype(BF)
            r.GP[at, lanes] = (phi + h * (jnp.exp(-0.5 * h * h) * 0.3989422804014327)).astype(BF)

    loop(8, up)


def hidden_grad(me, r):
    def body(i):
        at = block_of(i)
        for p in range(4):
            lanes = slice(256 * p, 256 * p + 256)
            acc = jnp.zeros((256, 256), F32)
            for k in range(4):
                down = r.F[DOWN0 + 1024 * k + 256 * p : DOWN0 + 1024 * k + 256 * p + 256, :]
                acc = acc + dot_nt(r.CA[at, 256 * k : 256 * k + 256], down)
            r.GH[at, lanes] = (acc * r.GP[at, lanes].astype(F32)).astype(BF)

    loop(4, body)


def hidden_sums(me, r):
    for p in range(4):
        sums = jnp.sum(r.GH[:, 256 * p : 256 * p + 256].astype(F32), axis=0, keepdims=True)
        for i in range(2):
            r.VG[5, pl.ds(4 * (2 * p + i) + me.blk, 1), :] = sums[:, 128 * i : 128 * i + 128]
    put_vec(r, 7, 0, jnp.sum(r.cot[...].astype(F32), axis=0, keepdims=True))


def weight_grad(r, left, right, base, height):
    def body(i):
        cols = pl.ds(pl.multiple_of(i * 256, 256), 256)
        lt = left[:, cols].T
        for p in range(right.shape[1] // 256):
            out = dot(lt, right[:, 256 * p : 256 * p + 256])
            r.G[pl.ds(pl.multiple_of(base + p * height + i * 256, 256), 256), :] = out.astype(BF)

    loop(height // 256, body)


def middle_grad(me, r, sums):
    def term(i):
        at = block_of(i)
        for n in range(4):
            acc = jnp.zeros((256, 256), F32)
            for p in range(4):
                up = r.F[UP0 + 1024 * p + 256 * n : UP0 + 1024 * p + 256 * n + 256, :]
                acc = acc + dot_nt(r.GH[at, 256 * p : 256 * p + 256], up)
            r.PB[at, 256 * n : 256 * n + 256] = acc.astype(BF)

    gain = wide(r, 2, 16)
    sums[:] = [jnp.zeros((1, 1024), F32)] * 3

    def finish(lo, dy):
        xhat, scale = normalize(r.MID[lo, :])
        gm = r.cot[lo, :].astype(F32) + norm_back(dy, xhat, scale, gain)
        r.GMID[lo, :] = gm
        low = gm.astype(BF)
        r.GM[pl.ds(pl.multiple_of(me.blk * 256 + lo.start, 64), 64), :] = low
        for n, term_of in enumerate((low.astype(F32), dy * xhat, dy)):
            sums[n] = sums[n] + jnp.sum(term_of, axis=0, keepdims=True)

    return QuadSum(me, r, r.PB, term, (r.s2s, r.s2r), finish, 4, r.GM)


def attended_grad(me, r):
    def body(i):
        at = block_of(i)
        acc = jnp.zeros((256, 256), F32)
        for p in range(4):
            acc = acc + dot_nt(r.GM[at, 256 * p : 256 * p + 256], r.F[OUT0 + 256 * p : OUT0 + 256 * p + 256, :])
        r.GP[at, 768:1024] = acc.astype(BF)

    loop(4, body)


def attention_grad(me, r, idle):
    r.E[...] = jnp.zeros_like(r.E)

    def attend(i):
        at = block_of(i)
        for t in range(2):
            lanes = slice(128 * t, 128 * t + 128)
            q = r.QKV[0, at, lanes]
            k = r.QKV[1, :, lanes]
            v = r.QKV[2, :, lanes]
            da = (r.GP[at, 768 + 128 * t : 896 + 128 * t].astype(F32) * r.RL[at, lanes]).astype(BF)
            overlap = da.astype(F32) * r.AT[at, lanes].astype(F32)
            dq = jnp.zeros((256, 128), F32)
            for h in range(2):
                m, m8 = lane_mask(h), lane_mask(h, 0.125)
                p = r.P[2 * t + h, at, :]
                delta = jnp.sum(overlap * m.astype(F32), axis=-1, keepdims=True)
                ds = (p.astype(F32) * (dot_nt(da * m, v) - delta)).astype(BF)
                dq = dq + dot(ds, k * m8)
                r.E[1024 * t : 1024 * t + 1024, :] += dot_tn(ds, q * m8)
                r.E[2048 + 1024 * t : 3072 + 1024 * t, :] += dot_tn(p, da * m)
            r.GP[at, lanes] = dq.astype(BF)

    for i in range(4):
        attend(i)
        if i < 3:
            idle(i)
    for n in range(4):
        r.GP[:, 256 + 128 * n : 384 + 128 * n] = r.E[1024 * n : 1024 * n + 1024, :].astype(BF)


def projection_sums(me, r):
    for j, q in ((0, 1), (2, 2)):
        sums = jnp.sum(r.GP[:, 256 * j : 256 * j + 256].astype(F32), axis=0, keepdims=True)
        for i in range(2):
            r.VG[q, pl.ds(2 * me.blk + i, 1), :] = sums[:, 128 * i : 128 * i + 128]


def projection_grad(me, r):
    def body(i):
        cols = pl.ds(pl.multiple_of(i * 256, 256), 256)
        lt = r.PA[:, cols].T
        for j in range(3):
            r.G[pl.ds(pl.multiple_of(j * 1024 + i * 256, 256), 256), :] = dot(lt, r.GP[:, 256 * j : 256 * j + 256]).astype(BF)

    loop(4, body)


def input_grad(me, r, sums):
    def term(i):
        at = block_of(i)
        for n in range(4):
            acc = jnp.zeros((256, 256), F32)
            for j in range(3):
                acc = acc + dot_nt(r.GP[at, 256 * j : 256 * j + 256], r.F[1024 * j + 256 * n : 1024 * j + 256 * n + 256, :])
            r.PB[at, 256 * n : 256 * n + 256] = acc.astype(BF)

    gain = wide(r, 0, 0)
    sums[:] = [jnp.zeros((1, 1024), F32)] * 2

    def finish(lo, dy):
        xhat, scale = normalize(r.pat[lo, :].astype(F32))
        r.ing[lo, :] = (r.GMID[lo, :] + norm_back(dy, xhat, scale, gain)).astype(BF)
        for n, term_of in enumerate((dy * xhat, dy)):
            sums[n] = sums[n] + jnp.sum(term_of, axis=0, keepdims=True)

    return QuadSum(me, r, r.PB, term, (r.s4s, r.s4r), finish, 4)


def layer_out(me, r):
    def term(i):
        at = block_of(i)
        for p in range(4):
            r.CA[at, 256 * p : 256 * p + 256] = dot(r.AC[at, :], r.F[DOWN0 + 1024 * p : DOWN0 + 1024 * p + 1024, :]).astype(BF)

    bias_down = wide(r, 7, 0)

    def finish(lo, total):
        r.act[lo, :] = (r.MID[lo, :] + (total + bias_down)).astype(BF)

    return QuadSum(me, r, r.CA, term, (r.s3s, r.s3r), finish, 2)


def reduce_send(me, r, zz, first=0, count=12):
    q = zz * 2 + 1 - me.x

    def body(i):
        k = first + i
        rdma(rows(r.G, chunk_row(q, k), 128), rows(r.XR.at[zz], crow(q, k), 128), r.rxs, r.rxr.at[zz * 12 + k], me.xpeer).start()

    loop(count, body)


def reduce_step(me, r, groups):
    e = by_z(me, groups)

    @pl.when(e < 24)
    def _():
        zz, g = e // 6, e % 6
        q = zz * 2 + me.x
        down = zz < me.z

        def body(i):
            k = g * 2 + i
            n = zz * 12 + k
            arrived(r.G.at[0:128], r.rxr.at[n])

            @pl.when((me.z > 0) & (me.z < 3))
            def _():
                arrived(r.G.at[0:128], r.rzr.at[n])

            src, at = pl.ds(pl.multiple_of(chunk_row(q, k), 128), 128), pl.ds(pl.multiple_of(crow(q, k), 128), 128)
            total = r.G[src, :].astype(F32) + r.XR[zz, at, :].astype(F32) + r.ZR[zz, at, :].astype(F32)
            r.XR[zz, at, :] = total.astype(BF)
            sent = rows(r.XR.at[zz], crow(q, k), 128)

            @pl.when(down)
            def _():
                rdma(sent, rows(r.ZR.at[zz], crow(q, k), 128), r.rzs.at[zz], r.rzr.at[n], me.below).start()

            @pl.when(jnp.logical_not(down))
            def _():
                last = zz == me.z + 1
                slot, sem = pick(last, 4, zz), pick(last, 48 + k, n)
                rdma(sent, rows(r.ZR.at[slot], crow(q, k), 128), r.rzs.at[zz], r.rzr.at[sem], me.above).start()

        loop(2, body)


def sums_at(me, r, place):
    for groups in SUMS[place]:
        reduce_step(me, r, groups)


def reduce_group(me, r, g):
    first_tensor = pick(me.dp < 2, 2, pick(me.dp == 2, 4, pick(me.dp < 6, 8, 10)))
    part = jnp.zeros((1, 128), F32)
    for i in range(2):
        k = g * 2 + i
        n = me.z * 12 + k
        arrived(r.G.at[0:128], r.rxr.at[n])

        @pl.when(me.z < 3)
        def _(n=n):
            arrived(r.G.at[0:128], r.rzr.at[n])

        @pl.when(me.z > 0)
        def _(k=k):
            arrived(r.G.at[0:128], r.rzr.at[48 + k])

        src, at = pl.ds(pl.multiple_of(chunk_row(me.dp, k), 128), 128), pl.ds(pl.multiple_of(crow(me.dp, k), 128), 128)
        total = r.G[src, :].astype(F32) + r.XR[me.z, at, :].astype(F32)
        total = total + (r.ZR[me.z, at, :].astype(F32) + r.ZR[4, at, :].astype(F32))
        part = part + squares(total)
        r.XR[me.z, at, :] = total.astype(BF)
    tensor = pick((g >= 4) & (me.dp == 2), 8, pick((g >= 2) & (me.dp == 5), 10, first_tensor))
    r.NB[0, pl.ds(tensor, 1), :] += part


def reduce_first(me, r):
    def pair(j):
        reduce_group(me, r, 2 * j)
        reduce_group(me, r, 2 * j + 1)
        for i in range(4):
            src = rows(r.XR.at[me.z], j * 512 + 128 * i, 128)
            dst = rows(r.S, (j * 4 + me.blk) * 128, 128)

            @pl.when(me.blk != i)
            def _(i=i, src=src, dst=dst):
                rdma(src, dst, r.qsem2.at[i * 24 + j * 4 + me.blk], r.csem2, (me.dp, i)).start()

            @pl.when(me.blk == i)
            def _(src=src, dst=dst):
                pltpu.make_async_copy(src, dst, r.csem2).start()

    loop(3, pair)


def reduce_rest(me, r):
    loop(6, lambda g: reduce_group(me, r, g))
    for i in range(4):
        def visit(n, srow, size, part, row, i=i):
            src, dst = rows(r.XR.at[me.z], row, size, 32), rows(r.S, srow, size, 32)

            @pl.when((part == me.blk) & (me.blk != i))
            def _():
                rdma(src, dst, r.qsem2.at[i * 24 + n], r.csem2, (me.dp, i)).start()

            @pl.when((part == me.blk) & (me.blk == i))
            def _():
                pltpu.make_async_copy(src, dst, r.csem2).start()

        Other(me, i).pieces(visit)


def column(me):
    return [(lax.rem(me.dp + k, 8), me.blk) for k in range(1, 8)]


VECTORS = ((0, 16), (1, 8), (2, 32), (5, 32), (7, 8))


def vectors_send(me, r, early):
    for q, count in VECTORS:
        if early == (q > 0):
            @pl.when(me.dp != q)
            def _(q=q, count=count):
                rdma(r.VG.at[q, 0:count], r.VX.at[me.dp, 0:count], r.wxs.at[q], r.wxr.at[me.dp], (q, me.blk)).start()


def vectors_sum(me, r):
    for q, count in VECTORS:
        @pl.when(me.dp == q)
        def _(q=q, count=count):
            total = r.VG[q, 0:count, :]
            for other in range(8):
                if other != q:
                    arrived(r.VX.at[0, 0:count], r.wxr.at[other])
                    total = total + r.VX[other, 0:count, :]
            r.VT[me.blk, 0:count, :] = total
            for peer in me.quad:
                rdma(r.VT.at[me.blk, 0:count], r.VT.at[me.blk, 0:count], r.wqs, r.wqr.at[me.blk], peer).start()


def vectors_end(me, r):
    for q, count in VECTORS:
        @pl.when(me.dp == q)
        def _(q=q, count=count):
            for k in (1, 2, 3):
                arrived(r.VT.at[0, 0:count], r.wqr.at[lax.rem(me.blk + k, 4)])
            r.VS[0:count, :] = r.VT[0, 0:count, :] + r.VT[1, 0:count, :] + r.VT[2, 0:count, :] + r.VT[3, 0:count, :]
            arrived(r.VT.at[0:3, 0:count], r.wqs)

        @pl.when(me.dp != q)
        def _(q=q, count=count):
            arrived(r.VG.at[q, 0:count], r.wxs.at[q])

    vector_squares(me, r)


def norms_pack(me, r):
    sums = jnp.sum(r.NB[0, 0:16, :], axis=1, keepdims=True)
    tensor = lax.broadcasted_iota(jnp.int32, (16, 128), 0)
    lane = lax.broadcasted_iota(jnp.int32, (16, 128), 1)
    line = jnp.sum(jnp.where(tensor == lane, sums, 0.0), axis=0, keepdims=True)
    r.NM[0:8, :] = jnp.broadcast_to(line, (8, 128))
    r.NM[8:16, :] = r.NB[0, 16:24, :]


def norms_send(me, r):
    norms_pack(me, r)
    for peer in column(me):
        rdma(r.NM, r.NR.at[me.dp], r.nsem, r.nrsem.at[me.dp], peer).start()
    r.NR[me.dp] = r.NM[...]


def norms_sum(me, r):
    for q, _ in column(me):
        arrived(r.NR.at[0], r.nrsem.at[q])
    total = r.NR[0]
    for q in range(1, 8):
        total = total + r.NR[q]
    r.NQ[me.blk] = total
    for peer in me.quad:
        rdma(r.NQ.at[me.blk], r.NQ.at[me.blk], r.nqs, r.nqr.at[me.blk], peer).start()


def norms_end(me, r):
    for k in (1, 2, 3):
        arrived(r.NQ.at[0], r.nqr.at[lax.rem(me.blk + k, 4)])
    r.norms[...] = r.NQ[0] + r.NQ[1] + r.NQ[2] + r.NQ[3]
    arrived(r.NR.at[0:7], r.nsem)
    arrived(r.NQ.at[0:3], r.nqs)


def vector_squares(me, r):
    for q, tensors in ((0, (0, 1, None, None)), (1, (3, None, None, None)), (2, (3, 5, 6, 7)), (5, (9, 9, 9, 9)), (7, (11, None, None, None))):
        @pl.when((me.dp == q) & (me.blk == 0))
        def _(q=q, tensors=tensors):
            for g, tensor in enumerate(tensors):
                if tensor is not None:
                    r.NB[0, tensor : tensor + 1, :] += squares(r.VS[8 * g : 8 * g + 8, :])
            if q == 7:
                r.NB[0, 16:24, :] = r.VS[0:8, :]


def reduce_drain(me, r):
    arrived(r.G.at[0:6144], r.rxs)
    for i in range(4):
        @pl.when(me.z != i)
        def _(i=i):
            arrived(r.G.at[0:1536], r.rzs.at[i])

        def visit(n, srow, size, part, row, i=i):
            @pl.when((part == me.blk) & (me.blk != i))
            def _():
                arrived(rows(r.XR.at[me.z], row, size, 32), r.qsem2.at[i * 24 + n])

        Other(me, i).pieces(visit)


def units_send(me, r):
    arrived(r.S, r.csem2)
    for lo, hi in ((0, 48), (3072, 3128)):
        r.E[lo:hi, :] = jnp.zeros((hi - lo, 128), F32)

    def tile(unit, stride, row, lane):
        r.E[unit_span(unit, stride), :] = r.S[pl.ds(pl.multiple_of(row, 16), 16), lane : lane + 128].astype(F32)

    for_tiles(me, tile)

    def vec(row, unit, count):
        r.E[unit : unit + count, :] = r.VS[row : row + count, :]

    vec_spots(me, vec)
    r.tail[...] = r.E[3099:3123, :]
    rdma(r.tail, r.hp2, r.hsem2.at[0], r.hsem2.at[1], me.next).start()
    rdma(r.E.at[0:24], r.hn2, r.hsem2.at[2], r.hsem2.at[3], me.prev).start()


def units_end(me, r):
    def put(i):
        r.grad[pl.ds(pl.multiple_of(64 * i, 8), 64), :] = r.E[pl.ds(pl.multiple_of(24 + 64 * i, 8), 64), :]

    loop(48, put)
    r.grad[3072:3075, :] = r.E[3096:3099, :]
    for n in range(4):
        arrived(r.tail, r.hsem2.at[n])
    r.grad[0:24, :] += r.hp2[...]
    r.grad[3051:3075, :] += r.hn2[...]


def whole_layer(me, r):
    r.VG[...] = jnp.zeros_like(r.VG)
    r.NB[0] = jnp.zeros((24, 128), F32)

    def clear(slot):
        r.ZR[slot] = jnp.zeros((1536, 256), BF)

    @pl.when(me.z == 0)
    def _():
        loop(4, lambda i: clear(i + 1))

    @pl.when(me.z == 3)
    def _():
        loop(4, clear)

    gate(me.quad + me.others + [me.xpeer, me.next, me.prev])
    prepare(me, r)
    chunk_here(me, r, 0)
    own_down(me, r)
    gather_at(me, r, "first")
    chunk_here(me, r, 1)
    gather_at(me, r, "second")
    chunk_here(me, r, 2)
    swap_send(me, r, r.pat, r.PA, r.pas, r.par_in)
    gather_at(me, r, "third")
    swap_pass(me, r, r.PA, r.pas, r.par_in)
    swap_send(me, r, r.cot, r.CA, r.cas, r.car)
    for peer in range(1, 8):
        arrived(r.XV.at[0], r.vxr.at[lax.rem(me.dp + peer, 8)])
    gather_at(me, r, "fourth")
    arrived(r.PA.at[0:256], r.par_in.at[0])
    first_norm(me, r, me.y)
    gather_at(me, r, "fifth")
    arrived(r.PA.at[0:256], r.par_in.at[2])
    swap_drain(me, r, r.PA, r.pas)
    first_norm(me, r, 1 - me.y)
    gather_at(me, r, "sixth")
    prepare_drain(me, r)
    gathered(me, r, 0)

    def between(n):
        if n == 1:
            swap_pass(me, r, r.CA, r.cas, r.car)
        gather_at(me, r, "rows%d" % n)

    attention(me, r, between)
    out_send(me, r, 0)
    out_send(me, r, 1)
    attended_pass(me, r, 3)
    gather_at(me, r, "out0")
    out_pass(me, r, 0)
    gather_at(me, r, "out1")
    out_pass(me, r, 1)
    shared_here(me, r)
    gather_at(me, r, "shared")
    second_norm(me, r)
    gather_at(me, r, "normed")

    @pl.when(me.x == 0)
    def _():
        gathered(me, r, 1, (0, 1, 2, 3))

    gathered(me, r, 1, (4, 5))
    gathered(me, r, 2)
    hidden(me, r)
    arrived(r.CA.at[0:256], r.car.at[0])
    arrived(r.CA.at[0:256], r.car.at[2])
    swap_drain(me, r, r.CA, r.cas)
    weight_grad(r, r.AC, r.CA, DOWN0, 1024)
    reduce_send(me, r, 3, 0, 6)

    @pl.when(me.z < 3)
    def _():
        reduce_send(me, r, 3, 6, 6)

    gathered(me, r, 3)
    gather_drain(me, r)
    hidden_grad(me, r)
    middle_sums, input_sums = [], []
    middle = middle_grad(me, r, middle_sums)
    middle.begin()
    weight_grad(r, r.NT, r.GH, UP0, 1024)
    reduce_send(me, r, 2)

    @pl.when(me.z == 3)
    def _():
        reduce_send(me, r, 3, 6, 6)

    result = layer_out(me, r)
    loop(4, result.make)
    sums_at(me, r, "start")
    middle.end(lambda n: sums_at(me, r, "middle%d" % n))
    for n in range(3):
        put_vec(r, 2, 8 + 8 * n, middle_sums[n])
    result.send_far_sib()
    weight_grad(r, r.AT, r.GM, OUT0, 256)
    reduce_send(me, r, 1)
    attended_grad(me, r)
    result.cross()
    result.send_near_sib()
    sums_at(me, r, "attended")
    attention_grad(me, r, lambda n: sums_at(me, r, "rows%d" % n))
    projection_grad(me, r)
    reduce_send(me, r, 0)
    last = input_grad(me, r, input_sums)
    sums_at(me, r, "weights")
    result.end()
    last.begin()
    sums_at(me, r, "last")
    hidden_sums(me, r)
    projection_sums(me, r)
    vectors_send(me, r, True)
    last.end(lambda n: sums_at(me, r, "last%d" % n))
    for n in range(2):
        put_vec(r, 0, 8 * n, input_sums[n])
    vectors_send(me, r, False)

    @pl.when(me.z > 0)
    def _():
        reduce_rest(me, r)

    sums_at(me, r, "end")
    vectors_sum(me, r)

    @pl.when(me.z == 0)
    def _():
        reduce_first(me, r)

    vectors_end(me, r)
    norms_send(me, r)
    units_send(me, r)
    norms_sum(me, r)
    units_end(me, r)
    norms_end(me, r)
    reduce_drain(me, r)


DMA = pltpu.SemaphoreType.DMA
VMEM = pltpu.VMEM
SCRATCH = dict(
    F=VMEM((12288, 256), BF),
    G=VMEM((12288, 256), BF),
    XV=VMEM((8, 32, 128), F32),
    PA=VMEM((1024, 1024), BF),
    CA=VMEM((1024, 1024), BF),
    E=VMEM((4096, 128), F32),
    S=VMEM((1536, 256), BF),
    VS=VMEM((32, 128), F32),
    VQ=VMEM((4, 32, 128), F32),
    VG=VMEM((8, 32, 128), F32),
    VX=VMEM((8, 32, 128), F32),
    VT=VMEM((4, 32, 128), F32),
    NB=VMEM((1, 24, 128), F32),
    NM=VMEM((16, 128), F32),
    NR=VMEM((8, 16, 128), F32),
    NQ=VMEM((4, 16, 128), F32),
    tail=VMEM((24, 128), F32),
    hp=VMEM((24, 128), F32),
    hn=VMEM((24, 128), F32),
    hp2=VMEM((24, 128), F32),
    hn2=VMEM((24, 128), F32),
    XR=VMEM((4, 1536, 256), BF),
    ZR=VMEM((5, 1536, 256), BF),
    QKV=VMEM((3, 1024, 256), BF),
    P=VMEM((4, 1024, 1024), BF),
    AT=VMEM((1024, 256), BF),
    RL=VMEM((1024, 256), F32),
    PB=VMEM((1024, 1024), BF),
    RB=VMEM((5, 256, 1024), BF),
    MID=VMEM((256, 1024), F32),
    GMID=VMEM((256, 1024), F32),
    NT=VMEM((1024, 1024), BF),
    GM=VMEM((1024, 1024), BF),
    AC=VMEM((1024, 1024), BF),
    GP=VMEM((1024, 1024), BF),
    GH=VMEM((1024, 1024), BF),
    hsem=DMA((4,)), pas=DMA((3,)), par_in=DMA((3,)), cas=DMA((3,)), car=DMA((3,)), qsem=DMA((24,)), csem=DMA((3,)), vsem=DMA((2,)), vxs=DMA, vxr=DMA((8,)),
    xs=DMA, xr=DMA((48,)), ats=DMA((12,)), atr=DMA((12,)), wos=DMA((6,)), wor=DMA((6,)), zsu=DMA((4,)), zsd=DMA((4,)), zr=DMA((48,)),
    s2s=DMA((18,)), s2r=DMA((18,)),
    s3s=DMA((18,)), s3r=DMA((18,)), s4s=DMA((18,)), s4r=DMA((18,)),
    hsem2=DMA((4,)), rxs=DMA, rxr=DMA((48,)), rzs=DMA((4,)), rzr=DMA((60,)),
    wxs=DMA((8,)), wxr=DMA((8,)), wqs=DMA, wqr=DMA((4,)),
    qsem2=DMA((96,)), csem2=DMA, nsem=DMA, nrsem=DMA((8,)), nqs=DMA, nqr=DMA((4,)),
)


class Refs:
    pass


def fast_layer(lens, pat, cot, par):
    outs = dict(
        act=((256, 1024), BF), ing=((256, 1024), BF), grad=((3075, 128), F32), norms=((16, 128), F32)
    )
    names = ["lens", "pat", "cot", "par"] + list(outs) + list(SCRATCH)

    def kernel(*refs):
        r = Refs()
        for name, ref in zip(names, refs):
            setattr(r, name, ref)
        whole_layer(Place(), r)

    whole = pl.BlockSpec(memory_space=pltpu.VMEM)
    return pl.pallas_call(
        kernel,
        out_shape=[jax.ShapeDtypeStruct(*o) for o in outs.values()],
        in_specs=[pl.BlockSpec(memory_space=pltpu.SMEM)] + [whole] * 3,
        out_specs=[whole] * len(outs),
        scratch_shapes=list(SCRATCH.values()),
        compiler_params=pltpu.CompilerParams(collective_id=0, has_side_effects=True, vmem_limit_bytes=VMEM_LIMIT),
    )(lens, pat, cot, par)


VMEM_LIMIT = 63 * 2**20
PLAIN_UNITS = ((0, 16), (24592, 24608), (32800, 32824), (65592, 65624), (98392, 98400))


def fast_shards(pat, cot, lens, params, m, v):
    def units(a):
        return a.reshape(-1, LANE)

    par = units(params)
    act, ing, grad, nb = fast_layer(lens[0], pat[0], cot[0], par)
    norms = nb[0, :GROUPS]
    clip = 1.0 / jnp.maximum(jnp.sqrt(jnp.sum(norms)), 1.0)
    start = lax.axis_index(("dp", "blk")) * par.shape[0]
    unit = start + lax.broadcasted_iota(jnp.int32, par.shape, 0)
    plain = jnp.zeros(par.shape, jnp.bool_)
    for lo, hi in PLAIN_UNITS:
        plain = plain | ((unit >= lo) & (unit < hi))
    scaled = clip * grad
    first = 0.9 * units(m) + 0.1 * scaled
    second = 0.999 * units(v) + 0.001 * scaled * scaled
    direction = first / (1.0 - 0.9**10) / (jnp.sqrt(second / (1.0 - 0.999**10)) + 1e-08)
    step = -0.001 * 0.9**12 * (direction + jnp.where(plain, 0.0, 0.05 * par))
    return act[None], ing[None], norms, step.reshape(-1), first.reshape(-1), nb[8:16].reshape(-1)


def solution(mesh):
    act, flat = P("dp", "blk", None), P(("dp", "blk"))
    specs = dict(
        in_specs=(act, act, P("dp", None), flat, flat, flat), out_specs=(act, act, P(), flat, flat, P()), check_vma=False
    )

    def layer(patches, cotangent, image_lengths, params, first_moment, second_moment):
        fits = (dict(mesh.shape), patches.shape, params.shape) == (dict(dp=8, blk=4), (8, 1024, D), (RAW,))
        step = jax.shard_map(fast_shards if fits else shards, mesh=mesh, **specs)
        return step(patches, cotangent, image_lengths, params, first_moment, second_moment)

    return layer
```

```python
from functools import partial
import math

import jax
import jax.numpy as jnp
from jax import lax
from jax.experimental import pallas as pl
from jax.experimental.pallas import tpu as pltpu
from jax.sharding import PartitionSpec as P

D = 1024
FF = 4096
HEADS = 16
HEAD_DIM = 64
GROUPS = 12
RAW = 12595200


eps_norm = 1e-06
neg_big = -1e30


def starts_of(model_width, hidden):
    square = model_width * model_width
    mlp_start = 7 * model_width + 4 * square
    return [
        0,
        model_width,
        2 * model_width,
        2 * model_width + 3 * square,
        4 * model_width + 3 * square,
        4 * model_width + 4 * square,
        5 * model_width + 4 * square,
        6 * model_width + 4 * square,
        mlp_start,
        mlp_start + model_width * hidden,
        mlp_start + model_width * hidden + hidden,
        mlp_start + 2 * model_width * hidden + hidden,
        mlp_start + 2 * model_width * hidden + hidden + model_width,
    ]


def unpack(flat_params):
    marks = starts_of(D, FF)
    pieces = [flat_params[marks[member] : marks[member + 1]] for member in range(12)]
    return (
        pieces[0],
        pieces[1],
        pieces[2].reshape(D, 3 * D),
        pieces[3],
        pieces[4].reshape(D, D),
        pieces[5],
        pieces[6],
        pieces[7],
        pieces[8].reshape(D, FF),
        pieces[9],
        pieces[10].reshape(FF, D),
        pieces[11],
    )


def layer_norm(values, gains, offsets):
    average = jnp.mean(values, axis=-1, keepdims=True)
    centred = values - average
    spread = jnp.mean(centred * centred, axis=-1, keepdims=True)
    return centred * lax.rsqrt(spread + eps_norm) * gains + offsets


def segment_ids(lengths, row_ids):
    bounds = jnp.cumsum(lengths)
    return jnp.sum((row_ids[:, None] >= bounds[None, :]).astype(jnp.int32), axis=1)


def shards(patches, cotangent, image_lengths, params, first_moment, second_moment):
    local_rows = patches.shape[1]
    seq_len = local_rows * lax.axis_size("blk")
    scale_of = HEAD_DIM ** (-0.5)
    inputs = patches[0].astype(jnp.float32)
    lengths = image_lengths[0]
    query_ids = lax.axis_index("blk") * local_rows + jnp.arange(local_rows, dtype=jnp.int32)
    query_labels = segment_ids(lengths, query_ids)
    weights_low = lax.all_gather(params.astype(jnp.bfloat16), ("dp", "blk"), axis=0, tiled=True)
    (
        gain_one,
        shift_one,
        w_qkv,
        bias_qv,
        w_out,
        bias_out,
        gain_two,
        shift_two,
        w_up,
        bias_up,
        w_down,
        bias_down,
    ) = unpack(weights_low)
    normed_one, pull_one = jax.vjp(
        layer_norm, inputs, gain_one.astype(jnp.float32), shift_one.astype(jnp.float32)
    )
    normed_low = normed_one.astype(jnp.bfloat16)
    bias_all = jnp.concatenate(
        [
            bias_qv[:D].astype(jnp.float32),
            jnp.zeros((D,), jnp.float32),
            bias_qv[D:].astype(jnp.float32),
        ]
    )
    projected = (jnp.dot(normed_low, w_qkv, preferred_element_type=jnp.float32) + bias_all).astype(
        jnp.bfloat16
    )
    queries = projected[:, :D].reshape(local_rows, HEADS, HEAD_DIM)
    key_value = projected[:, D:]

    def attend_block(state, block, block_labels):
        allowed = query_labels[:, None] == block_labels[None, :]
        best_in, total_in, summed_in = state
        raw = jnp.einsum("qhd,khd->hqk", queries, block[:, 0], preferred_element_type=jnp.float32)
        scores = jnp.where(allowed[None], raw * scale_of, neg_big)
        new_best = jnp.maximum(best_in, jnp.max(scores, axis=-1))
        factor = jnp.exp(best_in - new_best)
        weights = jnp.where(allowed[None], jnp.exp(scores - new_best[..., None]), 0.0)
        new_total = total_in * factor + jnp.sum(weights, axis=-1)
        added = jnp.einsum(
            "hqk,khd->qhd",
            weights.astype(jnp.bfloat16),
            block[:, 1],
            preferred_element_type=jnp.float32,
        )
        return (new_best, new_total, summed_in * factor.T[..., None] + added)

    start_state = (
        jnp.full((HEADS, local_rows), neg_big, jnp.float32),
        jnp.zeros((HEADS, local_rows), jnp.float32),
        jnp.zeros((local_rows, HEADS, HEAD_DIM), jnp.float32),
    )
    carry = start_state
    piece = lax.all_gather(key_value, "blk", axis=0, tiled=True)
    count = piece.shape[0]
    size = math.gcd(count, 512)
    blocks = piece.reshape(count // size, size, 2, HEADS, HEAD_DIM)
    labels = segment_ids(lengths, jnp.arange(count, dtype=jnp.int32)).reshape(count // size, size)

    def one_block(state, members):
        return (attend_block(state, members[0], members[1]), None)

    carry, ignored = lax.scan(one_block, carry, (blocks, labels))
    best, total, summed = carry
    attended = summed / total.T[..., None]
    log_total = best + jnp.log(total)
    attended_low = attended.reshape(local_rows, D).astype(jnp.bfloat16)
    branch = jnp.dot(attended_low, w_out, preferred_element_type=jnp.float32) + bias_out.astype(
        jnp.float32
    )
    middle = inputs + branch
    normed_two, pull_two = jax.vjp(
        layer_norm, middle, gain_two.astype(jnp.float32), shift_two.astype(jnp.float32)
    )
    normed_two_low = normed_two.astype(jnp.bfloat16)
    hidden_pre = jnp.dot(normed_two_low, w_up, preferred_element_type=jnp.float32) + bias_up.astype(
        jnp.float32
    )
    activated, pull_gelu = jax.vjp(partial(jax.nn.gelu, approximate=False), hidden_pre)
    activated_low = activated.astype(jnp.bfloat16)
    result = middle + (
        jnp.dot(activated_low, w_down, preferred_element_type=jnp.float32)
        + bias_down.astype(jnp.float32)
    )
    grad_out = cotangent[0]
    grad_down = jnp.dot(activated_low.T, grad_out, preferred_element_type=jnp.float32)
    grad_bias_down = jnp.sum(grad_out.astype(jnp.float32), axis=0)
    grad_act = jnp.dot(grad_out, w_down.T, preferred_element_type=jnp.float32)
    grad_hidden_low = pull_gelu(grad_act)[0].astype(jnp.bfloat16)
    grad_up = jnp.dot(normed_two_low.T, grad_hidden_low, preferred_element_type=jnp.float32)
    grad_bias_up = jnp.sum(grad_hidden_low.astype(jnp.float32), axis=0)
    grad_normed_two = jnp.dot(grad_hidden_low, w_up.T, preferred_element_type=jnp.float32)
    grad_mid_norm, grad_gain_two, grad_shift_two = pull_two(grad_normed_two)
    grad_middle = grad_out.astype(jnp.float32) + grad_mid_norm
    grad_middle_low = grad_middle.astype(jnp.bfloat16)
    grad_w_out = jnp.dot(attended_low.T, grad_middle_low, preferred_element_type=jnp.float32)
    grad_bias_out = jnp.sum(grad_middle_low.astype(jnp.float32), axis=0)
    grad_attended = (
        jnp.dot(grad_middle_low, w_out.T, preferred_element_type=jnp.float32)
        .astype(jnp.bfloat16)
        .reshape(local_rows, HEADS, HEAD_DIM)
    )
    delta_rows = jnp.sum(grad_attended.astype(jnp.float32) * attended, axis=-1).T
    gathered = lax.all_gather(key_value, "blk", axis=0, tiled=True)
    size = math.gcd(seq_len, 512)
    key_blocks = gathered.reshape(seq_len // size, size, 2, HEADS, HEAD_DIM)
    key_labels = segment_ids(lengths, jnp.arange(seq_len, dtype=jnp.int32)).reshape(
        seq_len // size, size
    )

    def back_block(grad_query, members):
        block, block_labels = members
        allowed = query_labels[:, None] == block_labels[None, :]
        raw = jnp.einsum("qhd,khd->hqk", queries, block[:, 0], preferred_element_type=jnp.float32)
        scores = jnp.where(allowed[None], raw * scale_of, neg_big)
        probs = jnp.where(allowed[None], jnp.exp(scores - log_total[..., None]), 0.0)
        grad_probs = jnp.einsum(
            "qhd,khd->hqk", grad_attended, block[:, 1], preferred_element_type=jnp.float32
        )
        grad_raw = (probs * (grad_probs - delta_rows[..., None]) * scale_of).astype(jnp.bfloat16)
        new_grad = grad_query + jnp.einsum(
            "hqk,khd->qhd", grad_raw, block[:, 0], preferred_element_type=jnp.float32
        )
        grad_keys = jnp.einsum(
            "hqk,qhd->khd", grad_raw, queries, preferred_element_type=jnp.float32
        )
        grad_values = jnp.einsum(
            "hqk,qhd->khd",
            probs.astype(jnp.bfloat16),
            grad_attended,
            preferred_element_type=jnp.float32,
        )
        return (new_grad, jnp.stack([grad_keys, grad_values], axis=1))

    grad_query, grad_kv_blocks = lax.scan(
        back_block, jnp.zeros((local_rows, HEADS, HEAD_DIM), jnp.float32), (key_blocks, key_labels)
    )
    grad_kv = lax.psum_scatter(
        grad_kv_blocks.reshape(seq_len, 2 * D).astype(jnp.bfloat16),
        "blk",
        scatter_dimension=0,
        tiled=True,
    ).astype(jnp.float32)
    grad_projected = jnp.concatenate([grad_query.reshape(local_rows, D), grad_kv], axis=1).astype(
        jnp.bfloat16
    )
    grad_w_qkv = jnp.dot(normed_low.T, grad_projected, preferred_element_type=jnp.float32)
    grad_proj_rows = jnp.sum(grad_projected.astype(jnp.float32), axis=0)
    grad_bias_qv = jnp.concatenate([grad_proj_rows[:D], grad_proj_rows[2 * D :]])
    grad_normed_one = jnp.dot(grad_projected, w_qkv.T, preferred_element_type=jnp.float32)
    grad_in_norm, grad_gain_one, grad_shift_one = pull_one(grad_normed_one)
    grad_inputs = grad_middle + grad_in_norm
    shard_len = params.shape[0]
    total_params = shard_len * lax.axis_size(("dp", "blk"))
    flat_grad = jnp.concatenate(
        [
            grad_gain_one,
            grad_shift_one,
            grad_w_qkv.reshape(-1),
            grad_bias_qv,
            grad_w_out.reshape(-1),
            grad_bias_out,
            grad_gain_two,
            grad_shift_two,
            grad_up.reshape(-1),
            grad_bias_up,
            grad_down.reshape(-1),
            grad_bias_down,
            jnp.zeros((total_params - RAW,), jnp.float32),
        ]
    )
    shard_grad = lax.psum_scatter(
        lax.slice_in_dim(flat_grad, 0, lax.axis_size(("dp", "blk")) * shard_len, axis=0),
        ("dp", "blk"),
        scatter_dimension=0,
        tiled=True,
    )
    positions = lax.axis_index(("dp", "blk")) * shard_len + jnp.arange(shard_len, dtype=jnp.int32)
    marks = jnp.array(starts_of(D, FF), dtype=jnp.int32)
    group_of = jnp.sum((positions[:, None] >= marks[None, :]).astype(jnp.int32), axis=1) - 1
    squares = shard_grad * shard_grad
    partials = jnp.sum(
        jnp.where(
            group_of[None, :] == jnp.arange(GROUPS, dtype=jnp.int32)[:, None], squares[None, :], 0.0
        ),
        axis=1,
    )
    norms, bias_total = lax.psum((partials, grad_bias_down), ("dp", "blk"))
    clip_factor = 1.0 / jnp.maximum(jnp.sqrt(jnp.sum(norms)), 1.0)
    decayed = ((group_of == 2) | (group_of == 4) | (group_of == 8) | (group_of == 10)).astype(
        jnp.float32
    )
    scaled = clip_factor * shard_grad
    new_first = 0.9 * first_moment + 0.1 * scaled
    new_second = 0.999 * second_moment + 0.001 * scaled * scaled
    direction = new_first / (1.0 - 0.9**10) / (jnp.sqrt(new_second / (1.0 - 0.999**10)) + 1e-08)
    param_step = -0.001 * 0.9**12 * (direction + 0.05 * decayed * params)
    return (
        result.astype(jnp.bfloat16)[None],
        grad_inputs.astype(jnp.bfloat16)[None],
        norms,
        param_step,
        new_first,
        bias_total,
    )


MESH = pl.DeviceIdType.MESH
LANE = 128


def pick(cond, yes, no):
    return jnp.where(cond, jnp.int32(yes), jnp.int32(no))


def rdma(src, dst, ssem, rsem, dev):
    return pltpu.make_async_remote_copy(src_ref=src, dst_ref=dst, send_sem=ssem, recv_sem=rsem, device_id=dev, device_id_type=MESH)


def rows(ref, start, size, step=128):
    return ref.at[pl.ds(pl.multiple_of(start, step), size)]


def gate(peers):
    sem = pltpu.get_barrier_semaphore()
    for peer in peers:
        pl.semaphore_signal(sem, inc=1, device_id=peer, device_id_type=MESH)
    pl.semaphore_wait(sem, len(peers))


class Place:
    def __init__(self):
        self.dp = lax.axis_index("dp")
        self.blk = lax.axis_index("blk")
        self.d = self.dp * 4 + self.blk
        self.z = self.dp // 2
        self.x = self.dp % 2
        self.y = self.blk // 2
        self.c = self.blk % 2
        self.xpeer = (self.z * 2 + 1 - self.x, self.blk)
        self.zs = [lax.rem(self.z + k, 4) for k in (1, 3, 2)]
        self.zpeers = [(zz * 2 + self.x, self.blk) for zz in self.zs]
        self.quad = [(self.dp, lax.rem(self.blk + k, 4)) for k in (1, 2, 3)]
        up = lax.rem(self.d + 1, 32)
        down = lax.rem(self.d + 31, 32)
        self.above = (self.dp + 2, self.blk)
        self.below = (self.dp - 2, self.blk)
        self.others = self.zpeers + [(zz * 2 + 1 - self.x, self.blk) for zz in self.zs]
        self.near = ((self.dp, self.y * 2 + 1 - self.c), (self.dp, (1 - self.y) * 2 + self.c))
        self.far = (1 - self.y) * 2 + self.c
        self.next = (up // 4, up % 4)
        self.prev = (down // 4, down % 4)
        d = self.d
        self.is_qkv = d < 8
        self.is_out = (d == 8) | (d == 9)
        self.is_mix_out = d == 10
        self.is_up = (d >= 11) & (d < 21)
        self.is_mix_down = d == 21
        self.is_down = d >= 22
        self.is_seg = self.is_out | self.is_down
        self.is_mix = self.is_mix_out | self.is_mix_down
        self.base = pick(d < 8, 16, pick(d < 11, 32, pick(d < 21, 56, 88))) - 3 * d
        self.seg0 = pick(d < 11, 3 * (d - 8), jnp.maximum(3 * (d - 21) - 1, 0))
        self.mix_up = pick(self.is_mix_out, 2074, -7)
        self.mix_seg = pick(self.is_mix_out, 2, 1049)

    def seg_home(self, n):
        seg = self.seg0 + n // 4
        panel = n % 4
        out_row = 3072 + 256 * panel + 128 * (seg % 2)
        down_row = 8192 + 1024 * panel + 128 * (seg // 4)
        low = self.d < 11
        return pick(low, seg // 2, seg % 4), pick(low, out_row, down_row)

    def block_home(self, n):
        part, row = self.seg_home(n)
        return pick(self.is_qkv, n % 4, part), pick(self.is_qkv, (n // 4) * 1024 + 128 * self.d, row)

    def up_home(self, n):
        start = pick(self.is_up, 32 + 96 * (self.d - 11), pick(self.is_mix_out, 0, 992))
        return n // 4, 4096 + 1024 * (n % 4) + start


def chunk_row(q, k):
    first = (k // 4) * 1024 + 512 * q + 128 * (k % 4)
    turn = 3 * (q - 2) + k // 4
    panel = k % 4
    other = pick(
        turn < 2,
        3072 + 256 * panel + 128 * turn,
        pick(turn < 10, 4096 + 1024 * panel + 128 * (turn - 2), 8192 + 1024 * panel + 128 * (turn - 10)),
    )
    return pick(q < 2, first, other)


def loop(count, body):
    def step(i, carry):
        body(i)
        return carry

    lax.fori_loop(0, count, step, 0)


def unit_span(start, stride):
    return pl.ds(start, 16, stride=stride)


def for_tiles(me, visit):
    e0 = 24 + me.base

    @pl.when(me.is_qkv)
    def _():
        def body(rb):
            for ct in range(24):
                n = (ct // 8) * 4 + (ct % 8) // 2
                visit(e0 + 384 * rb + ct, 24, n * 128 + 16 * rb, 128 * (ct % 2))

        loop(8, body)

    @pl.when(me.is_up)
    def _():
        def body(rb):
            for ct in range(32):
                n = (ct % 4) * 4 + ct // 8
                visit(e0 + 512 * rb + ct, 32, n * 96 + 16 * rb, 128 * ((ct // 4) % 2))

        loop(6, body)

    def segs(count, first):
        def body(i):
            for ct in range(8):
                visit(first + 128 * i + ct, 8, ((i // 8) * 4 + ct // 2) * 128 + 16 * (i % 8), 128 * (ct % 2))

        loop(count, body)

    @pl.when(me.is_seg)
    def _():
        segs(24, e0)

    @pl.when(me.is_mix)
    def _():
        segs(16, 24 + me.mix_seg)

        def body(rb):
            for ct in range(32):
                n = (ct % 4) * 4 + ct // 8
                visit(24 + me.mix_up + 512 * rb + ct, 32, 1024 + n * 32 + 16 * rb, 128 * ((ct // 4) % 2))

        loop(2, body)


def for_pieces(me, visit):
    @pl.when(me.is_qkv | me.is_seg)
    def _():
        def body(n):
            part, row = me.block_home(n)
            visit(n, n * 128, 128, part, row, 128)

        loop(12, body)

    @pl.when(me.is_up)
    def _():
        def body(n):
            part, row = me.up_home(n)
            visit(n, n * 96, 96, part, row, 32)

        loop(16, body)

    @pl.when(me.is_mix)
    def _():
        def body(n):
            part, row = me.seg_home(n)
            visit(n, n * 128, 128, part, row, 128)

        loop(8, body)

        def body_up(n):
            part, row = me.up_home(n)
            visit(8 + n, 1024 + n * 32, 32, part, row, 32)

        loop(16, body_up)


def vec_spots(me, visit):
    for cond, row, unit, count in (
        (me.d == 0, 0, 0, 16),
        (me.d == 7, 0, 3067, 8),
        (me.d == 8, 0, 0, 8),
        (me.d == 10, 8, 2050, 24),
        (me.d == 21, 0, 1017, 32),
        (me.d == 31, 0, 3067, 8),
    ):

        @pl.when(cond)
        def _(row=row, unit=unit, count=count):
            visit(row, 24 + unit, count)


BF, F32 = jnp.bfloat16, jnp.float32
EPS = 1e-06
OUT0, UP0, DOWN0 = 3072, 4096, 8192


def dot(a, b):
    return lax.dot_general(a, b, (((1,), (0,)), ((), ())), preferred_element_type=F32)


def dot_nt(a, b):
    return lax.dot_general(a, b, (((1,), (1,)), ((), ())), preferred_element_type=F32)


def dot_tn(a, b):
    return lax.dot_general(a, b, (((0,), (0,)), ((), ())), preferred_element_type=F32)


def block_of(i):
    return pl.ds(pl.multiple_of(i * 256, 256), 256)


def wide(r, q, first, count=8):
    return jnp.concatenate([r.XV[q, first + i : first + i + 1, :] for i in range(count)], axis=1)


def narrow(r, q, first):
    return jnp.concatenate([r.XV[q, pl.ds(first + i, 1), :] for i in range(2)], axis=1)


def put_vec(r, q, first, row, add=False):
    for i in range(row.shape[1] // 128):
        part = row[:, i * 128 : i * 128 + 128]
        if add:
            part = part + r.VG[q, first + i : first + i + 1, :]
        r.VG[q, first + i : first + i + 1, :] = part


def normalize(x):
    mean = jnp.mean(x, axis=-1, keepdims=True)
    cen = x - mean
    var = jnp.mean(cen * cen, axis=-1, keepdims=True)
    scale = lax.rsqrt(var + EPS)
    return cen * scale, scale


def norm_back(dy, xhat, scale, gain):
    t = dy * gain
    return scale * (t - jnp.mean(t, axis=-1, keepdims=True) - xhat * jnp.mean(t * xhat, axis=-1, keepdims=True))


def labels_at(r, at):
    total = jnp.zeros_like(at)
    bound = 0
    for k in range(9):
        bound = bound + r.lens[k]
        total = total + (at >= bound).astype(jnp.int32)
    return total


def lane_mask(h, value=1.0):
    lane = lax.broadcasted_iota(jnp.int32, (1, 128), 1)
    return jnp.where((lane // 64) == h, value, 0.0).astype(BF)


def crow(q, k):
    return pick(q < 2, 128 * k, 384 * (k % 4) + 128 * (k // 4))


class Other(Place):
    def __init__(self, me, i):
        d = me.dp * 4 + i
        self.d, self.blk, self.dp = d, i, me.dp
        self.is_qkv = d < 8
        self.is_out = (d == 8) | (d == 9)
        self.is_mix_out = d == 10
        self.is_up = (d >= 11) & (d < 21)
        self.is_mix_down = d == 21
        self.is_down = d >= 22
        self.is_seg = self.is_out | self.is_down
        self.is_mix = self.is_mix_out | self.is_mix_down
        self.seg0 = pick(d < 11, 3 * (d - 8), jnp.maximum(3 * (d - 21) - 1, 0))

    def seg_spot(self, n):
        seg = self.seg0 + n // 4
        low = self.d < 11
        turn = pick(low, seg % 2, 10 + seg // 4 - 3 * (self.dp - 2))
        return pick(low, seg // 2, seg % 4), 384 * (n % 4) + 128 * turn

    def block_spot(self, n):
        part, row = self.seg_spot(n)
        return pick(self.is_qkv, n % 4, part), pick(self.is_qkv, (n // 4) * 512 + 128 * (self.d % 4), row)

    def up_spot(self, n):
        start = pick(self.is_up, 32 + 96 * (self.d - 11), pick(self.is_mix_out, 0, 992))
        return n // 4, 384 * (n % 4) + 256 + start - 384 * (self.dp - 2)

    def pieces(self, visit):
        @pl.when(self.is_qkv | self.is_seg)
        def _():
            loop(12, lambda n: visit(n, n * 128, 128, *self.block_spot(n)))

        @pl.when(self.is_up)
        def _():
            loop(16, lambda n: visit(n, n * 96, 96, *self.up_spot(n)))

        @pl.when(self.is_mix)
        def _():
            loop(8, lambda n: visit(n, n * 128, 128, *self.seg_spot(n)))
            loop(16, lambda n: visit(8 + n, 1024 + n * 32, 32, *self.up_spot(n)))


def arrived(ref, sem):
    pltpu.make_async_copy(ref, ref, sem).wait()


def squares(x):
    s = jnp.sum(x * x, axis=0, keepdims=True)
    return s[:, :128] + s[:, 128:] if x.shape[1] == 256 else s


def by_z(me, values):
    out = jnp.int32(values[0])
    for n in (1, 2, 3):
        out = pick(me.z == n, values[n], out)
    return out


def span(zz, *groups):
    return tuple(zz * 6 + g for g in groups)


ALL = (0, 1, 2, 3, 4, 5)
def spots(*by_depth):
    most = max(len(groups) for groups in by_depth)
    return tuple(zip(*(groups + (24,) * (most - len(groups)) for groups in by_depth)))


NONE = ()
GATHER = dict(
    first=spots(span(0, 0, 1), span(1, 0, 1), span(2, 0, 1), span(3, 0, 1)),
    second=spots(span(0, 2, 3), span(0, 0, 1), span(2, 2, 3), span(3, 2, 3)),
    third=spots(span(0, 4, 5) + span(1, 0), span(0, 2, 3, 4), span(0, 0, 1, 2), span(3, 4, 5) + span(0, 0)),
    fourth=spots(span(1, 1), NONE, NONE, span(0, 1)),
    fifth=spots(span(1, 2, 3), span(0, 5), span(0, 3, 4), span(0, 2, 3)),
    sixth=spots(span(1, 4, 5), span(1, 2, 3), span(0, 5) + span(1, 0), span(0, 4, 5)),
    rows0=spots(NONE, span(1, 4, 5), span(1, 1) + span(3, 0), span(2, 0)),
    rows1=spots(NONE, span(2, 0, 1), span(1, 2) + span(3, 1), span(1, 0) + span(2, 1)),
    rows2=spots(span(2, 0), span(2, 2, 3), span(1, 3) + span(3, 2), span(1, 1) + span(2, 2)),
    rows3=spots(span(2, 1, 2), span(2, 4, 5), span(1, 4, 5) + span(3, 3), span(1, 2, 3)),
    out0=spots(span(2, 3, 4), span(3, 0, 1), span(2, 4, 5) + span(3, 4), span(1, 4, 5) + span(2, 3)),
    out1=spots(span(2, 5), span(3, 2, 3), span(3, 5), span(2, 4)),
    shared=spots(span(3, 0, 1, 2), span(3, 4, 5), NONE, span(2, 5)),
    normed=spots(span(3, 3, 4, 5), NONE, NONE, NONE),
)
SUMS = dict(
    start=spots(span(3, 0, 1, 2, 3), NONE, NONE, span(2, 0)),
    middle0=spots(span(3, 4), span(3, 0), NONE, NONE),
    middle1=spots(span(3, 5), span(3, 1, 2), span(3, 0), span(2, 1)),
    middle2=spots(span(2, 0), span(3, 3), span(3, 1), span(2, 2)),
    middle3=spots(span(2, 1, 2), span(3, 4, 5), span(3, 2, 3), span(2, 3)),
    attended=spots(span(2, 3, 4), span(2, 0, 1), span(3, 4, 5), span(2, 4, 5)),
    rows0=spots(span(2, 5), span(2, 2, 3), NONE, span(1, 0)),
    rows1=spots(span(1, 0), span(2, 4), NONE, span(1, 1)),
    rows2=spots(span(1, 1), NONE, NONE, span(1, 2)),
    weights=spots(span(1, 2, 3), span(2, 5), span(1, 0, 1, 2), span(1, 3, 4)),
    last=spots(span(1, 4, 5), NONE, span(1, 3), span(1, 5) + span(0, 0)),
    last0=spots(NONE, NONE, span(1, 4), span(0, 1)),
    last1=spots(NONE, NONE, span(1, 5) + span(0, 0), span(0, 2)),
    last2=spots(NONE, NONE, span(0, 1), span(0, 3)),
    last3=spots(NONE, span(0, 0), span(0, 2), span(0, 4)),
    end=spots(NONE, span(0, 1, 2, 3, 4, 5), span(0, 3, 4, 5), span(0, 5)),
)


def prepare(me, r):
    r.tail[...] = r.par[3051:3075, :]
    up = rdma(r.tail, r.hp, r.hsem.at[0], r.hsem.at[1], me.next)
    down = rdma(r.par.at[0:24], r.hn, r.hsem.at[2], r.hsem.at[3], me.prev)
    up.start()
    down.start()

    def put(i):
        r.E[pl.ds(pl.multiple_of(24 + 64 * i, 8), 64), :] = r.par[pl.ds(pl.multiple_of(64 * i, 8), 64), :]

    loop(48, put)
    r.E[3096:3099, :] = r.par[3072:3075, :]
    r.VS[...] = jnp.zeros_like(r.VS)

    def vec(row, unit, count):
        r.VS[row : row + count, :] = r.E[unit : unit + count, :].astype(BF).astype(F32)

    vec_spots(me, vec)
    vq = [rdma(r.VS, r.VQ.at[me.blk], r.vsem.at[0], r.vsem.at[1], peer) for peer in me.quad]
    for v in vq:
        v.start()
    r.VQ[me.blk] = r.VS[...]
    up.wait()
    down.wait()
    r.E[0:24, :] = r.hp[...]
    r.E[3099:3123, :] = r.hn[...]

    def tile(unit, stride, row, lane):
        r.S[pl.ds(pl.multiple_of(row, 16), 16), lane : lane + 128] = r.E[unit_span(unit, stride), :].astype(BF)

    for_tiles(me, tile)

    def which(i):
        return pick(me.is_qkv, jnp.minimum(i // 4, 2), 0)

    def visit(i, srow, size, part, frow, step):
        src, dst = rows(r.S, srow, size, 32), rows(r.F, frow, size, step)

        @pl.when(part != me.blk)
        def _():
            rdma(src, dst, r.qsem.at[i], r.csem.at[which(i)], (me.dp, part)).start()

        @pl.when(part == me.blk)
        def _():
            pltpu.make_async_copy(src, dst, r.csem.at[which(i)]).start()

    for_pieces(me, visit)
    arrived(r.VQ.at[0:3], r.vsem.at[0])
    arrived(r.VQ.at[0:3], r.vsem.at[1])
    r.XV[me.dp] = r.VQ[0] + r.VQ[1] + r.VQ[2] + r.VQ[3]
    for peer in me.others + [me.xpeer]:
        rdma(r.XV.at[me.dp], r.XV.at[me.dp], r.vxs, r.vxr.at[me.dp], peer).start()


def chunk_here(me, r, panel):
    @pl.when(me.is_qkv)
    def _():
        arrived(r.F.at[0:512], r.csem.at[panel])

    if panel == 0:

        @pl.when(jnp.logical_not(me.is_qkv))
        def _():
            arrived(r.F.at[0:1536], r.csem.at[0])


def prepare_drain(me, r):
    def visit(i, srow, size, part, frow, step):
        @pl.when(part != me.blk)
        def _():
            arrived(rows(r.S, srow, size, 32), r.qsem.at[i])

    for_pieces(me, visit)
    arrived(r.XV.at[0:7], r.vxs)


def own_down(me, r):
    @pl.when(me.z > 0)
    def _():
        def body(k):
            ref = rows(r.F, chunk_row(me.dp, k), 128)
            rdma(ref, ref, r.zsd.at[me.z], r.zr.at[me.z * 12 + k], me.below).start()

        loop(12, body)


def gather_step(me, r, groups):
    e = by_z(me, groups)
    if 24 in groups:

        @pl.when(e < 24)
        def _():
            gather_group(me, r, e)

    else:
        gather_group(me, r, e)


def gather_group(me, r, e):
    zz, g = e // 6, e % 6
    for i in range(2):
        n = 2 * e + i

        @pl.when(zz != me.z)
        def _(n=n):
            arrived(r.F.at[0:128], r.zr.at[n])

        ref = rows(r.F, chunk_row(zz * 2 + me.x, g * 2 + i), 128)

        @pl.when((zz <= me.z) & (me.z < 3))
        def _(n=n, ref=ref):
            rdma(ref, ref, r.zsu.at[zz], r.zr.at[n], me.above).start()

        @pl.when((zz > me.z) & (me.z > 0))
        def _(n=n, ref=ref):
            rdma(ref, ref, r.zsd.at[zz], r.zr.at[n], me.below).start()

        rdma(ref, ref, r.xs, r.xr.at[n], me.xpeer).start()


def gather_at(me, r, place):
    for groups in GATHER[place]:
        gather_step(me, r, groups)


def gathered(me, r, zz, groups=ALL):
    for g in groups:
        for i in range(2):
            arrived(r.F.at[0:128], r.xr.at[zz * 12 + 2 * g + i])


def gather_drain(me, r):
    arrived(r.F.at[0:6144], r.xs)
    for zz in range(4):
        @pl.when((zz <= me.z) & (me.z < 3))
        def _():
            arrived(r.F.at[0:1536], r.zsu.at[zz])

        @pl.when((zz >= me.z) & (me.z > 0))
        def _():
            arrived(r.F.at[0:1536], r.zsd.at[zz])


def swap_send(me, r, src, dst, ssem, rsem):
    mine = block_of(me.blk)
    for n, peer in enumerate(me.near):
        rdma(src, dst.at[mine], ssem.at[n], rsem.at[n], peer).start()
    dst[mine, :] = src[...]


def swap_pass(me, r, dst, ssem, rsem):
    far = dst.at[block_of((1 - me.y) * 2 + me.c)]
    arrived(far, rsem.at[1])
    rdma(far, far, ssem.at[2], rsem.at[2], me.near[0]).start()


def swap_drain(me, r, dst, ssem):
    for n in range(3):
        arrived(dst.at[0:256], ssem.at[n])


def nothing(n):
    pass


class QuadSum:
    def __init__(self, me, r, term, make, sems, finish, slot, out=None):
        self.me, self.r, self.term, self.make, self.finish, self.slot, self.out = me, r, term, make, finish, slot, out
        self.ssem, self.rsem = sems
        y, c = me.y, me.c
        self.far_sib, self.far, self.near_sib, self.own = (1 - y) * 2 + 1 - c, (1 - y) * 2 + c, y * 2 + 1 - c, me.blk
        self.sib, self.yp = me.near
        self.over = []

    def copy(self, src, dst, n, dev):
        return rdma(src, dst, self.ssem.at[n], self.rsem.at[n], dev)

    def at(self, dev, i):
        return pl.ds(pl.multiple_of(dev * 256 + 64 * i, 64), 64)

    def send_far_sib(self):
        self.a = self.copy(self.term.at[block_of(self.far_sib)], self.r.RB.at[0], 0, self.sib)
        self.a.start()

    def send_near_sib(self):
        self.d = self.copy(self.term.at[block_of(self.near_sib)], self.r.RB.at[1], 1, self.sib)
        self.d.start()

    def cross(self):
        r = self.r
        self.a.wait_recv()
        for i in range(4):
            lo = pl.ds(64 * i, 64)
            r.RB[3, lo, :] = (self.term[self.at(self.far, i), :].astype(F32) + r.RB[0, lo, :].astype(F32)).astype(BF)
            self.over.append(self.copy(r.RB.at[3, lo], r.RB.at[self.slot, lo], 2 + i, self.yp))
            self.over[i].start()

    def begin(self):
        self.make(self.far_sib)
        self.send_far_sib()
        self.make(self.far)
        self.cross()
        self.make(self.near_sib)
        self.send_near_sib()
        self.make(self.own)

    def end(self, idle=nothing):
        r = self.r
        self.d.wait_recv()
        out, near, on = [], [], []
        for i in range(4):
            self.over[i].wait_recv()
            lo = slice(64 * i, 64 * i + 64)
            total = self.term[self.at(self.own, i), :].astype(F32) + r.RB[1, lo, :].astype(F32)
            self.finish(lo, total + r.RB[self.slot, lo, :].astype(F32))
            if self.out is not None:
                part, passed = self.out.at[self.at(self.own, i)], self.out.at[self.at(self.far, i)]
                out.append(self.copy(part, part, 6 + i, self.yp))
                near.append(self.copy(part, part, 10 + i, self.sib))
                on.append(self.copy(passed, passed, 14 + i, self.sib))
                out[i].start()
                near[i].start()
            idle(i)
        for i in range(len(out)):
            out[i].wait_recv()
            on[i].start()
        for cp in near + on:
            cp.wait()
        for cp in [self.a, self.d] + self.over + out:
            cp.wait_send()


def first_norm(me, r, half):
    gain, shift = wide(r, 0, 0), wide(r, 0, 8)

    def ln(i):
        at = pl.ds(pl.multiple_of(half * 512 + i * 64, 64), 64)
        x = r.PA[at, :]
        for p in range(4):
            row = pl.multiple_of(PATCH0 + 1024 * p + half * 512 + i * 64, 64)
            r.G[pl.ds(row, 64), :] = x[:, 256 * p : 256 * p + 256]
        xhat, _ = normalize(x.astype(F32))
        r.PA[at, :] = (xhat * gain + shift).astype(BF)

    loop(8, ln)


def attention(me, r, idle):
    bias = [narrow(r, 1, 2 * me.blk), None, narrow(r, 2, 2 * me.blk)]

    def proj(i):
        at = block_of(i)
        for j in range(3):
            out = dot(r.PA[at, :], r.F[j * 1024 : j * 1024 + 1024, :])
            if bias[j] is not None:
                out = out + bias[j]
            r.QKV[j, at, :] = out.astype(BF)

    loop(4, proj)
    key_labels = labels_at(r, lax.broadcasted_iota(jnp.int32, (1, 1024), 1))

    def attend(i):
        at = block_of(i)
        row_labels = labels_at(r, lax.broadcasted_iota(jnp.int32, (256, 1), 0) + i * 256)
        allowed = row_labels == key_labels
        for t in range(2):
            lanes = slice(128 * t, 128 * t + 128)
            q = r.QKV[0, at, lanes]
            k = r.QKV[1, :, lanes]
            v = r.QKV[2, :, lanes]
            out = jnp.zeros((256, 128), F32)
            inverse = []
            for h in range(2):
                s = jnp.where(allowed, dot_nt(q * lane_mask(h, 0.125), k), -1e30)
                w = jnp.exp(s - jnp.max(s, axis=-1, keepdims=True))
                inverse.append(1.0 / jnp.sum(w, axis=-1, keepdims=True))
                p = w.astype(BF)
                r.P[2 * t + h, at, :] = p
                out = out + dot(p, v * lane_mask(h))
            low_lanes = lax.broadcasted_iota(jnp.int32, (256, 128), 1) < 64
            scale = jnp.where(low_lanes, inverse[0], inverse[1])
            r.RL[at, lanes] = scale
            r.AT[at, lanes] = (out * scale).astype(BF)

    for i in range(4):
        attend(i)
        attended_send(me, r, i)
        if i > 0:
            attended_pass(me, r, i - 1)
        idle(i)


ATTENDED0, WHOLE_OUT0, PATCH0 = 0, 4096, 8192


def attended_send(me, r, i):
    dst = rows(r.G, ATTENDED0 + 1024 * me.blk + 256 * i, 256)
    for n in range(2):
        rdma(r.AT.at[256 * i : 256 * i + 256], dst, r.ats.at[2 * i + n], r.atr.at[2 * i + n], me.near[n]).start()


def attended_pass(me, r, i):
    ref = rows(r.G, ATTENDED0 + 1024 * me.far + 256 * i, 256)
    arrived(ref, r.atr.at[2 * i + 1])
    rdma(ref, ref, r.ats.at[8 + i], r.atr.at[8 + i], me.near[0]).start()


def out_send(me, r, half):
    @pl.when(me.x == 1)
    def _():
        gathered(me, r, 1, (0, 1) if half == 0 else (2, 3))

    for p in range(4):
        at = 256 * p + 128 * half
        src, dst = r.F.at[OUT0 + at : OUT0 + at + 128], rows(r.G, WHOLE_OUT0 + 1024 * me.blk + at, 128)
        for n in range(2):
            rdma(src, dst, r.wos.at[2 * half + n], r.wor.at[2 * half + n], me.near[n]).start()


def out_pass(me, r, half):
    arrived(r.G.at[0:512], r.wor.at[2 * half + 1])
    for p in range(4):
        ref = rows(r.G, WHOLE_OUT0 + 1024 * me.far + 256 * p + 128 * half, 128)
        rdma(ref, ref, r.wos.at[4 + half], r.wor.at[4 + half], me.near[0]).start()


def shared_here(me, r):
    for i in range(4):
        arrived(r.G.at[0:256], r.atr.at[2 * i])
        arrived(r.G.at[0:256], r.atr.at[8 + i])
    for half in range(2):
        arrived(r.G.at[0:512], r.wor.at[2 * half])
        arrived(r.G.at[0:512], r.wor.at[4 + half])
    for i in range(12):
        arrived(r.G.at[0:256], r.ats.at[i])
    for i in range(6):
        arrived(r.G.at[0:512], r.wos.at[i])
    r.G[pl.ds(pl.multiple_of(ATTENDED0 + 1024 * me.blk, 1024), 1024), :] = r.AT[...]
    r.G[pl.ds(pl.multiple_of(WHOLE_OUT0 + 1024 * me.blk, 1024), 1024), :] = r.F[OUT0 : OUT0 + 1024, :]


def second_norm(me, r):
    bias_out = wide(r, 2, 8)
    gain, shift = wide(r, 2, 16), wide(r, 2, 24)

    def body(i):
        for p in range(4):
            lanes = slice(256 * p, 256 * p + 256)
            acc = r.G[pl.ds(pl.multiple_of(PATCH0 + 1024 * p + 256 * i, 256), 256), :].astype(F32) + bias_out[:, lanes]
            for part in range(4):
                weights = r.G[WHOLE_OUT0 + 1024 * part + 256 * p : WHOLE_OUT0 + 1024 * part + 256 * p + 256, :]
                acc = acc + dot(r.G[pl.ds(pl.multiple_of(ATTENDED0 + 1024 * part + 256 * i, 256), 256), :], weights)
            r.GMID[:, lanes] = acc

        def ln(n):
            at = pl.ds(pl.multiple_of(n * 64, 64), 64)
            xhat, _ = normalize(r.GMID[at, :])
            r.NT[pl.ds(pl.multiple_of(i * 256 + n * 64, 64), 64), :] = (xhat * gain + shift).astype(BF)

        loop(4, ln)

        @pl.when(i == me.blk)
        def _():
            r.MID[...] = r.GMID[...]

    loop(4, body)


def hidden(me, r):
    biases = [jnp.concatenate([r.XV[5, pl.ds(4 * (2 * p + i) + me.blk, 1), :] for i in range(2)], axis=1) for p in range(4)]

    def up(i):
        at = pl.ds(pl.multiple_of(i * 128, 128), 128)
        for p in range(4):
            h = dot(r.NT[at, :], r.F[UP0 + 1024 * p : UP0 + 1024 * p + 1024, :]) + biases[p]
            phi = 0.5 + 0.5 * lax.erf(h * 0.7071067811865476)
            lanes = slice(256 * p, 256 * p + 256)
            r.AC[at, lanes] = (h * phi).astype(BF)
            r.GP[at, lanes] = (phi + h * (jnp.exp(-0.5 * h * h) * 0.3989422804014327)).astype(BF)

    loop(8, up)


def hidden_grad(me, r):
    def body(i):
        at = block_of(i)
        for p in range(4):
            lanes = slice(256 * p, 256 * p + 256)
            acc = jnp.zeros((256, 256), F32)
            for k in range(4):
                down = r.F[DOWN0 + 1024 * k + 256 * p : DOWN0 + 1024 * k + 256 * p + 256, :]
                acc = acc + dot_nt(r.CA[at, 256 * k : 256 * k + 256], down)
            r.GH[at, lanes] = (acc * r.GP[at, lanes].astype(F32)).astype(BF)

    loop(4, body)


def hidden_sums(me, r):
    for p in range(4):
        sums = jnp.sum(r.GH[:, 256 * p : 256 * p + 256].astype(F32), axis=0, keepdims=True)
        for i in range(2):
            r.VG[5, pl.ds(4 * (2 * p + i) + me.blk, 1), :] = sums[:, 128 * i : 128 * i + 128]
    put_vec(r, 7, 0, jnp.sum(r.cot[...].astype(F32), axis=0, keepdims=True))


def weight_grad(r, left, right, base, height):
    def body(i):
        cols = pl.ds(pl.multiple_of(i * 256, 256), 256)
        lt = left[:, cols].T
        for p in range(right.shape[1] // 256):
            out = dot(lt, right[:, 256 * p : 256 * p + 256])
            r.G[pl.ds(pl.multiple_of(base + p * height + i * 256, 256), 256), :] = out.astype(BF)

    loop(height // 256, body)


def middle_grad(me, r, sums):
    def term(i):
        at = block_of(i)
        for n in range(4):
            acc = jnp.zeros((256, 256), F32)
            for p in range(4):
                up = r.F[UP0 + 1024 * p + 256 * n : UP0 + 1024 * p + 256 * n + 256, :]
                acc = acc + dot_nt(r.GH[at, 256 * p : 256 * p + 256], up)
            r.PB[at, 256 * n : 256 * n + 256] = acc.astype(BF)

    gain = wide(r, 2, 16)
    sums[:] = [jnp.zeros((1, 1024), F32)] * 3

    def finish(lo, dy):
        xhat, scale = normalize(r.MID[lo, :])
        gm = r.cot[lo, :].astype(F32) + norm_back(dy, xhat, scale, gain)
        r.GMID[lo, :] = gm
        low = gm.astype(BF)
        r.GM[pl.ds(pl.multiple_of(me.blk * 256 + lo.start, 64), 64), :] = low
        for n, term_of in enumerate((low.astype(F32), dy * xhat, dy)):
            sums[n] = sums[n] + jnp.sum(term_of, axis=0, keepdims=True)

    return QuadSum(me, r, r.PB, term, (r.s2s, r.s2r), finish, 4, r.GM)


def attended_grad(me, r):
    def body(i):
        at = block_of(i)
        acc = jnp.zeros((256, 256), F32)
        for p in range(4):
            acc = acc + dot_nt(r.GM[at, 256 * p : 256 * p + 256], r.F[OUT0 + 256 * p : OUT0 + 256 * p + 256, :])
        r.GP[at, 768:1024] = acc.astype(BF)

    loop(4, body)


def attention_grad(me, r, idle):
    r.E[...] = jnp.zeros_like(r.E)

    def attend(i):
        at = block_of(i)
        for t in range(2):
            lanes = slice(128 * t, 128 * t + 128)
            q = r.QKV[0, at, lanes]
            k = r.QKV[1, :, lanes]
            v = r.QKV[2, :, lanes]
            da = (r.GP[at, 768 + 128 * t : 896 + 128 * t].astype(F32) * r.RL[at, lanes]).astype(BF)
            overlap = da.astype(F32) * r.AT[at, lanes].astype(F32)
            dq = jnp.zeros((256, 128), F32)
            for h in range(2):
                m, m8 = lane_mask(h), lane_mask(h, 0.125)
                p = r.P[2 * t + h, at, :]
                delta = jnp.sum(overlap * m.astype(F32), axis=-1, keepdims=True)
                ds = (p.astype(F32) * (dot_nt(da * m, v) - delta)).astype(BF)
                dq = dq + dot(ds, k * m8)
                r.E[1024 * t : 1024 * t + 1024, :] += dot_tn(ds, q * m8)
                r.E[2048 + 1024 * t : 3072 + 1024 * t, :] += dot_tn(p, da * m)
            r.GP[at, lanes] = dq.astype(BF)

    for i in range(4):
        attend(i)
        if i < 3:
            idle(i)
    for n in range(4):
        r.GP[:, 256 + 128 * n : 384 + 128 * n] = r.E[1024 * n : 1024 * n + 1024, :].astype(BF)


def projection_sums(me, r):
    for j, q in ((0, 1), (2, 2)):
        sums = jnp.sum(r.GP[:, 256 * j : 256 * j + 256].astype(F32), axis=0, keepdims=True)
        for i in range(2):
            r.VG[q, pl.ds(2 * me.blk + i, 1), :] = sums[:, 128 * i : 128 * i + 128]


def projection_grad(me, r):
    def body(i):
        cols = pl.ds(pl.multiple_of(i * 256, 256), 256)
        lt = r.PA[:, cols].T
        for j in range(3):
            r.G[pl.ds(pl.multiple_of(j * 1024 + i * 256, 256), 256), :] = dot(lt, r.GP[:, 256 * j : 256 * j + 256]).astype(BF)

    loop(4, body)


def input_grad(me, r, sums):
    def term(i):
        at = block_of(i)
        for n in range(4):
            acc = jnp.zeros((256, 256), F32)
            for j in range(3):
                acc = acc + dot_nt(r.GP[at, 256 * j : 256 * j + 256], r.F[1024 * j + 256 * n : 1024 * j + 256 * n + 256, :])
            r.PB[at, 256 * n : 256 * n + 256] = acc.astype(BF)

    gain = wide(r, 0, 0)
    sums[:] = [jnp.zeros((1, 1024), F32)] * 2

    def finish(lo, dy):
        xhat, scale = normalize(r.pat[lo, :].astype(F32))
        r.ing[lo, :] = (r.GMID[lo, :] + norm_back(dy, xhat, scale, gain)).astype(BF)
        for n, term_of in enumerate((dy * xhat, dy)):
            sums[n] = sums[n] + jnp.sum(term_of, axis=0, keepdims=True)

    return QuadSum(me, r, r.PB, term, (r.s4s, r.s4r), finish, 4)


def layer_out(me, r):
    def term(i):
        at = block_of(i)
        for p in range(4):
            r.CA[at, 256 * p : 256 * p + 256] = dot(r.AC[at, :], r.F[DOWN0 + 1024 * p : DOWN0 + 1024 * p + 1024, :]).astype(BF)

    bias_down = wide(r, 7, 0)

    def finish(lo, total):
        r.act[lo, :] = (r.MID[lo, :] + (total + bias_down)).astype(BF)

    return QuadSum(me, r, r.CA, term, (r.s3s, r.s3r), finish, 2)


def reduce_send(me, r, zz, first=0, count=12):
    q = zz * 2 + 1 - me.x

    def body(i):
        k = first + i
        rdma(rows(r.G, chunk_row(q, k), 128), rows(r.XR.at[zz], crow(q, k), 128), r.rxs, r.rxr.at[zz * 12 + k], me.xpeer).start()

    loop(count, body)


def reduce_step(me, r, groups):
    e = by_z(me, groups)

    @pl.when(e < 24)
    def _():
        zz, g = e // 6, e % 6
        q = zz * 2 + me.x
        down = zz < me.z

        def body(i):
            k = g * 2 + i
            n = zz * 12 + k
            arrived(r.G.at[0:128], r.rxr.at[n])

            @pl.when((me.z > 0) & (me.z < 3))
            def _():
                arrived(r.G.at[0:128], r.rzr.at[n])

            src, at = pl.ds(pl.multiple_of(chunk_row(q, k), 128), 128), pl.ds(pl.multiple_of(crow(q, k), 128), 128)
            total = r.G[src, :].astype(F32) + r.XR[zz, at, :].astype(F32) + r.ZR[zz, at, :].astype(F32)
            r.XR[zz, at, :] = total.astype(BF)
            sent = rows(r.XR.at[zz], crow(q, k), 128)

            @pl.when(down)
            def _():
                rdma(sent, rows(r.ZR.at[zz], crow(q, k), 128), r.rzs.at[zz], r.rzr.at[n], me.below).start()

            @pl.when(jnp.logical_not(down))
            def _():
                last = zz == me.z + 1
                slot, sem = pick(last, 4, zz), pick(last, 48 + k, n)
                rdma(sent, rows(r.ZR.at[slot], crow(q, k), 128), r.rzs.at[zz], r.rzr.at[sem], me.above).start()

        loop(2, body)


def sums_at(me, r, place):
    for groups in SUMS[place]:
        reduce_step(me, r, groups)


def reduce_group(me, r, g):
    first_tensor = pick(me.dp < 2, 2, pick(me.dp == 2, 4, pick(me.dp < 6, 8, 10)))
    part = jnp.zeros((1, 128), F32)
    for i in range(2):
        k = g * 2 + i
        n = me.z * 12 + k
        arrived(r.G.at[0:128], r.rxr.at[n])

        @pl.when(me.z < 3)
        def _(n=n):
            arrived(r.G.at[0:128], r.rzr.at[n])

        @pl.when(me.z > 0)
        def _(k=k):
            arrived(r.G.at[0:128], r.rzr.at[48 + k])

        src, at = pl.ds(pl.multiple_of(chunk_row(me.dp, k), 128), 128), pl.ds(pl.multiple_of(crow(me.dp, k), 128), 128)
        total = r.G[src, :].astype(F32) + r.XR[me.z, at, :].astype(F32)
        total = total + (r.ZR[me.z, at, :].astype(F32) + r.ZR[4, at, :].astype(F32))
        part = part + squares(total)
        r.XR[me.z, at, :] = total.astype(BF)
    tensor = pick((g >= 4) & (me.dp == 2), 8, pick((g >= 2) & (me.dp == 5), 10, first_tensor))
    r.NB[0, pl.ds(tensor, 1), :] += part


def reduce_first(me, r):
    def pair(j):
        reduce_group(me, r, 2 * j)
        reduce_group(me, r, 2 * j + 1)
        for i in range(4):
            src = rows(r.XR.at[me.z], j * 512 + 128 * i, 128)
            dst = rows(r.S, (j * 4 + me.blk) * 128, 128)

            @pl.when(me.blk != i)
            def _(i=i, src=src, dst=dst):
                rdma(src, dst, r.qsem2.at[i * 24 + j * 4 + me.blk], r.csem2, (me.dp, i)).start()

            @pl.when(me.blk == i)
            def _(src=src, dst=dst):
                pltpu.make_async_copy(src, dst, r.csem2).start()

    loop(3, pair)


def reduce_rest(me, r):
    loop(6, lambda g: reduce_group(me, r, g))
    for i in range(4):
        def visit(n, srow, size, part, row, i=i):
            src, dst = rows(r.XR.at[me.z], row, size, 32), rows(r.S, srow, size, 32)

            @pl.when((part == me.blk) & (me.blk != i))
            def _():
                rdma(src, dst, r.qsem2.at[i * 24 + n], r.csem2, (me.dp, i)).start()

            @pl.when((part == me.blk) & (me.blk == i))
            def _():
                pltpu.make_async_copy(src, dst, r.csem2).start()

        Other(me, i).pieces(visit)


def column(me):
    return [(lax.rem(me.dp + k, 8), me.blk) for k in range(1, 8)]


VECTORS = ((0, 16), (1, 8), (2, 32), (5, 32), (7, 8))


def vectors_send(me, r, early):
    for q, count in VECTORS:
        if early == (q > 0):
            @pl.when(me.dp != q)
            def _(q=q, count=count):
                rdma(r.VG.at[q, 0:count], r.VX.at[me.dp, 0:count], r.wxs.at[q], r.wxr.at[me.dp], (q, me.blk)).start()


def vectors_sum(me, r):
    for q, count in VECTORS:
        @pl.when(me.dp == q)
        def _(q=q, count=count):
            total = r.VG[q, 0:count, :]
            for other in range(8):
                if other != q:
                    arrived(r.VX.at[0, 0:count], r.wxr.at[other])
                    total = total + r.VX[other, 0:count, :]
            r.VT[me.blk, 0:count, :] = total
            for peer in me.quad:
                rdma(r.VT.at[me.blk, 0:count], r.VT.at[me.blk, 0:count], r.wqs, r.wqr.at[me.blk], peer).start()


def vectors_end(me, r):
    for q, count in VECTORS:
        @pl.when(me.dp == q)
        def _(q=q, count=count):
            for k in (1, 2, 3):
                arrived(r.VT.at[0, 0:count], r.wqr.at[lax.rem(me.blk + k, 4)])
            r.VS[0:count, :] = r.VT[0, 0:count, :] + r.VT[1, 0:count, :] + r.VT[2, 0:count, :] + r.VT[3, 0:count, :]
            arrived(r.VT.at[0:3, 0:count], r.wqs)

        @pl.when(me.dp != q)
        def _(q=q, count=count):
            arrived(r.VG.at[q, 0:count], r.wxs.at[q])

    vector_squares(me, r)


def norms_pack(me, r):
    sums = jnp.sum(r.NB[0, 0:16, :], axis=1, keepdims=True)
    tensor = lax.broadcasted_iota(jnp.int32, (16, 128), 0)
    lane = lax.broadcasted_iota(jnp.int32, (16, 128), 1)
    line = jnp.sum(jnp.where(tensor == lane, sums, 0.0), axis=0, keepdims=True)
    r.NM[0:8, :] = jnp.broadcast_to(line, (8, 128))
    r.NM[8:16, :] = r.NB[0, 16:24, :]


def norms_send(me, r):
    norms_pack(me, r)
    for peer in column(me):
        rdma(r.NM, r.NR.at[me.dp], r.nsem, r.nrsem.at[me.dp], peer).start()
    r.NR[me.dp] = r.NM[...]


def norms_sum(me, r):
    for q, _ in column(me):
        arrived(r.NR.at[0], r.nrsem.at[q])
    total = r.NR[0]
    for q in range(1, 8):
        total = total + r.NR[q]
    r.NQ[me.blk] = total
    for peer in me.quad:
        rdma(r.NQ.at[me.blk], r.NQ.at[me.blk], r.nqs, r.nqr.at[me.blk], peer).start()


def norms_end(me, r):
    for k in (1, 2, 3):
        arrived(r.NQ.at[0], r.nqr.at[lax.rem(me.blk + k, 4)])
    r.norms[...] = r.NQ[0] + r.NQ[1] + r.NQ[2] + r.NQ[3]
    arrived(r.NR.at[0:7], r.nsem)
    arrived(r.NQ.at[0:3], r.nqs)


def vector_squares(me, r):
    for q, tensors in ((0, (0, 1, None, None)), (1, (3, None, None, None)), (2, (3, 5, 6, 7)), (5, (9, 9, 9, 9)), (7, (11, None, None, None))):
        @pl.when((me.dp == q) & (me.blk == 0))
        def _(q=q, tensors=tensors):
            for g, tensor in enumerate(tensors):
                if tensor is not None:
                    r.NB[0, tensor : tensor + 1, :] += squares(r.VS[8 * g : 8 * g + 8, :])
            if q == 7:
                r.NB[0, 16:24, :] = r.VS[0:8, :]


def reduce_drain(me, r):
    arrived(r.G.at[0:6144], r.rxs)
    for i in range(4):
        @pl.when(me.z != i)
        def _(i=i):
            arrived(r.G.at[0:1536], r.rzs.at[i])

        def visit(n, srow, size, part, row, i=i):
            @pl.when((part == me.blk) & (me.blk != i))
            def _():
                arrived(rows(r.XR.at[me.z], row, size, 32), r.qsem2.at[i * 24 + n])

        Other(me, i).pieces(visit)


def units_send(me, r):
    arrived(r.S, r.csem2)
    for lo, hi in ((0, 48), (3072, 3128)):
        r.E[lo:hi, :] = jnp.zeros((hi - lo, 128), F32)

    def tile(unit, stride, row, lane):
        r.E[unit_span(unit, stride), :] = r.S[pl.ds(pl.multiple_of(row, 16), 16), lane : lane + 128].astype(F32)

    for_tiles(me, tile)

    def vec(row, unit, count):
        r.E[unit : unit + count, :] = r.VS[row : row + count, :]

    vec_spots(me, vec)
    r.tail[...] = r.E[3099:3123, :]
    rdma(r.tail, r.hp2, r.hsem2.at[0], r.hsem2.at[1], me.next).start()
    rdma(r.E.at[0:24], r.hn2, r.hsem2.at[2], r.hsem2.at[3], me.prev).start()


def units_end(me, r):
    def put(i):
        r.grad[pl.ds(pl.multiple_of(64 * i, 8), 64), :] = r.E[pl.ds(pl.multiple_of(24 + 64 * i, 8), 64), :]

    loop(48, put)
    r.grad[3072:3075, :] = r.E[3096:3099, :]
    for n in range(4):
        arrived(r.tail, r.hsem2.at[n])
    r.grad[0:24, :] += r.hp2[...]
    r.grad[3051:3075, :] += r.hn2[...]


def whole_layer(me, r):
    r.VG[...] = jnp.zeros_like(r.VG)
    r.NB[0] = jnp.zeros((24, 128), F32)

    def clear(slot):
        r.ZR[slot] = jnp.zeros((1536, 256), BF)

    @pl.when(me.z == 0)
    def _():
        loop(4, lambda i: clear(i + 1))

    @pl.when(me.z == 3)
    def _():
        loop(4, clear)

    gate(me.quad + me.others + [me.xpeer, me.next, me.prev])
    prepare(me, r)
    chunk_here(me, r, 0)
    own_down(me, r)
    gather_at(me, r, "first")
    chunk_here(me, r, 1)
    gather_at(me, r, "second")
    chunk_here(me, r, 2)
    swap_send(me, r, r.pat, r.PA, r.pas, r.par_in)
    gather_at(me, r, "third")
    swap_pass(me, r, r.PA, r.pas, r.par_in)
    swap_send(me, r, r.cot, r.CA, r.cas, r.car)
    for peer in range(1, 8):
        arrived(r.XV.at[0], r.vxr.at[lax.rem(me.dp + peer, 8)])
    gather_at(me, r, "fourth")
    arrived(r.PA.at[0:256], r.par_in.at[0])
    first_norm(me, r, me.y)
    gather_at(me, r, "fifth")
    arrived(r.PA.at[0:256], r.par_in.at[2])
    swap_drain(me, r, r.PA, r.pas)
    first_norm(me, r, 1 - me.y)
    gather_at(me, r, "sixth")
    prepare_drain(me, r)
    gathered(me, r, 0)

    def between(n):
        if n == 1:
            swap_pass(me, r, r.CA, r.cas, r.car)
        gather_at(me, r, "rows%d" % n)

    attention(me, r, between)
    out_send(me, r, 0)
    out_send(me, r, 1)
    attended_pass(me, r, 3)
    gather_at(me, r, "out0")
    out_pass(me, r, 0)
    gather_at(me, r, "out1")
    out_pass(me, r, 1)
    shared_here(me, r)
    gather_at(me, r, "shared")
    second_norm(me, r)
    gather_at(me, r, "normed")

    @pl.when(me.x == 0)
    def _():
        gathered(me, r, 1, (0, 1, 2, 3))

    gathered(me, r, 1, (4, 5))
    gathered(me, r, 2)
    hidden(me, r)
    arrived(r.CA.at[0:256], r.car.at[0])
    arrived(r.CA.at[0:256], r.car.at[2])
    swap_drain(me, r, r.CA, r.cas)
    weight_grad(r, r.AC, r.CA, DOWN0, 1024)
    reduce_send(me, r, 3, 0, 6)

    @pl.when(me.z < 3)
    def _():
        reduce_send(me, r, 3, 6, 6)

    gathered(me, r, 3)
    gather_drain(me, r)
    hidden_grad(me, r)
    middle_sums, input_sums = [], []
    middle = middle_grad(me, r, middle_sums)
    middle.begin()
    weight_grad(r, r.NT, r.GH, UP0, 1024)
    reduce_send(me, r, 2)

    @pl.when(me.z == 3)
    def _():
        reduce_send(me, r, 3, 6, 6)

    result = layer_out(me, r)
    loop(4, result.make)
    sums_at(me, r, "start")
    middle.end(lambda n: sums_at(me, r, "middle%d" % n))
    for n in range(3):
        put_vec(r, 2, 8 + 8 * n, middle_sums[n])
    result.send_far_sib()
    weight_grad(r, r.AT, r.GM, OUT0, 256)
    reduce_send(me, r, 1)
    attended_grad(me, r)
    result.cross()
    result.send_near_sib()
    sums_at(me, r, "attended")
    attention_grad(me, r, lambda n: sums_at(me, r, "rows%d" % n))
    projection_grad(me, r)
    reduce_send(me, r, 0)
    last = input_grad(me, r, input_sums)
    sums_at(me, r, "weights")
    result.end()
    last.begin()
    sums_at(me, r, "last")
    hidden_sums(me, r)
    projection_sums(me, r)
    vectors_send(me, r, True)
    last.end(lambda n: sums_at(me, r, "last%d" % n))
    for n in range(2):
        put_vec(r, 0, 8 * n, input_sums[n])
    vectors_send(me, r, False)

    @pl.when(me.z > 0)
    def _():
        reduce_rest(me, r)

    sums_at(me, r, "end")
    vectors_sum(me, r)

    @pl.when(me.z == 0)
    def _():
        reduce_first(me, r)

    vectors_end(me, r)
    norms_send(me, r)
    units_send(me, r)
    norms_sum(me, r)
    units_end(me, r)
    norms_end(me, r)
    reduce_drain(me, r)


DMA = pltpu.SemaphoreType.DMA
VMEM = pltpu.VMEM
SCRATCH = dict(
    F=VMEM((12288, 256), BF),
    G=VMEM((12288, 256), BF),
    XV=VMEM((8, 32, 128), F32),
    PA=VMEM((1024, 1024), BF),
    CA=VMEM((1024, 1024), BF),
    E=VMEM((4096, 128), F32),
    S=VMEM((1536, 256), BF),
    VS=VMEM((32, 128), F32),
    VQ=VMEM((4, 32, 128), F32),
    VG=VMEM((8, 32, 128), F32),
    VX=VMEM((8, 32, 128), F32),
    VT=VMEM((4, 32, 128), F32),
    NB=VMEM((1, 24, 128), F32),
    NM=VMEM((16, 128), F32),
    NR=VMEM((8, 16, 128), F32),
    NQ=VMEM((4, 16, 128), F32),
    tail=VMEM((24, 128), F32),
    hp=VMEM((24, 128), F32),
    hn=VMEM((24, 128), F32),
    hp2=VMEM((24, 128), F32),
    hn2=VMEM((24, 128), F32),
    XR=VMEM((4, 1536, 256), BF),
    ZR=VMEM((5, 1536, 256), BF),
    QKV=VMEM((3, 1024, 256), BF),
    P=VMEM((4, 1024, 1024), BF),
    AT=VMEM((1024, 256), BF),
    RL=VMEM((1024, 256), F32),
    PB=VMEM((1024, 1024), BF),
    RB=VMEM((5, 256, 1024), BF),
    MID=VMEM((256, 1024), F32),
    GMID=VMEM((256, 1024), F32),
    NT=VMEM((1024, 1024), BF),
    GM=VMEM((1024, 1024), BF),
    AC=VMEM((1024, 1024), BF),
    GP=VMEM((1024, 1024), BF),
    GH=VMEM((1024, 1024), BF),
    hsem=DMA((4,)), pas=DMA((3,)), par_in=DMA((3,)), cas=DMA((3,)), car=DMA((3,)), qsem=DMA((24,)), csem=DMA((3,)), vsem=DMA((2,)), vxs=DMA, vxr=DMA((8,)),
    xs=DMA, xr=DMA((48,)), ats=DMA((12,)), atr=DMA((12,)), wos=DMA((6,)), wor=DMA((6,)), zsu=DMA((4,)), zsd=DMA((4,)), zr=DMA((48,)),
    s2s=DMA((18,)), s2r=DMA((18,)),
    s3s=DMA((18,)), s3r=DMA((18,)), s4s=DMA((18,)), s4r=DMA((18,)),
    hsem2=DMA((4,)), rxs=DMA, rxr=DMA((48,)), rzs=DMA((4,)), rzr=DMA((60,)),
    wxs=DMA((8,)), wxr=DMA((8,)), wqs=DMA, wqr=DMA((4,)),
    qsem2=DMA((96,)), csem2=DMA, nsem=DMA, nrsem=DMA((8,)), nqs=DMA, nqr=DMA((4,)),
)


class Refs:
    pass


def fast_layer(lens, pat, cot, par):
    outs = dict(
        act=((256, 1024), BF), ing=((256, 1024), BF), grad=((3075, 128), F32), norms=((16, 128), F32)
    )
    names = ["lens", "pat", "cot", "par"] + list(outs) + list(SCRATCH)

    def kernel(*refs):
        r = Refs()
        for name, ref in zip(names, refs):
            setattr(r, name, ref)
        whole_layer(Place(), r)

    whole = pl.BlockSpec(memory_space=pltpu.VMEM)
    return pl.pallas_call(
        kernel,
        out_shape=[jax.ShapeDtypeStruct(*o) for o in outs.values()],
        in_specs=[pl.BlockSpec(memory_space=pltpu.SMEM)] + [whole] * 3,
        out_specs=[whole] * len(outs),
        scratch_shapes=list(SCRATCH.values()),
        compiler_params=pltpu.CompilerParams(collective_id=0, has_side_effects=True, vmem_limit_bytes=VMEM_LIMIT),
    )(lens, pat, cot, par)


VMEM_LIMIT = 63 * 2**20
PLAIN_UNITS = ((0, 16), (24592, 24608), (32800, 32824), (65592, 65624), (98392, 98400))


def fast_shards(pat, cot, lens, params, m, v):
    def units(a):
        return a.reshape(-1, LANE)

    par = units(params)
    act, ing, grad, nb = fast_layer(lens[0], pat[0], cot[0], par)
    norms = nb[0, :GROUPS]
    clip = 1.0 / jnp.maximum(jnp.sqrt(jnp.sum(norms)), 1.0)
    start = lax.axis_index(("dp", "blk")) * par.shape[0]
    unit = start + lax.broadcasted_iota(jnp.int32, par.shape, 0)
    plain = jnp.zeros(par.shape, jnp.bool_)
    for lo, hi in PLAIN_UNITS:
        plain = plain | ((unit >= lo) & (unit < hi))
    scaled = clip * grad
    first = 0.9 * units(m) + 0.1 * scaled
    second = 0.999 * units(v) + 0.001 * scaled * scaled
    direction = first / (1.0 - 0.9**10) / (jnp.sqrt(second / (1.0 - 0.999**10)) + 1e-08)
    step = -0.001 * 0.9**12 * (direction + jnp.where(plain, 0.0, 0.05 * par))
    return act[None], ing[None], norms, step.reshape(-1), first.reshape(-1), nb[8:16].reshape(-1)


def solution(mesh):
    act, flat = P("dp", "blk", None), P(("dp", "blk"))
    specs = dict(
        in_specs=(act, act, P("dp", None), flat, flat, flat), out_specs=(act, act, P(), flat, flat, P()), check_vma=False
    )

    def layer(patches, cotangent, image_lengths, params, first_moment, second_moment):
        fits = (dict(mesh.shape), patches.shape, params.shape) == (dict(dp=8, blk=4), (8, 1024, D), (RAW,))
        step = jax.shard_map(fast_shards if fits else shards, mesh=mesh, **specs)
        return step(patches, cotangent, image_lengths, params, first_moment, second_moment)

    return layer
```
